32 devices in a mesh: section: 2 (over core), fsdp: 8 (over z, x), tensor: 2 (over y).
Axes of the slice: x: 2, y: 2, z: 4, core: 2. Of those that a mesh axis runs over, the one named last changes fastest.
Arguments:
- block_input: bfloat16 [2, 1792, 1024], P(None, 'fsdp'), may hold values from -6 to 6
- image_ids: int32 [2, 1792], P(None, 'fsdp'), may hold values from -1 to 7, as said below
- qkv_weight: bfloat16 [4, 1024, 3, 1024], P('section', 'fsdp', None, 'tensor'), may hold values from -0.1875 to 0.1875
- out_weight: bfloat16 [4, 1024, 1024], P('section', 'fsdp', 'tensor'), may hold values from -0.5 to 0.5
- up_weight: bfloat16 [4, 1024, 4096], P('section', 'fsdp', 'tensor'), may hold values from -0.1875 to 0.1875
- down_weight: bfloat16 [4, 1024, 4096], P('section', 'fsdp', 'tensor'), may hold values from -0.09375 to 0.09375
- norm_gains: bfloat16 [4, 2, 1024], P('section', None, 'fsdp'), may hold values from 0.5 to 1.5
- biases: bfloat16 [4, 4, 1024], P('section', None, 'fsdp'), may hold values from -3 to 3
- inner_bias: bfloat16 [4, 2, 3072], P('section', 'tensor', 'fsdp'), may hold values from -3 to 3
- cotangent: bfloat16 [2, 1792, 1024], P(None, 'fsdp'), may hold values from -6 to 6
Outputs:
- section_ends: float32 [2, 2, 1792, 1024], P('section', None, 'fsdp')
- qkv_grad: float32 [4, 1024, 3, 1024], P('section', 'fsdp', None, 'tensor')
- out_grad: float32 [4, 1024, 1024], P('section', 'fsdp', 'tensor')
- up_grad: float32 [4, 1024, 4096], P('section', 'fsdp', 'tensor')
- down_grad: float32 [4, 1024, 4096], P('section', 'fsdp', 'tensor')
- gains_grad: float32 [4, 2, 1024], P('section', None, 'fsdp')
- biases_grad: float32 [4, 4, 1024], P('section', None, 'fsdp')
- inner_grad: float32 [4, 2, 3072], P('section', 'tensor', 'fsdp')
The draws below stay inside these ranges and needn't reach their ends.
Inputs may be any that keep to these rules, and one draw needn't show every extreme that they name: `image_ids`: -1 marks padding; in each aligned block of 224 tokens of a micro-batch (block r) lie images r*1 to (r+1) - 1 in this order, each of exactly 197 consecutive tokens, with padding between, before or after them.
All inputs are finite; a program needn't handle non-finite values.
Results may differ from the reference program's by a relative error of at most 0.02.
Values may be sent and summed in bfloat16 or wider, within the bound.
A program may use at most 256 MiB of HBM per device.

```python
import math
import jax
import jax.numpy as jnp
from jax import lax

D = 1024
HEADS = 16
HEAD_DIM = 64
FF = 4096
IMG_LEN = 197
LAYERS_SECTION = 2
MICRO = 2
ROWS_DEV = 224
LAYERS = 4
SPLITS = 2
MB_TOK = 1792
IMG_DEV = 1


def draw_image_ids(key, part):
    block_total = MICRO * (MB_TOK // ROWS_DEV)
    spare_rows = ROWS_DEV - IMG_DEV * IMG_LEN
    offsets = jax.random.randint(key, (block_total, IMG_DEV), 0, spare_rows + 1).astype(jnp.int32)
    offsets = jnp.sort(offsets, axis=-1)
    starts = offsets + jnp.arange(IMG_DEV, dtype=jnp.int32)[None, :] * IMG_LEN
    places = jnp.arange(ROWS_DEV, dtype=jnp.int32)
    counted = jnp.sum((places[None, :, None] >= starts[:, None, :]).astype(jnp.int32), axis=-1) - 1
    chosen = jnp.take_along_axis(starts, jnp.clip(counted, 0, IMG_DEV - 1), axis=-1)
    inside = (counted >= 0) & (places[None, :] < chosen + IMG_LEN)
    block_place = (jnp.arange(block_total, dtype=jnp.int32) % (MB_TOK // ROWS_DEV))[:, None]
    ids = jnp.where(inside, counted + block_place * IMG_DEV, -1).astype(jnp.int32)
    return ids.reshape(MICRO, MB_TOK)


def with_spikes(drawn, rng, source, target, blocks, factor):
    def block_of(dim):
        return (jnp.arange(drawn.shape[dim]) // (drawn.shape[dim] // blocks)).reshape((-1,) + (1,) * (drawn.ndim - 1 - dim))

    near = jax.random.permutation(rng, blocks)[block_of(target)]
    other_side = (block_of(target) + blocks // 2) % blocks
    return jnp.where((block_of(source) == near) | (block_of(source) == other_side), factor * drawn, drawn)


def block_levels(rng, extent, pieces, least, top_value):
    level, own = 1.0, jax.random.fold_in(rng, 6)
    for position, parts in pieces:
        steps = jnp.exp(jax.random.uniform(jax.random.fold_in(own, position), (parts,), jnp.float32, least / len(pieces), top_value / len(pieces)))
        level = level * jnp.repeat(steps, extent[position] // parts).reshape([-1 if axis == position else 1 for axis in range(len(extent))])
    return level


def scatter_about(stream_key, shape, scale, bound, cuts=(), kind=jnp.bfloat16):
    entries = scale * jax.random.normal(stream_key, shape, jnp.float32)
    if cuts:
        entries = entries * block_levels(stream_key, shape, cuts, -0.22, 0.18)
    return jnp.clip(entries, -bound, bound).astype(kind)


def noise_with(key, dims, scale, reach, shards, heavy, held_as=jnp.bfloat16):
    result = scale * jax.random.normal(key, dims, jnp.float32)
    if shards:
        result = result * block_levels(key, dims, shards, -0.22, 0.18)
    return jnp.clip(with_spikes(result, jax.random.fold_in(key, 3), *heavy), -reach, reach).astype(held_as)


def setup_inputs(seed: int = 0) -> dict:
    keys = jax.random.split(jax.random.key(seed), 11)
    return {
        "block_input": scatter_about(keys[0], (MICRO, MB_TOK, D), 1.0, 6.0, ((1, 8),)),
        "image_ids": draw_image_ids(jax.random.fold_in(keys[10], 71), 0),
        "qkv_weight": scatter_about(keys[2], (LAYERS, D, 3, D), D ** -0.5, 0.1875, ((0, 2), (1, 8), (3, 2))),
        "out_weight": scatter_about(keys[3], (LAYERS, D, D), (D * 24 // IMG_LEN) ** -0.5, 0.5, ((0, 2), (1, 8), (2, 2))),
        "up_weight": scatter_about(keys[4], (LAYERS, D, FF), D ** -0.5, 0.1875, ((0, 2), (1, 8), (2, 2))),
        "down_weight": scatter_about(keys[5], (LAYERS, D, FF), FF ** -0.5, 0.09375, ((0, 2), (1, 8), (2, 2))),
        "norm_gains": jnp.clip(1.0 + 0.1 * jax.random.normal(keys[6], (LAYERS, 2, D), jnp.float32), 0.5, 1.5).astype(jnp.bfloat16),
        "biases": scatter_about(keys[7], (LAYERS, 4, D), 0.5, 3.0, ((0, 2), (2, 8))),
        "inner_bias": scatter_about(keys[8], (LAYERS, SPLITS, (2 * D + FF) // SPLITS), 0.5, 3.0, ((0, 2), (1, 2), (2, 8))),
        "cotangent": noise_with(keys[9], (MICRO, MB_TOK, D), 1.0, 6.0, ((1, 8),), (1, 2, 8, 2.0)),
    }


@jax.custom_vjp
def low(v):
    return lax.optimization_barrier(v.astype(jnp.bfloat16)).astype(jnp.float32)

@jax.custom_vjp
def low_back(v):
    return v

def low_keep(v):
    return (low(v), None)

def low_pass(kept, grad):
    return (grad,)

def back_keep(v):
    return (v, None)

def back_low(kept, grad):
    return (low(grad),)
low.defvjp(low_keep, low_pass)
low_back.defvjp(back_keep, back_low)
EPSILON = 1e-06
HIGHEST = lax.Precision.HIGHEST

def layer_norm(hidden, weight_gain, weight_shift):
    average = lax.optimization_barrier(jnp.mean(hidden, axis=-1, keepdims=True))
    centred = hidden - average
    spread = lax.optimization_barrier(jnp.mean(centred * centred, axis=-1, keepdims=True))
    return centred * lax.rsqrt(spread + EPSILON) * weight_gain + weight_shift

def product(left, right):
    return jnp.dot(left, right, precision=HIGHEST)

def attention(queries, key_rows, value_rows, ids_batch):
    token_count = queries.shape[0]
    block_rows = ROWS_DEV
    block_count = token_count // block_rows
    places = jnp.arange(block_rows, dtype=jnp.int32)
    score_scale = 1.0 / math.sqrt(HEAD_DIM)

    def one_block(block_piece):
        query_block, key_block, value_block, block_ids = block_piece
        scores = jnp.einsum('qhe,khe->hqk', query_block, key_block, precision=HIGHEST) * score_scale
        scores = low_back(scores)
        same_image = (block_ids[:, None] == block_ids[None, :]) & (block_ids[:, None] >= 0)
        allowed = same_image | (places[:, None] == places[None, :])
        scores = jnp.where(allowed[None], scores, -1e+30)
        row_top = lax.optimization_barrier(jnp.max(scores, axis=-1, keepdims=True))
        exponent = jnp.exp(scores - row_top)
        row_total = lax.optimization_barrier(jnp.sum(exponent, axis=-1, keepdims=True))
        probs = low(exponent / row_total)
        return jnp.einsum('hqk,khe->qhe', probs, value_block, precision=HIGHEST)
    block_shape = (block_count, block_rows, HEADS, HEAD_DIM)
    block_pieces = (queries.reshape(block_shape), key_rows.reshape(block_shape), value_rows.reshape(block_shape), ids_batch.reshape(block_count, block_rows))
    mixed_heads = lax.map(jax.checkpoint(one_block), block_pieces)
    return mixed_heads.reshape(token_count, HEADS * HEAD_DIM)

def layer_forward(hidden, layer_params, ids_batch):
    qkv_w, out_w, up_w, down_w, gains, shifts, inner_part = layer_params
    token_count = hidden.shape[0]
    group_width = D // SPLITS
    query_bias = inner_part[:, :group_width].reshape(D)
    value_bias = inner_part[:, group_width:2 * group_width].reshape(D)
    up_bias = inner_part[:, 2 * group_width:].reshape(FF)
    normed = low(layer_norm(hidden, gains[0], shifts[0]))
    projected = product(normed, qkv_w.reshape(D, 3 * D)).reshape(token_count, 3, D)
    queries = low(low_back(projected[:, 0] + query_bias))
    key_rows = low(low_back(projected[:, 1]))
    value_rows = low(low_back(projected[:, 2] + value_bias))
    head_shape = (token_count, HEADS, HEAD_DIM)
    mixed_heads = attention(queries.reshape(head_shape), key_rows.reshape(head_shape), value_rows.reshape(head_shape), ids_batch)
    mixed_heads = low(low_back(mixed_heads))
    attended = low_back(product(mixed_heads, out_w.T) + shifts[1])
    middle = hidden + attended
    normed_mlp = low(layer_norm(middle, gains[1], shifts[2]))
    upward = low_back(product(normed_mlp, up_w) + up_bias)
    activated = low(jax.nn.gelu(upward, approximate=False))
    downward = low_back(product(activated, down_w.T) + shifts[3])
    return middle + downward

def reference(block_input, image_ids, qkv_weight, out_weight, up_weight, down_weight, norm_gains, biases, inner_bias, cotangent):
    params = tuple((array.astype(jnp.float32) for array in (qkv_weight, out_weight, up_weight, down_weight, norm_gains, biases, inner_bias)))

    def forward(inputs, *weights):
        results = []
        for micro_index in range(MICRO):
            hidden = inputs[micro_index]
            for layer_index in range(LAYERS):
                layer_params = tuple((array[layer_index] for array in weights))
                hidden = layer_forward(hidden, layer_params, image_ids[micro_index])
                if (layer_index + 1) % LAYERS_SECTION == 0 and layer_index + 1 < LAYERS:
                    hidden = low(low_back(hidden))
            results.append(hidden)
        return jnp.stack(results)
    outputs, pullback = jax.vjp(forward, block_input.astype(jnp.float32), *params)
    grads = pullback(cotangent.astype(jnp.float32))
    section_ends = jnp.stack([grads[0], outputs])
    return (section_ends, grads[1], grads[2], grads[3], grads[4], grads[5], grads[6], grads[7])
```

```python
import functools
import math

import jax
import jax.numpy as jnp
from jax import lax
from jax.experimental import pallas as pl
from jax.experimental.pallas import tpu as pltpu
from jax.sharding import PartitionSpec as P

HEAD_DIM = 64
MESH = pl.DeviceIdType.MESH
X_FIRST_COLS = 1024


def gather_kernel(line, w_ref, g_ref, local_sem, go_sem, sax, rax, sau, rau, sad, rad, sbx, rbx, sbu, rbu, sbd, rbd):
    layers, shard_rows, cols = w_ref.shape
    cols_a = cols - X_FIRST_COLS
    section = lax.axis_index("section")
    place = lax.axis_index("fsdp")
    z = place // 2
    x = lax.rem(place, 2)
    has_up = z < line - 1
    has_down = z > 0
    to_x = {"fsdp": z * 2 + 1 - x}
    to_up = {"fsdp": jnp.minimum(z + 1, line - 1) * 2 + x}
    to_down = {"fsdp": jnp.maximum(z - 1, 0) * 2 + x}

    barrier = pltpu.get_barrier_semaphore()
    pl.semaphore_signal(barrier, inc=1, device_id=to_x, device_id_type=MESH)
    pl.semaphore_signal(barrier, inc=1, device_id={"section": 1 - section}, device_id_type=MESH)

    @pl.when(has_up)
    def _():
        pl.semaphore_signal(barrier, inc=1, device_id=to_up, device_id_type=MESH)

    @pl.when(has_down)
    def _():
        pl.semaphore_signal(barrier, inc=1, device_id=to_down, device_id_type=MESH)

    pl.semaphore_wait(barrier, 2 + jnp.where(has_up, 1, 0) + jnp.where(has_down, 1, 0))

    span_a = pl.ds(0, cols_a)
    span_b = pl.ds(cols_a, X_FIRST_COLS)

    def spot(layer, row_z, row_x, span):
        start = pl.multiple_of((row_z * 2 + row_x) * shard_rows, shard_rows)
        return g_ref.at[layer, pl.ds(start, shard_rows), span]

    def own(layer, span):
        return w_ref.at[layer, :, span]

    def send(source, layer, row_z, row_x, span, send_sem, recv_sem, target):
        return pltpu.make_async_remote_copy(
            src_ref=source,
            dst_ref=spot(layer, row_z, row_x, span),
            send_sem=send_sem,
            recv_sem=recv_sem,
            device_id=target,
            device_id_type=MESH,
        )

    def relay(layer, row_z, row_x, span, send_sem, recv_sem, target):
        return send(spot(layer, row_z, row_x, span), layer, row_z, row_x, span, send_sem, recv_sem, target)

    @pl.when(section == 1)
    def _():
        pl.semaphore_wait(go_sem, 1)

    finish = []

    def launch(copy, condition=None):
        if condition is None:
            copy.start()
            finish.append((copy, None))
        else:
            pl.when(condition)(copy.start)
            finish.append((copy, condition))

    locals_ = []
    for layer in range(layers):
        copy = pltpu.make_async_copy(
            w_ref.at[layer], spot(layer, z, x, pl.ds(0, cols)), local_sem.at[layer]
        )
        copy.start()
        locals_.append(copy)
        a, b = own(layer, span_a), own(layer, span_b)
        launch(send(b, layer, z, x, span_b, sbx.at[layer], rbx.at[layer], to_x))
        launch(send(a, layer, z, x, span_a, sau.at[layer, 0], rau.at[layer, 0], to_up), has_up)
        launch(send(a, layer, z, x, span_a, sad.at[layer, 0], rad.at[layer, 0], to_down), has_down)
        launch(send(a, layer, z, x, span_a, sax.at[layer, 0], rax.at[layer, 0], to_x))
        launch(send(b, layer, z, x, span_b, sbu.at[layer, 0, 0], rbu.at[layer, 0, 0], to_up), has_up)
        launch(send(b, layer, z, x, span_b, sbd.at[layer, 0, 0], rbd.at[layer, 0, 0], to_down), has_down)

    def arrive(layer, row_z, row_x, span, sem):
        relay(layer, row_z, row_x, span, sem, sem, to_x).wait_recv()

    for layer in range(layers):
        arrive(layer, z, 1 - x, span_b, rbx.at[layer])
        launch(relay(layer, z, 1 - x, span_b, sbu.at[layer, 0, 1], rbu.at[layer, 0, 1], to_up), has_up)
        launch(relay(layer, z, 1 - x, span_b, sbd.at[layer, 0, 1], rbd.at[layer, 0, 1], to_down), has_down)
    for hop in range(line - 1):
        for layer in range(layers):
            from_below = z - 1 - hop
            from_above = z + 1 + hop
            below = from_below >= 0
            above = from_above < line
            row_below = jnp.maximum(from_below, 0)
            row_above = jnp.minimum(from_above, line - 1)

            def pass_on(live, row, rau, sau, rbu, sbu, sem_place, onward, target, hop=hop, layer=layer):
                pl.when(live)(lambda: arrive(layer, row, x, span_a, rau.at[layer, hop]))
                launch(relay(layer, row, x, span_a, sax.at[layer, sem_place], rax.at[layer, sem_place], to_x), live)
                if hop + 1 < line - 1:
                    launch(
                        relay(layer, row, x, span_a, sau.at[layer, hop + 1], rau.at[layer, hop + 1], target),
                        live & onward,
                    )
                for side, row_x in ((0, x), (1, 1 - x)):
                    pl.when(live)(
                        functools.partial(arrive, layer, row, row_x, span_b, rbu.at[layer, hop, side])
                    )
                    if hop + 1 < line - 1:
                        launch(
                            relay(
                                layer, row, row_x, span_b,
                                sbu.at[layer, hop + 1, side], rbu.at[layer, hop + 1, side], target,
                            ),
                            live & onward,
                        )

            pass_on(below, row_below, rau, sau, rbu, sbu, 1 + hop, has_up, to_up)
            pass_on(above, row_above, rad, sad, rbd, sbd, line + hop, has_down, to_down)
    for layer in range(layers):
        arrive(layer, z, 1 - x, span_a, rax.at[layer, 0])
        for hop in range(line - 1):
            from_below = z - 1 - hop
            from_above = z + 1 + hop
            pl.when(from_below >= 0)(
                functools.partial(
                    arrive, layer, jnp.maximum(from_below, 0), 1 - x, span_a, rax.at[layer, 1 + hop]
                )
            )
            pl.when(from_above < line)(
                functools.partial(
                    arrive, layer, jnp.minimum(from_above, line - 1), 1 - x, span_a, rax.at[layer, line + hop]
                )
            )

    @pl.when(section == 0)
    def _():
        pl.semaphore_signal(go_sem, inc=1, device_id={"section": 1}, device_id_type=MESH)

    for copy in locals_:
        copy.wait()
    for copy, condition in finish:
        if condition is None:
            copy.wait_send()
        else:
            pl.when(condition)(copy.wait_send)


def gather_weights(shard):
    layers, shard_rows, cols = shard.shape
    count = lax.axis_size("fsdp")
    line = count // 2
    dma = pltpu.SemaphoreType.DMA
    return pl.pallas_call(
        functools.partial(gather_kernel, line),
        out_shape=jax.ShapeDtypeStruct((layers, shard_rows * count, cols), shard.dtype),
        in_specs=[pl.BlockSpec(memory_space=pl.ANY)],
        out_specs=pl.BlockSpec(memory_space=pl.ANY),
        scratch_shapes=[
            dma((layers,)),
            pltpu.SemaphoreType.REGULAR,
            dma((layers, 2 * line - 1)),
            dma((layers, 2 * line - 1)),
            dma((layers, line - 1)),
            dma((layers, line - 1)),
            dma((layers, line - 1)),
            dma((layers, line - 1)),
            dma((layers,)),
            dma((layers,)),
            dma((layers, line - 1, 2)),
            dma((layers, line - 1, 2)),
            dma((layers, line - 1, 2)),
            dma((layers, line - 1, 2)),
        ],
        compiler_params=pltpu.CompilerParams(collective_id=0, has_side_effects=True),
        name="gather_weights",
    )(shard)


def add_into(target, source):
    rows = target.shape[0]

    @pl.loop(0, rows, step=16)
    def _(start):
        span = pl.ds(pl.multiple_of(start, 16), 16)
        target[span] = target[span] + source[span]


def scatter_kernel(
    line, d_ref, out_ref,
    sa, xa, ua, da, sb, ub, db, xb,
    load_a, load_b, sxa, rxa, sua, rua, sda, rda, sub, rub, sdb, rdb, sxb, rxb,
):
    layers, all_rows, cols = d_ref.shape
    shard_rows = all_rows // (2 * line)
    cols_a = cols - X_FIRST_COLS
    place = lax.axis_index("fsdp")
    z = place // 2
    x = lax.rem(place, 2)
    has_up = z < line - 1
    has_down = z > 0
    to_x = {"fsdp": z * 2 + 1 - x}
    to_up = {"fsdp": jnp.minimum(z + 1, line - 1) * 2 + x}
    to_down = {"fsdp": jnp.maximum(z - 1, 0) * 2 + x}

    barrier = pltpu.get_barrier_semaphore()
    pl.semaphore_signal(barrier, inc=1, device_id=to_x, device_id_type=MESH)

    @pl.when(has_up)
    def _():
        pl.semaphore_signal(barrier, inc=1, device_id=to_up, device_id_type=MESH)

    @pl.when(has_down)
    def _():
        pl.semaphore_signal(barrier, inc=1, device_id=to_down, device_id_type=MESH)

    pl.semaphore_wait(barrier, 1 + jnp.where(has_up, 1, 0) + jnp.where(has_down, 1, 0))

    span_a = pl.ds(0, cols_a)
    span_b = pl.ds(cols_a, X_FIRST_COLS)

    def part(layer, row_z, row_x, span):
        start = pl.multiple_of((row_z * 2 + row_x) * shard_rows, shard_rows)
        return d_ref.at[layer, pl.ds(start, shard_rows), span]

    def remote(source, target_ref, send_sem, recv_sem, target):
        return pltpu.make_async_remote_copy(
            src_ref=source, dst_ref=target_ref, send_sem=send_sem, recv_sem=recv_sem,
            device_id=target, device_id_type=MESH,
        )

    finish = []

    def launch(copy, condition=None):
        if condition is None:
            copy.start()
            finish.append((copy, None))
        else:
            pl.when(condition)(copy.start)
            finish.append((copy, condition))

    def arrived(buffer, sem):
        remote(buffer, buffer, sem, sem, to_x).wait_recv()

    loads = {}
    order = []
    for reach in range(line - 1, 0, -1):
        order.append((reach, 1, z + reach < line, jnp.minimum(z + reach, line - 1)))
        order.append((reach, 0, z - reach >= 0, jnp.maximum(z - reach, 0)))
    order.append((0, 0, None, z))
    for number, (reach, upward, live, row) in enumerate(order):
        for layer in range(layers):
            copy = pltpu.make_async_copy(part(layer, row, x, span_a), sa.at[layer, row], load_a.at[layer, number])
            both = pltpu.make_async_copy(
                d_ref.at[layer, pl.ds(pl.multiple_of(row * 2 * shard_rows, 2 * shard_rows), 2 * shard_rows), span_b],
                sb.at[layer, row],
                load_b.at[layer, number],
            )
            for local in (copy, both):
                if live is None:
                    local.start()
                else:
                    pl.when(live)(local.start)
            loads[number, layer] = (copy, both)
            launch(
                remote(part(layer, row, 1 - x, span_a), xa.at[layer, row], sxa.at[layer, number], rxa.at[layer, number], to_x),
                live,
            )
    for number, (reach, upward, live, row) in enumerate(order):
        for layer in range(layers):
            copy, both = loads[number, layer]
            if reach:
                wide, narrow = (ub, ua) if upward else (db, da)
                s_a, r_a, s_b, r_b = (sua, rua, sub, rub) if upward else (sda, rda, sdb, rdb)
                target = to_up if upward else to_down
                fed = (z > 0) if upward else (z < line - 1)
                slot = reach - 1

                def step(copy=copy, both=both, layer=layer, row=row, number=number, wide=wide, narrow=narrow,
                         r_a=r_a, r_b=r_b, fed=fed, slot=slot, reach=reach):
                    both.wait()
                    if reach < line - 1:

                        @pl.when(fed)
                        def _():
                            arrived(wide.at[layer, slot + 1], r_b.at[layer, slot + 1])
                            add_into(sb.at[layer, row], wide.at[layer, slot + 1])

                def step_a(copy=copy, layer=layer, row=row, number=number, narrow=narrow, r_a=r_a, fed=fed, slot=slot, reach=reach):
                    copy.wait()
                    arrived(xa.at[layer, row], rxa.at[layer, number])
                    add_into(sa.at[layer, row], xa.at[layer, row])
                    if reach < line - 1:

                        @pl.when(fed)
                        def _():
                            arrived(narrow.at[layer, slot + 1], r_a.at[layer, slot + 1])
                            add_into(sa.at[layer, row], narrow.at[layer, slot + 1])

                pl.when(live)(step)
                launch(remote(sb.at[layer, row], wide.at[layer, slot], s_b.at[layer, slot], r_b.at[layer, slot], target), live)
                pl.when(live)(step_a)
                launch(remote(sa.at[layer, row], narrow.at[layer, slot], s_a.at[layer, slot], r_a.at[layer, slot], target), live)
            else:
                both.wait()

                @pl.when(has_down)
                def _(layer=layer):
                    arrived(ub.at[layer, 0], rub.at[layer, 0])
                    add_into(sb.at[layer, z], ub.at[layer, 0])

                @pl.when(has_up)
                def _(layer=layer):
                    arrived(db.at[layer, 0], rdb.at[layer, 0])
                    add_into(sb.at[layer, z], db.at[layer, 0])

                theirs = pl.ds(pl.multiple_of((1 - x) * shard_rows, shard_rows), shard_rows)
                launch(remote(sb.at[layer, z, theirs], xb.at[layer], sxb.at[layer], rxb.at[layer], to_x))
                copy.wait()
                arrived(xa.at[layer, z], rxa.at[layer, number])
                add_into(sa.at[layer, z], xa.at[layer, z])

                @pl.when(has_down)
                def _(layer=layer):
                    arrived(ua.at[layer, 0], rua.at[layer, 0])
                    add_into(sa.at[layer, z], ua.at[layer, 0])

                @pl.when(has_up)
                def _(layer=layer):
                    arrived(da.at[layer, 0], rda.at[layer, 0])
                    add_into(sa.at[layer, z], da.at[layer, 0])

    for layer in range(layers):
        arrived(xb.at[layer], rxb.at[layer])

        @pl.loop(0, shard_rows, step=16)
        def _(start, layer=layer):
            span = pl.ds(pl.multiple_of(start, 16), 16)
            mine = pl.ds(pl.multiple_of(x * shard_rows + start, 16), 16)
            out_ref[layer, span, span_a] = sa[layer, z, span].astype(jnp.float32)
            out_ref[layer, span, span_b] = sb[layer, z, mine].astype(jnp.float32) + xb[layer, span].astype(jnp.float32)

    for copy, condition in finish:
        if condition is None:
            copy.wait_send()
        else:
            pl.when(condition)(copy.wait_send)


def scatter_grads(partial):
    layers, all_rows, cols = partial.shape
    count = lax.axis_size("fsdp")
    line = count // 2
    shard_rows = all_rows // count
    cols_a = cols - X_FIRST_COLS
    dma = pltpu.SemaphoreType.DMA
    low = partial.dtype
    slots = 2 * line - 1
    return pl.pallas_call(
        functools.partial(scatter_kernel, line),
        out_shape=jax.ShapeDtypeStruct((layers, shard_rows, cols), jnp.float32),
        in_specs=[pl.BlockSpec(memory_space=pl.ANY)],
        out_specs=pl.BlockSpec(memory_space=pltpu.VMEM),
        scratch_shapes=[
            pltpu.VMEM((layers, line, shard_rows, cols_a), low),
            pltpu.VMEM((layers, line, shard_rows, cols_a), low),
            pltpu.VMEM((layers, line - 1, shard_rows, cols_a), low),
            pltpu.VMEM((layers, line - 1, shard_rows, cols_a), low),
            pltpu.VMEM((layers, line, 2 * shard_rows, X_FIRST_COLS), low),
            pltpu.VMEM((layers, line - 1, 2 * shard_rows, X_FIRST_COLS), low),
            pltpu.VMEM((layers, line - 1, 2 * shard_rows, X_FIRST_COLS), low),
            pltpu.VMEM((layers, shard_rows, X_FIRST_COLS), low),
            dma((layers, slots)),
            dma((layers, slots)),
            dma((layers, slots)),
            dma((layers, slots)),
            dma((layers, line - 1)),
            dma((layers, line - 1)),
            dma((layers, line - 1)),
            dma((layers, line - 1)),
            dma((layers, line - 1)),
            dma((layers, line - 1)),
            dma((layers, line - 1)),
            dma((layers, line - 1)),
            dma((layers,)),
            dma((layers,)),
        ],
        compiler_params=pltpu.CompilerParams(
            collective_id=1, has_side_effects=True, vmem_limit_bytes=60 << 20
        ),
        name="scatter_grads",
    )(partial)


EPSILON = 1e-06


def shifted(value, axis, steps):
    count = lax.axis_size(axis)
    initial, last = (max(0, -steps), min(count, count - steps))
    return lax.ppermute(value, axis, [(source, source + steps) for source in range(initial, last)])


def layer_norm(hidden, weight_gain, weight_shift):
    average = jnp.mean(hidden, axis=-1, keepdims=True)
    centred = hidden - average
    spread = jnp.mean(centred * centred, axis=-1, keepdims=True)
    return centred * lax.rsqrt(spread + EPSILON) * weight_gain + weight_shift


def gelu_exact(upward):
    return jax.nn.gelu(upward, approximate=False)


def contract_last(left, right):
    return lax.dot_general(
        left, right, (((1,), (1,)), ((), ())), preferred_element_type=jnp.float32
    )


def contract_rows(left, right):
    return lax.dot_general(
        left, right, (((0,), (0,)), ((), ())), preferred_element_type=jnp.float32
    )


def mix_sum(partial_sum):
    return lax.psum(partial_sum.astype(jnp.bfloat16), "tensor").astype(jnp.float32)


def mix_back(partial_sum):
    return lax.psum(partial_sum.astype(jnp.bfloat16), "tensor").astype(jnp.float32)


def allowed_pairs(ids_batch):
    places = jnp.arange(ids_batch.shape[0], dtype=jnp.int32)
    same_image = (ids_batch[:, None] == ids_batch[None, :]) & (ids_batch[:, None] >= 0)
    return same_image | (places[:, None] == places[None, :])


def masked_scores(query_heads, key_rows, allowed):
    head_count = query_heads.shape[1]
    key_heads = key_rows.reshape(-1, head_count, HEAD_DIM)
    scores = jnp.einsum("qhe,khe->hqk", query_heads, key_heads, preferred_element_type=jnp.float32)
    scores = scores * (1.0 / math.sqrt(HEAD_DIM))
    return (jnp.where(allowed[None], scores, -1e30), key_heads)


def layer_slice(gathered, layer_index):
    return tuple((array[layer_index] for array in gathered))


def layer_forward(hidden, weights, ids_batch):
    qkv_w, out_w, up_w, down_w, gains, shifts, inner_part = weights
    row_count, model_width = hidden.shape
    head_width = out_w.shape[1]
    head_count = head_width // HEAD_DIM
    gains32 = gains.astype(jnp.float32)
    shifts32 = shifts.astype(jnp.float32)
    inner32 = inner_part[0].astype(jnp.float32)
    normed = layer_norm(hidden, gains32[0], shifts32[0]).astype(jnp.bfloat16)
    projected = jnp.dot(
        normed, qkv_w.reshape(model_width, 3 * head_width), preferred_element_type=jnp.float32
    ).reshape(row_count, 3, head_width)
    queries = (projected[:, 0] + inner32[:head_width]).astype(jnp.bfloat16)
    key_rows = projected[:, 1].astype(jnp.bfloat16)
    value_rows = (projected[:, 2] + inner32[head_width : 2 * head_width]).astype(jnp.bfloat16)
    allowed = allowed_pairs(ids_batch)
    scores, key_heads = masked_scores(
        queries.reshape(row_count, head_count, HEAD_DIM), key_rows, allowed
    )
    row_top = jnp.max(scores, axis=-1, keepdims=True)
    exponent = jnp.exp(scores - row_top)
    row_total = jnp.sum(exponent, axis=-1, keepdims=True)
    probs = (exponent / row_total).astype(jnp.bfloat16)
    log_total = row_top + jnp.log(row_total)
    value_heads = value_rows.reshape(-1, head_count, HEAD_DIM)
    mixed_heads = jnp.einsum("hqk,khe->qhe", probs, value_heads, preferred_element_type=jnp.float32)
    mixed_heads = mixed_heads.reshape(row_count, head_width).astype(jnp.bfloat16)
    attended = mix_sum(contract_last(mixed_heads, out_w)) + shifts32[1]
    middle = hidden + attended
    normed_mlp = layer_norm(middle, gains32[1], shifts32[2]).astype(jnp.bfloat16)
    upward = (
        jnp.dot(normed_mlp, up_w, preferred_element_type=jnp.float32) + inner32[2 * head_width :]
    )
    activated = gelu_exact(upward).astype(jnp.bfloat16)
    result = middle + (mix_sum(contract_last(activated, down_w)) + shifts32[3])
    kept = (hidden, queries, key_rows, value_rows, log_total, mixed_heads, middle, upward)
    return (result, kept)


def layer_backward(grad_out, kept, weights, ids_batch):
    qkv_w, out_w, up_w, down_w, gains, shifts, inner_part = weights
    hidden, queries, key_rows, value_rows, log_total, mixed_heads, middle, upward = kept
    row_count, model_width = hidden.shape
    head_width = out_w.shape[1]
    head_count = head_width // HEAD_DIM
    gains32 = gains.astype(jnp.float32)
    shifts32 = shifts.astype(jnp.float32)
    score_scale = 1.0 / math.sqrt(HEAD_DIM)
    grad_low = grad_out.astype(jnp.bfloat16)
    down_bias_grad = jnp.sum(grad_low.astype(jnp.float32), axis=0)
    activated, gelu_back = jax.vjp(gelu_exact, upward)
    activated = activated.astype(jnp.bfloat16)
    down_w_grad = contract_rows(grad_low, activated)
    grad_act = jnp.dot(grad_low, down_w, preferred_element_type=jnp.float32)
    grad_up = gelu_back(grad_act)[0].astype(jnp.bfloat16)
    up_bias_grad = jnp.sum(grad_up.astype(jnp.float32), axis=0)
    normed_mlp, second_back = jax.vjp(layer_norm, middle, gains32[1], shifts32[2])
    up_w_grad = contract_rows(normed_mlp.astype(jnp.bfloat16), grad_up)
    grad_norm = mix_back(contract_last(grad_up, up_w))
    middle_part, second_gain_grad, second_shift_grad = second_back(grad_norm)
    grad_middle = grad_out + middle_part
    grad_attn = grad_middle.astype(jnp.bfloat16)
    out_bias_grad = jnp.sum(grad_attn.astype(jnp.float32), axis=0)
    out_w_grad = contract_rows(grad_attn, mixed_heads)
    grad_mixed = jnp.dot(grad_attn, out_w, preferred_element_type=jnp.float32).astype(jnp.bfloat16)
    allowed = allowed_pairs(ids_batch)
    query_heads = queries.reshape(row_count, head_count, HEAD_DIM)
    scores, key_heads = masked_scores(query_heads, key_rows, allowed)
    probs = jnp.exp(scores - log_total)
    value_heads = value_rows.reshape(-1, head_count, HEAD_DIM)
    grad_mixed_heads = grad_mixed.reshape(row_count, head_count, HEAD_DIM)
    grad_probs = jnp.einsum(
        "qhe,khe->hqk", grad_mixed_heads, value_heads, preferred_element_type=jnp.float32
    )
    value_term = jnp.einsum(
        "hqk,qhe->khe",
        probs.astype(jnp.bfloat16),
        grad_mixed_heads,
        preferred_element_type=jnp.float32,
    )
    centre_term = jnp.sum(probs * grad_probs, axis=-1, keepdims=True)
    grad_scores = (probs * (grad_probs - centre_term)).astype(jnp.bfloat16)
    grad_queries = jnp.einsum(
        "hqk,khe->qhe", grad_scores, key_heads, preferred_element_type=jnp.float32
    )
    grad_queries = (grad_queries * score_scale).reshape(row_count, head_width).astype(jnp.bfloat16)
    key_term = jnp.einsum(
        "hqk,qhe->khe", grad_scores, query_heads, preferred_element_type=jnp.float32
    )
    grad_keys = (key_term * score_scale).reshape(row_count, head_width).astype(jnp.bfloat16)
    grad_values = value_term.reshape(row_count, head_width).astype(jnp.bfloat16)
    grad_qkv = jnp.stack([grad_queries, grad_keys, grad_values], axis=1).reshape(
        row_count, 3 * head_width
    )
    normed, first_back = jax.vjp(layer_norm, hidden, gains32[0], shifts32[0])
    qkv_w_grad = contract_rows(normed.astype(jnp.bfloat16), grad_qkv).reshape(
        model_width, 3, head_width
    )
    grad_normed = mix_back(contract_last(grad_qkv, qkv_w.reshape(model_width, 3 * head_width)))
    hidden_part, first_gain_grad, first_shift_grad = first_back(grad_normed)
    grad_in = grad_middle + hidden_part
    inner_grad = jnp.concatenate(
        [
            jnp.sum(grad_queries.astype(jnp.float32), axis=0),
            jnp.sum(grad_values.astype(jnp.float32), axis=0),
            up_bias_grad,
        ]
    )[None]
    layer_grads = (
        qkv_w_grad,
        out_w_grad,
        up_w_grad,
        down_w_grad,
        jnp.stack([first_gain_grad, second_gain_grad]),
        jnp.stack([first_shift_grad, out_bias_grad, second_shift_grad, down_bias_grad]),
        inner_grad,
    )
    return (grad_in, layer_grads)


SMALL_COLS = 128


def pack_shard(qkv_w, out_w, up_w, down_w, gains, shifts, inner_part):
    layers, rows = qkv_w.shape[:2]
    columns = jnp.concatenate([gains, shifts, inner_part.reshape(layers, -1, rows)], axis=1)
    columns = jnp.swapaxes(columns, 1, 2)
    columns = jnp.pad(columns, ((0, 0), (0, 0), (0, SMALL_COLS - columns.shape[2])))
    return jnp.concatenate([qkv_w.reshape(layers, rows, -1), out_w, up_w, down_w, columns], axis=2)


def unpack(full, head_width, hidden_width, count):
    layers, width, cols = full.shape
    ends = [3 * head_width, 4 * head_width, 4 * head_width + hidden_width, 4 * head_width + 2 * hidden_width]
    small = jnp.swapaxes(full[:, :, ends[3] : ends[3] + 9], 1, 2)
    inner = small[:, 6:].reshape(layers, 3, count, width // count)
    inner = jnp.swapaxes(inner, 1, 2).reshape(layers, 1, -1)
    return (
        full[:, :, : ends[0]].reshape(layers, width, 3, head_width),
        full[:, :, ends[0] : ends[1]],
        full[:, :, ends[1] : ends[2]],
        full[:, :, ends[2] : ends[3]],
        small[:, :2],
        small[:, 2:6],
        inner,
    )


def pack_grads(grads, count):
    qkv_g, out_g, up_g, down_g, gain_g, shift_g, inner_g = grads
    layers, width = qkv_g.shape[:2]
    inner = jnp.swapaxes(inner_g.reshape(layers, count, 3, width // count), 1, 2).reshape(layers, 3, width)
    small = jnp.swapaxes(jnp.concatenate([gain_g, shift_g, inner], axis=1), 1, 2)
    small = jnp.pad(small, ((0, 0), (0, 0), (0, SMALL_COLS - small.shape[2])))
    whole = jnp.concatenate([qkv_g.reshape(layers, width, -1), out_g, up_g, down_g, small], axis=2)
    return whole.astype(jnp.bfloat16)


def unpack_grads(full, head_width, hidden_width):
    layers, rows, cols = full.shape
    ends = [3 * head_width, 4 * head_width, 4 * head_width + hidden_width, 4 * head_width + 2 * hidden_width]
    small = jnp.swapaxes(full[:, :, ends[3] : ends[3] + 9], 1, 2)
    return (
        full[:, :, : ends[0]].reshape(layers, rows, 3, head_width),
        full[:, :, ends[0] : ends[1]],
        full[:, :, ends[1] : ends[2]],
        full[:, :, ends[2] : ends[3]],
        small[:, :2],
        small[:, 2:6],
        small[:, 6:].reshape(layers, 1, -1),
    )


def body(
    block_input,
    image_ids,
    qkv_weight,
    out_weight,
    up_weight,
    down_weight,
    norm_gains,
    biases,
    inner_bias,
    cotangent,
):
    section = lax.axis_index("section")
    micro_count = block_input.shape[0]
    layer_count = qkv_weight.shape[0]
    ticks = micro_count + 1
    shard = pack_shard(
        qkv_weight, out_weight, up_weight, down_weight, norm_gains, biases, inner_bias
    )
    gathered = unpack(gather_weights(shard), out_weight.shape[2], up_weight.shape[2], lax.axis_size("fsdp"))
    stored = []
    outputs = []
    received = jnp.zeros(block_input.shape[1:], jnp.bfloat16)
    for tick_index in range(ticks):
        micro_index = jnp.clip(tick_index - section, 0, micro_count - 1)
        ids_batch = lax.dynamic_index_in_dim(image_ids, micro_index, 0, keepdims=False)
        fresh = block_input[min(tick_index, micro_count - 1)]
        hidden = jnp.where(section == 0, fresh, received).astype(jnp.float32)
        kept_layers = []
        for layer_index in range(layer_count):
            hidden, kept = layer_forward(hidden, layer_slice(gathered, layer_index), ids_batch)
            kept_layers.append(kept)
        stored.append((ids_batch, kept_layers))
        outputs.append(hidden)
        if tick_index + 1 < ticks:
            received = shifted(hidden.astype(jnp.bfloat16), "section", 1)
    accumulated = None
    grad_inputs = []
    received = jnp.zeros(block_input.shape[1:], jnp.bfloat16)
    for tick_index in range(ticks):
        micro_index = micro_count - tick_index - section
        is_valid = (micro_index >= 0) & (micro_index < micro_count)
        fresh = cotangent[max(micro_count - 1 - tick_index, 0)]
        grad_out = jnp.where(section == 1, fresh, received).astype(jnp.float32)
        grad_out = jnp.where(is_valid, grad_out, jnp.zeros_like(grad_out))
        ids_batch, kept_layers = stored[micro_count - tick_index]
        per_layer = [None] * layer_count
        for layer_index in reversed(range(layer_count)):
            grad_out, per_layer[layer_index] = layer_backward(
                grad_out, kept_layers[layer_index], layer_slice(gathered, layer_index), ids_batch
            )
        tick_grads = tuple(
            (
                jnp.stack([per_layer[which_layer][member] for which_layer in range(layer_count)])
                for member in range(7)
            )
        )
        grad_inputs.append(grad_out)
        if tick_index + 1 < ticks:
            received = shifted(grad_out.astype(jnp.bfloat16), "section", -1)
        if accumulated is None:
            accumulated = tuple(tick_grads)
        else:
            accumulated = jax.tree.map(jnp.add, tuple(accumulated), tuple(tick_grads))
    accumulated = unpack_grads(
        scatter_grads(pack_grads(accumulated, lax.axis_size("fsdp"))), out_weight.shape[2], up_weight.shape[2]
    )
    block_outputs = jnp.stack([outputs[micro + 1] for micro in range(micro_count)])
    input_grads = jnp.stack([grad_inputs[micro_count - micro] for micro in range(micro_count)])
    section_ends = jnp.where(section == 0, input_grads, block_outputs)[None]
    return (
        section_ends,
        accumulated[0],
        accumulated[1],
        accumulated[2],
        accumulated[3],
        accumulated[4],
        accumulated[5],
        accumulated[6],
    )


def solution(mesh):
    placed = (
        P(None, "fsdp", None),
        P(None, "fsdp"),
        P("section", "fsdp", None, "tensor"),
        P("section", "fsdp", "tensor"),
        P("section", "fsdp", "tensor"),
        P("section", "fsdp", "tensor"),
        P("section", None, "fsdp"),
        P("section", None, "fsdp"),
        P("section", "tensor", "fsdp"),
        P(None, "fsdp", None),
    )
    return jax.shard_map(
        body,
        mesh=mesh,
        in_specs=placed,
        out_specs=(
            P("section", None, "fsdp", None),
            P("section", "fsdp", None, "tensor"),
            P("section", "fsdp", "tensor"),
            P("section", "fsdp", "tensor"),
            P("section", "fsdp", "tensor"),
            P("section", None, "fsdp"),
            P("section", None, "fsdp"),
            P("section", "tensor", "fsdp"),
        ),
        check_vma=False,
    )
```

```python
import functools
import math

import jax
import jax.numpy as jnp
from jax import lax
from jax.experimental import pallas as pl
from jax.experimental.pallas import tpu as pltpu
from jax.sharding import PartitionSpec as P

HEAD_DIM = 64
EPSILON = 1e-06


MESH = pl.DeviceIdType.MESH
X_FIRST_COLS = 1024


def gather_kernel(line, w_ref, g_ref, local_sem, go_sem, sax, rax, sau, rau, sad, rad, sbx, rbx, sbu, rbu, sbd, rbd):
    layers, shard_rows, cols = w_ref.shape
    cols_a = cols - X_FIRST_COLS
    section = lax.axis_index("section")
    place = lax.axis_index("fsdp")
    z = place // 2
    x = lax.rem(place, 2)
    has_up = z < line - 1
    has_down = z > 0
    to_x = {"fsdp": z * 2 + 1 - x}
    to_up = {"fsdp": jnp.minimum(z + 1, line - 1) * 2 + x}
    to_down = {"fsdp": jnp.maximum(z - 1, 0) * 2 + x}

    barrier = pltpu.get_barrier_semaphore()
    pl.semaphore_signal(barrier, inc=1, device_id=to_x, device_id_type=MESH)
    pl.semaphore_signal(barrier, inc=1, device_id={"section": 1 - section}, device_id_type=MESH)

    @pl.when(has_up)
    def _():
        pl.semaphore_signal(barrier, inc=1, device_id=to_up, device_id_type=MESH)

    @pl.when(has_down)
    def _():
        pl.semaphore_signal(barrier, inc=1, device_id=to_down, device_id_type=MESH)

    pl.semaphore_wait(barrier, 2 + jnp.where(has_up, 1, 0) + jnp.where(has_down, 1, 0))

    span_a = pl.ds(0, cols_a)
    span_b = pl.ds(cols_a, X_FIRST_COLS)

    def spot(layer, row_z, row_x, span):
        start = pl.multiple_of((row_z * 2 + row_x) * shard_rows, shard_rows)
        return g_ref.at[layer, pl.ds(start, shard_rows), span]

    def own(layer, span):
        return w_ref.at[layer, :, span]

    def send(source, layer, row_z, row_x, span, send_sem, recv_sem, target):
        return pltpu.make_async_remote_copy(
            src_ref=source,
            dst_ref=spot(layer, row_z, row_x, span),
            send_sem=send_sem,
            recv_sem=recv_sem,
            device_id=target,
            device_id_type=MESH,
        )

    def relay(layer, row_z, row_x, span, send_sem, recv_sem, target):
        return send(spot(layer, row_z, row_x, span), layer, row_z, row_x, span, send_sem, recv_sem, target)

    @pl.when(section == 1)
    def _():
        pl.semaphore_wait(go_sem, 1)

    finish = []

    def launch(copy, condition=None):
        if condition is None:
            copy.start()
            finish.append((copy, None))
        else:
            pl.when(condition)(copy.start)
            finish.append((copy, condition))

    locals_ = []
    for layer in range(layers):
        copy = pltpu.make_async_copy(
            w_ref.at[layer], spot(layer, z, x, pl.ds(0, cols)), local_sem.at[layer]
        )
        copy.start()
        locals_.append(copy)
        a, b = own(layer, span_a), own(layer, span_b)
        launch(send(b, layer, z, x, span_b, sbx.at[layer], rbx.at[layer], to_x))
        launch(send(a, layer, z, x, span_a, sau.at[layer, 0], rau.at[layer, 0], to_up), has_up)
        launch(send(a, layer, z, x, span_a, sad.at[layer, 0], rad.at[layer, 0], to_down), has_down)
        launch(send(a, layer, z, x, span_a, sax.at[layer, 0], rax.at[layer, 0], to_x))
        launch(send(b, layer, z, x, span_b, sbu.at[layer, 0, 0], rbu.at[layer, 0, 0], to_up), has_up)
        launch(send(b, layer, z, x, span_b, sbd.at[layer, 0, 0], rbd.at[layer, 0, 0], to_down), has_down)

    def arrive(layer, row_z, row_x, span, sem):
        relay(layer, row_z, row_x, span, sem, sem, to_x).wait_recv()

    for layer in range(layers):
        arrive(layer, z, 1 - x, span_b, rbx.at[layer])
        launch(relay(layer, z, 1 - x, span_b, sbu.at[layer, 0, 1], rbu.at[layer, 0, 1], to_up), has_up)
        launch(relay(layer, z, 1 - x, span_b, sbd.at[layer, 0, 1], rbd.at[layer, 0, 1], to_down), has_down)
    for hop in range(line - 1):
        for layer in range(layers):
            from_below = z - 1 - hop
            from_above = z + 1 + hop
            below = from_below >= 0
            above = from_above < line
            row_below = jnp.maximum(from_below, 0)
            row_above = jnp.minimum(from_above, line - 1)

            def pass_on(live, row, rau, sau, rbu, sbu, sem_place, onward, target, hop=hop, layer=layer):
                pl.when(live)(lambda: arrive(layer, row, x, span_a, rau.at[layer, hop]))
                launch(relay(layer, row, x, span_a, sax.at[layer, sem_place], rax.at[layer, sem_place], to_x), live)
                if hop + 1 < line - 1:
                    launch(
                        relay(layer, row, x, span_a, sau.at[layer, hop + 1], rau.at[layer, hop + 1], target),
                        live & onward,
                    )
                for side, row_x in ((0, x), (1, 1 - x)):
                    pl.when(live)(
                        functools.partial(arrive, layer, row, row_x, span_b, rbu.at[layer, hop, side])
                    )
                    if hop + 1 < line - 1:
                        launch(
                            relay(
                                layer, row, row_x, span_b,
                                sbu.at[layer, hop + 1, side], rbu.at[layer, hop + 1, side], target,
                            ),
                            live & onward,
                        )

            pass_on(below, row_below, rau, sau, rbu, sbu, 1 + hop, has_up, to_up)
            pass_on(above, row_above, rad, sad, rbd, sbd, line + hop, has_down, to_down)
    for layer in range(layers):
        arrive(layer, z, 1 - x, span_a, rax.at[layer, 0])
        for hop in range(line - 1):
            from_below = z - 1 - hop
            from_above = z + 1 + hop
            pl.when(from_below >= 0)(
                functools.partial(
                    arrive, layer, jnp.maximum(from_below, 0), 1 - x, span_a, rax.at[layer, 1 + hop]
                )
            )
            pl.when(from_above < line)(
                functools.partial(
                    arrive, layer, jnp.minimum(from_above, line - 1), 1 - x, span_a, rax.at[layer, line + hop]
                )
            )

    @pl.when(section == 0)
    def _():
        pl.semaphore_signal(go_sem, inc=1, device_id={"section": 1}, device_id_type=MESH)

    for copy in locals_:
        copy.wait()
    for copy, condition in finish:
        if condition is None:
            copy.wait_send()
        else:
            pl.when(condition)(copy.wait_send)


def gather_weights(shard):
    layers, shard_rows, cols = shard.shape
    count = lax.axis_size("fsdp")
    line = count // 2
    dma = pltpu.SemaphoreType.DMA
    return pl.pallas_call(
        functools.partial(gather_kernel, line),
        out_shape=jax.ShapeDtypeStruct((layers, shard_rows * count, cols), shard.dtype),
        in_specs=[pl.BlockSpec(memory_space=pl.ANY)],
        out_specs=pl.BlockSpec(memory_space=pl.ANY),
        scratch_shapes=[
            dma((layers,)),
            pltpu.SemaphoreType.REGULAR,
            dma((layers, 2 * line - 1)),
            dma((layers, 2 * line - 1)),
            dma((layers, line - 1)),
            dma((layers, line - 1)),
            dma((layers, line - 1)),
            dma((layers, line - 1)),
            dma((layers,)),
            dma((layers,)),
            dma((layers, line - 1, 2)),
            dma((layers, line - 1, 2)),
            dma((layers, line - 1, 2)),
            dma((layers, line - 1, 2)),
        ],
        compiler_params=pltpu.CompilerParams(collective_id=0, has_side_effects=True),
        name="gather_weights",
    )(shard)


def add_into(target, source):
    rows = target.shape[0]

    @pl.loop(0, rows, step=16)
    def _(start):
        span = pl.ds(pl.multiple_of(start, 16), 16)
        target[span] = target[span] + source[span]


def scatter_kernel(
    line, d_ref, out_ref,
    sa, xa, ua, da, sb, ub, db, xb,
    load_a, load_b, sxa, rxa, sua, rua, sda, rda, sub, rub, sdb, rdb, sxb, rxb,
):
    layers, all_rows, cols = d_ref.shape
    shard_rows = all_rows // (2 * line)
    cols_a = cols - X_FIRST_COLS
    place = lax.axis_index("fsdp")
    z = place // 2
    x = lax.rem(place, 2)
    has_up = z < line - 1
    has_down = z > 0
    to_x = {"fsdp": z * 2 + 1 - x}
    to_up = {"fsdp": jnp.minimum(z + 1, line - 1) * 2 + x}
    to_down = {"fsdp": jnp.maximum(z - 1, 0) * 2 + x}

    barrier = pltpu.get_barrier_semaphore()
    pl.semaphore_signal(barrier, inc=1, device_id=to_x, device_id_type=MESH)

    @pl.when(has_up)
    def _():
        pl.semaphore_signal(barrier, inc=1, device_id=to_up, device_id_type=MESH)

    @pl.when(has_down)
    def _():
        pl.semaphore_signal(barrier, inc=1, device_id=to_down, device_id_type=MESH)

    pl.semaphore_wait(barrier, 1 + jnp.where(has_up, 1, 0) + jnp.where(has_down, 1, 0))

    span_a = pl.ds(0, cols_a)
    span_b = pl.ds(cols_a, X_FIRST_COLS)

    def part(layer, row_z, row_x, span):
        start = pl.multiple_of((row_z * 2 + row_x) * shard_rows, shard_rows)
        return d_ref.at[layer, pl.ds(start, shard_rows), span]

    def remote(source, target_ref, send_sem, recv_sem, target):
        return pltpu.make_async_remote_copy(
            src_ref=source, dst_ref=target_ref, send_sem=send_sem, recv_sem=recv_sem,
            device_id=target, device_id_type=MESH,
        )

    finish = []

    def launch(copy, condition=None):
        if condition is None:
            copy.start()
            finish.append((copy, None))
        else:
            pl.when(condition)(copy.start)
            finish.append((copy, condition))

    def arrived(buffer, sem):
        remote(buffer, buffer, sem, sem, to_x).wait_recv()

    loads = {}
    order = []
    for reach in range(line - 1, 0, -1):
        order.append((reach, 1, z + reach < line, jnp.minimum(z + reach, line - 1)))
        order.append((reach, 0, z - reach >= 0, jnp.maximum(z - reach, 0)))
    order.append((0, 0, None, z))
    for number, (reach, upward, live, row) in enumerate(order):
        for layer in range(layers):
            copy = pltpu.make_async_copy(part(layer, row, x, span_a), sa.at[layer, row], load_a.at[layer, number])
            both = pltpu.make_async_copy(
                d_ref.at[layer, pl.ds(pl.multiple_of(row * 2 * shard_rows, 2 * shard_rows), 2 * shard_rows), span_b],
                sb.at[layer, row],
                load_b.at[layer, number],
            )
            for local in (copy, both):
                if live is None:
                    local.start()
                else:
                    pl.when(live)(local.start)
            loads[number, layer] = (copy, both)
            launch(
                remote(part(layer, row, 1 - x, span_a), xa.at[layer, row], sxa.at[layer, number], rxa.at[layer, number], to_x),
                live,
            )
    for number, (reach, upward, live, row) in enumerate(order):
        for layer in range(layers):
            copy, both = loads[number, layer]
            if reach:
                wide, narrow = (ub, ua) if upward else (db, da)
                s_a, r_a, s_b, r_b = (sua, rua, sub, rub) if upward else (sda, rda, sdb, rdb)
                target = to_up if upward else to_down
                fed = (z > 0) if upward else (z < line - 1)
                slot = reach - 1

                def step(copy=copy, both=both, layer=layer, row=row, number=number, wide=wide, narrow=narrow,
                         r_a=r_a, r_b=r_b, fed=fed, slot=slot, reach=reach):
                    both.wait()
                    if reach < line - 1:

                        @pl.when(fed)
                        def _():
                            arrived(wide.at[layer, slot + 1], r_b.at[layer, slot + 1])
                            add_into(sb.at[layer, row], wide.at[layer, slot + 1])

                def step_a(copy=copy, layer=layer, row=row, number=number, narrow=narrow, r_a=r_a, fed=fed, slot=slot, reach=reach):
                    copy.wait()
                    arrived(xa.at[layer, row], rxa.at[layer, number])
                    add_into(sa.at[layer, row], xa.at[layer, row])
                    if reach < line - 1:

                        @pl.when(fed)
                        def _():
                            arrived(narrow.at[layer, slot + 1], r_a.at[layer, slot + 1])
                            add_into(sa.at[layer, row], narrow.at[layer, slot + 1])

                pl.when(live)(step)
                launch(remote(sb.at[layer, row], wide.at[layer, slot], s_b.at[layer, slot], r_b.at[layer, slot], target), live)
                pl.when(live)(step_a)
                launch(remote(sa.at[layer, row], narrow.at[layer, slot], s_a.at[layer, slot], r_a.at[layer, slot], target), live)
            else:
                both.wait()

                @pl.when(has_down)
                def _(layer=layer):
                    arrived(ub.at[layer, 0], rub.at[layer, 0])
                    add_into(sb.at[layer, z], ub.at[layer, 0])

                @pl.when(has_up)
                def _(layer=layer):
                    arrived(db.at[layer, 0], rdb.at[layer, 0])
                    add_into(sb.at[layer, z], db.at[layer, 0])

                theirs = pl.ds(pl.multiple_of((1 - x) * shard_rows, shard_rows), shard_rows)
                launch(remote(sb.at[layer, z, theirs], xb.at[layer], sxb.at[layer], rxb.at[layer], to_x))
                copy.wait()
                arrived(xa.at[layer, z], rxa.at[layer, number])
                add_into(sa.at[layer, z], xa.at[layer, z])

                @pl.when(has_down)
                def _(layer=layer):
                    arrived(ua.at[layer, 0], rua.at[layer, 0])
                    add_into(sa.at[layer, z], ua.at[layer, 0])

                @pl.when(has_up)
                def _(layer=layer):
                    arrived(da.at[layer, 0], rda.at[layer, 0])
                    add_into(sa.at[layer, z], da.at[layer, 0])

    for layer in range(layers):
        arrived(xb.at[layer], rxb.at[layer])

        @pl.loop(0, shard_rows, step=16)
        def _(start, layer=layer):
            span = pl.ds(pl.multiple_of(start, 16), 16)
            mine = pl.ds(pl.multiple_of(x * shard_rows + start, 16), 16)
            out_ref[layer, span, span_a] = sa[layer, z, span].astype(jnp.float32)
            out_ref[layer, span, span_b] = sb[layer, z, mine].astype(jnp.float32) + xb[layer, span].astype(jnp.float32)

    for copy, condition in finish:
        if condition is None:
            copy.wait_send()
        else:
            pl.when(condition)(copy.wait_send)


def scatter_grads(partial):
    layers, all_rows, cols = partial.shape
    count = lax.axis_size("fsdp")
    line = count // 2
    shard_rows = all_rows // count
    cols_a = cols - X_FIRST_COLS
    dma = pltpu.SemaphoreType.DMA
    low = partial.dtype
    slots = 2 * line - 1
    return pl.pallas_call(
        functools.partial(scatter_kernel, line),
        out_shape=jax.ShapeDtypeStruct((layers, shard_rows, cols), jnp.float32),
        in_specs=[pl.BlockSpec(memory_space=pl.ANY)],
        out_specs=pl.BlockSpec(memory_space=pltpu.VMEM),
        scratch_shapes=[
            pltpu.VMEM((layers, line, shard_rows, cols_a), low),
            pltpu.VMEM((layers, line, shard_rows, cols_a), low),
            pltpu.VMEM((layers, line - 1, shard_rows, cols_a), low),
            pltpu.VMEM((layers, line - 1, shard_rows, cols_a), low),
            pltpu.VMEM((layers, line, 2 * shard_rows, X_FIRST_COLS), low),
            pltpu.VMEM((layers, line - 1, 2 * shard_rows, X_FIRST_COLS), low),
            pltpu.VMEM((layers, line - 1, 2 * shard_rows, X_FIRST_COLS), low),
            pltpu.VMEM((layers, shard_rows, X_FIRST_COLS), low),
            dma((layers, slots)),
            dma((layers, slots)),
            dma((layers, slots)),
            dma((layers, slots)),
            dma((layers, line - 1)),
            dma((layers, line - 1)),
            dma((layers, line - 1)),
            dma((layers, line - 1)),
            dma((layers, line - 1)),
            dma((layers, line - 1)),
            dma((layers, line - 1)),
            dma((layers, line - 1)),
            dma((layers,)),
            dma((layers,)),
        ],
        compiler_params=pltpu.CompilerParams(
            collective_id=1, has_side_effects=True, vmem_limit_bytes=60 << 20
        ),
        name="scatter_grads",
    )(partial)


SMALL_COLS = 128


def contract_last(left, right):
    return lax.dot_general(
        left, right, (((1,), (1,)), ((), ())), preferred_element_type=jnp.float32
    )


def contract_rows(left, right):
    return lax.dot_general(
        left, right, (((0,), (0,)), ((), ())), preferred_element_type=jnp.float32
    )


def shifted(value, axis, steps):
    count = lax.axis_size(axis)
    initial, last = (max(0, -steps), min(count, count - steps))
    return lax.ppermute(value, axis, [(source, source + steps) for source in range(initial, last)])


def pack_shard(qkv_w, out_w, up_w, down_w, gains, shifts, inner_part):
    layers, rows = qkv_w.shape[:2]
    columns = jnp.concatenate([gains, shifts, inner_part.reshape(layers, -1, rows)], axis=1)
    columns = jnp.swapaxes(columns, 1, 2)
    columns = jnp.pad(columns, ((0, 0), (0, 0), (0, SMALL_COLS - columns.shape[2])))
    return jnp.concatenate([qkv_w.reshape(layers, rows, -1), out_w, up_w, down_w, columns], axis=2)


def unpack_params(full, head_width, count):
    layers, width, cols = full.shape
    small = jnp.swapaxes(full[:, :, cols - SMALL_COLS : cols - SMALL_COLS + 9], 1, 2).astype(jnp.float32)
    inner = small[:, 6:].reshape(layers, 3, count, width // count)
    inner = jnp.swapaxes(inner, 1, 2).reshape(layers, 1, -1)
    query_bias, value_bias, up_bias = jnp.split(inner, [head_width, 2 * head_width], axis=2)
    qkv_bias = jnp.concatenate([query_bias, jnp.zeros_like(query_bias), value_bias], axis=2)
    return small[:, :6], qkv_bias, up_bias


LANES = 128


def forward_kernel(
    tick, has_alias, head_width, hidden_width, h0_ref, ids_col_ref, ids_row_ref, rows_ref, qkv_bias_ref, up_bias_ref, full_ref, *refs
):
    saved_count = 9
    if has_alias:
        refs = refs[saved_count:]
    outs = refs[:saved_count]
    (
        w_qkv, w_out, w_up, w_down, hid, qkv, lse, mixed, mid, act, slope, final, final_low,
        normed, mask, send, recv, w_sem, save_sem, send_sem, recv_sem,
    ) = refs[saved_count:]
    layers, micro, tokens, width = hid.shape
    section = lax.axis_index("section")
    partner = {"tensor": 1 - lax.axis_index("tensor")}

    @pl.when(section == tick)
    def _():
        ends = (0, 3 * head_width, 4 * head_width, 4 * head_width + hidden_width, 4 * head_width + 2 * hidden_width)

        def fetch(layer, index):
            buffer = (w_qkv, w_out, w_up, w_down)[index]
            return pltpu.make_async_copy(
                full_ref.at[layer, :, pl.ds(ends[index], ends[index + 1] - ends[index])],
                buffer.at[layer],
                w_sem.at[layer, index],
            )

        for layer in range(layers):
            for index in range(4):
                fetch(layer, index).start()
        barrier = pltpu.get_barrier_semaphore()
        pl.semaphore_signal(barrier, inc=1, device_id=partner, device_id_type=MESH)
        pl.semaphore_wait(barrier, 1)

        def save(index, source, layer, part):
            return pltpu.make_async_copy(source.at[layer, part], outs[index].at[layer, part], save_sem.at[index, layer, part])

        saves = ((0, hid), (1, qkv), (2, lse), (3, mixed), (4, mid), (5, act), (6, slope))

        def exchange(layer, stage, part):
            return pltpu.make_async_remote_copy(
                src_ref=send.at[layer, stage, part],
                dst_ref=recv.at[layer, stage, part],
                send_sem=send_sem.at[layer, stage, part],
                recv_sem=recv_sem.at[layer, stage, part],
                device_id=partner,
                device_id_type=MESH,
            )

        for part in range(micro):
            col = ids_col_ref[part]
            row = ids_row_ref[part]
            one = lax.broadcasted_iota(jnp.int32, (tokens, tokens), 0)
            two = lax.broadcasted_iota(jnp.int32, (tokens, tokens), 1)
            allowed = ((col == row) & (col >= 0)) | (one == two)
            mask[part] = jnp.where(allowed, 0.0, -1e30)

        def norm_rows(value, gain, shift):
            average = jnp.mean(value, axis=-1, keepdims=True)
            centred = value - average
            spread = jnp.mean(centred * centred, axis=-1, keepdims=True)
            return centred * lax.rsqrt(spread + EPSILON) * gain + shift

        def joined(layer, stage, part, span):
            return send[layer, stage, part, span].astype(jnp.float32) + recv[layer, stage, part, span].astype(jnp.float32)

        def attention_stage(layer, part):
            @pl.when(layer > 0)
            def _():
                exchange(layer - 1, 1, part).wait_recv()

                @pl.loop(0, tokens, step=32)
                def _(start):
                    span = pl.ds(pl.multiple_of(start, 32), 32)
                    hid[layer, part, span] = mid[layer - 1, part, span] + (
                        joined(layer - 1, 1, part, span) + rows_ref[layer - 1, 5:6]
                    )

            @pl.when(layer == 0)
            def _():
                @pl.loop(0, tokens, step=32)
                def _(start):
                    span = pl.ds(pl.multiple_of(start, 32), 32)
                    hid[layer, part, span] = h0_ref[part, span].astype(jnp.float32)

            @pl.loop(0, tokens, step=32)
            def _(start):
                span = pl.ds(pl.multiple_of(start, 32), 32)
                normed[span] = norm_rows(hid[layer, part, span], rows_ref[layer, 0:1], rows_ref[layer, 2:3]).astype(jnp.bfloat16)

            @pl.when(part == 0)
            def _():
                fetch(layer, 0).wait()

            for piece in range(3):
                @pl.loop(0, head_width, step=256)
                def _(start, piece=piece):
                    span = pl.ds(pl.multiple_of(piece * head_width + start, 256), 256)
                    value = jnp.dot(normed[...], w_qkv[layer, :, span], preferred_element_type=jnp.float32)
                    value = (value + qkv_bias_ref[layer, :, span]).astype(jnp.bfloat16)
                    if piece == 0:
                        value = value * jnp.asarray(1.0 / math.sqrt(HEAD_DIM), jnp.bfloat16)
                    qkv[layer, part, :, span] = value

            lane = lax.broadcasted_iota(jnp.int32, (tokens, LANES), 1)
            tops = []
            for pair in range(head_width // LANES):
                q2 = qkv[layer, part, :, pair * LANES : (pair + 1) * LANES]
                k2 = qkv[layer, part, :, head_width + pair * LANES : head_width + (pair + 1) * LANES]
                v2 = qkv[layer, part, :, 2 * head_width + pair * LANES : 2 * head_width + (pair + 1) * LANES]
                halves = []
                for side in range(2):
                    live = (lane < HEAD_DIM) if side == 0 else (lane >= HEAD_DIM)
                    scores = contract_last(jnp.where(live, q2, jnp.zeros_like(q2)), k2) + mask[part]
                    top = jnp.max(scores, axis=-1, keepdims=True)
                    exponent = jnp.exp(scores - top)
                    total = jnp.sum(exponent, axis=-1, keepdims=True)
                    probs = (exponent / total).astype(jnp.bfloat16)
                    halves.append(jnp.dot(probs, v2, preferred_element_type=jnp.float32))
                    head = 2 * pair + side
                    lse[layer, part, :, head : head + 1] = top + jnp.log(total)
                mixed[layer, part, :, pair * LANES : (pair + 1) * LANES] = jnp.where(
                    lane < HEAD_DIM, halves[0], halves[1]
                ).astype(jnp.bfloat16)

            @pl.when(part == 0)
            def _():
                fetch(layer, 1).wait()

            @pl.loop(0, width, step=256)
            def _(start):
                span = pl.ds(pl.multiple_of(start, 256), 256)
                value = contract_last(mixed[layer, part], w_out[layer, span])
                send[layer, 0, part, :, span] = value.astype(jnp.bfloat16)

            exchange(layer, 0, part).start()
            for index in range(4):
                save(index, saves[index][1], layer, part).start()

        def mlp_stage(layer, part):
            exchange(layer, 0, part).wait_recv()

            @pl.loop(0, tokens, step=32)
            def _(start):
                span = pl.ds(pl.multiple_of(start, 32), 32)
                middle = hid[layer, part, span] + (joined(layer, 0, part, span) + rows_ref[layer, 3:4])
                mid[layer, part, span] = middle
                normed[span] = norm_rows(middle, rows_ref[layer, 1:2], rows_ref[layer, 4:5]).astype(jnp.bfloat16)

            @pl.when(part == 0)
            def _():
                fetch(layer, 2).wait()

            @pl.loop(0, hidden_width, step=256)
            def _(start):
                span = pl.ds(pl.multiple_of(start, 256), 256)
                upward = jnp.dot(normed[...], w_up[layer, :, span], preferred_element_type=jnp.float32)
                upward = upward + up_bias_ref[layer, :, span]
                phi = 0.5 + 0.5 * lax.erf(upward * math.sqrt(0.5))
                density = jnp.exp(-0.5 * upward * upward) * (1.0 / math.sqrt(2.0 * math.pi))
                act[layer, part, :, span] = (upward * phi).astype(jnp.bfloat16)
                slope[layer, part, :, span] = (phi + upward * density).astype(jnp.bfloat16)

            @pl.when(part == 0)
            def _():
                fetch(layer, 3).wait()

            @pl.loop(0, width, step=256)
            def _(start):
                span = pl.ds(pl.multiple_of(start, 256), 256)
                value = contract_last(act[layer, part], w_down[layer, span])
                send[layer, 1, part, :, span] = value.astype(jnp.bfloat16)

            exchange(layer, 1, part).start()
            for index in range(4, 7):
                save(index, saves[index][1], layer, part).start()

        @pl.loop(0, layers)
        def _(layer):
            @pl.loop(0, micro)
            def _(part):
                attention_stage(layer, part)

            @pl.loop(0, micro)
            def _(part):
                mlp_stage(layer, part)

        last = layers - 1

        @pl.loop(0, micro)
        def _(part):
            exchange(last, 1, part).wait_recv()

            @pl.loop(0, tokens, step=32)
            def _(start):
                span = pl.ds(pl.multiple_of(start, 32), 32)
                value = mid[last, part, span] + (joined(last, 1, part, span) + rows_ref[last, 5:6])
                final[part, span] = value
                final_low[part, span] = value.astype(jnp.bfloat16)

        ending = [
            pltpu.make_async_copy(final, outs[7], save_sem.at[7, 0, 0]),
            pltpu.make_async_copy(final_low, outs[8], save_sem.at[8, 0, 0]),
        ]
        for copy in ending:
            copy.start()

        @pl.loop(0, layers)
        def _(layer):
            @pl.loop(0, micro)
            def _(part):
                for stage in range(2):
                    exchange(layer, stage, part).wait_send()
                for index, source in saves:
                    save(index, source, layer, part).wait()

        for copy in ending:
            copy.wait()


def saved_shapes(layers, micro, tokens, width, head_width, hidden_width):
    low, full = jnp.bfloat16, jnp.float32
    heads = head_width // HEAD_DIM
    return (
        ((layers, micro, tokens, width), full),
        ((layers, micro, tokens, 3 * head_width), low),
        ((layers, micro, tokens, heads), full),
        ((layers, micro, tokens, head_width), low),
        ((layers, micro, tokens, width), full),
        ((layers, micro, tokens, hidden_width), low),
        ((layers, micro, tokens, hidden_width), low),
        ((micro, tokens, width), full),
        ((micro, tokens, width), low),
    )


def forward(tick, h0, ids, params, full, previous, head_width, hidden_width):
    rows, qkv_bias, up_bias = params
    layers, width = full.shape[:2]
    micro, tokens = ids.shape
    shapes = saved_shapes(layers, micro, tokens, width, head_width, hidden_width)
    vmem = pl.BlockSpec(memory_space=pltpu.VMEM)
    hbm = pl.BlockSpec(memory_space=pl.ANY)
    dma = pltpu.SemaphoreType.DMA
    low = jnp.bfloat16
    aliased = () if previous is None else tuple(previous)
    return pl.pallas_call(
        functools.partial(forward_kernel, tick, previous is not None, head_width, hidden_width),
        out_shape=[jax.ShapeDtypeStruct(shape, kind) for shape, kind in shapes],
        in_specs=[vmem] * 6 + [hbm] * (1 + len(aliased)),
        out_specs=[hbm] * len(shapes),
        input_output_aliases={7 + number: number for number in range(len(aliased))},
        scratch_shapes=[
            pltpu.VMEM((layers, width, 3 * head_width), low),
            pltpu.VMEM((layers, width, head_width), low),
            pltpu.VMEM((layers, width, hidden_width), low),
            pltpu.VMEM((layers, width, hidden_width), low),
            *(pltpu.VMEM(shape, kind) for shape, kind in shapes),
            pltpu.VMEM((tokens, width), low),
            pltpu.VMEM((micro, tokens, tokens), jnp.float32),
            pltpu.VMEM((layers, 2, micro, tokens, width), low),
            pltpu.VMEM((layers, 2, micro, tokens, width), low),
            dma((layers, 4)),
            dma((len(shapes), layers, micro)),
            dma((layers, 2, micro)),
            dma((layers, 2, micro)),
        ],
        compiler_params=pltpu.CompilerParams(
            collective_id=2 + tick, has_side_effects=True, vmem_limit_bytes=62 << 20
        ),
        name="forward",
    )(h0, ids[:, :, None], ids[:, None, :], rows, qkv_bias, up_bias, full, *aliased)


def backward_kernel(
    tick, has_alias, head_width, hidden_width, g0_ref, ids_col_ref, ids_row_ref, rows_ref, full_ref, *refs
):
    saves = refs[:7]
    refs = refs[7:]
    out_count = 6
    if has_alias:
        refs = refs[out_count:]
    d_out, small_out, qkv_bias_out, up_bias_out, g_out, low_out = refs[:out_count]
    (
        w_qkv, w_out, w_up, w_down, hid, qkv, lse, mixed, mid, act, slope, grad, low, hidden_grad, qkv_grad, normed,
        mixed_grad, mask, send, recv, stage, small, qkv_bias, up_bias,
        w_sem, load_sem, send_sem, recv_sem, stage_sem, end_sem,
    ) = refs[out_count:]
    held = (hid, qkv, lse, mixed, mid, act, slope)
    layers, micro, tokens, width = hid.shape
    section = lax.axis_index("section")
    partner = {"tensor": 1 - lax.axis_index("tensor")}
    tile = 256
    scale = 1.0 / math.sqrt(HEAD_DIM)

    @pl.when(section == 1 - tick)
    def _():
        ends = (0, 3 * head_width, 4 * head_width, 4 * head_width + hidden_width, 4 * head_width + 2 * hidden_width)

        def fetch(layer, index):
            buffer = (w_qkv, w_out, w_up, w_down)[index]
            return pltpu.make_async_copy(
                full_ref.at[layer, :, pl.ds(ends[index], ends[index + 1] - ends[index])], buffer, w_sem.at[index]
            )

        def load(index, layer):
            return pltpu.make_async_copy(saves[index].at[layer], held[index].at[layer], load_sem.at[index, layer])

        last = layers - 1
        fetch(last, 3).start()
        load(6, last).start()
        fetch(last, 2).start()
        for index in (5, 4):
            load(index, last).start()
        fetch(last, 1).start()
        for index in (1, 2, 3, 0):
            load(index, last).start()
        fetch(last, 0).start()
        for layer in range(last - 1, -1, -1):
            for index in range(7):
                load(index, layer).start()
        barrier = pltpu.get_barrier_semaphore()
        pl.semaphore_signal(barrier, inc=1, device_id=partner, device_id_type=MESH)
        pl.semaphore_wait(barrier, 1)

        small[...] = jnp.zeros_like(small)
        qkv_bias[...] = jnp.zeros_like(qkv_bias)
        up_bias[...] = jnp.zeros_like(up_bias)
        for part in range(micro):
            col = ids_col_ref[part]
            row = ids_row_ref[part]
            one = lax.broadcasted_iota(jnp.int32, (tokens, tokens), 0)
            two = lax.broadcasted_iota(jnp.int32, (tokens, tokens), 1)
            allowed = ((col == row) & (col >= 0)) | (one == two)
            mask[part] = jnp.where(allowed, 0.0, -1e30)
            grad[part] = g0_ref[part].astype(jnp.float32)

        def exchange(layer, step, part):
            return pltpu.make_async_remote_copy(
                src_ref=send.at[layer, step, part],
                dst_ref=recv.at[layer, step, part],
                send_sem=send_sem.at[layer, step, part],
                recv_sem=recv_sem.at[layer, step, part],
                device_id=partner,
                device_id_type=MESH,
            )

        def rows_of(part):
            return pl.ds(pl.multiple_of(part * tokens, tokens), tokens)

        def column_sum(value):
            return jnp.sum(value.astype(jnp.float32), axis=0, keepdims=True)

        def norm_parts(value):
            average = jnp.mean(value, axis=-1, keepdims=True)
            centred = value - average
            spread = jnp.mean(centred * centred, axis=-1, keepdims=True)
            inverse = lax.rsqrt(spread + EPSILON)
            return centred * inverse, inverse

        def norm_back(layer, step, part, source, gain_row, shift_row):
            gain = rows_ref[layer, gain_row : gain_row + 1]

            @pl.loop(0, tokens, step=32)
            def _(start):
                span = pl.ds(pl.multiple_of(start, 32), 32)
                outer = send[layer, step, part, span].astype(jnp.float32) + recv[layer, step, part, span].astype(jnp.float32)
                unit, inverse = norm_parts(source[layer, part, span])
                inner = outer * gain
                first = jnp.mean(inner, axis=-1, keepdims=True)
                second = jnp.mean(inner * unit, axis=-1, keepdims=True)
                small[layer, gain_row : gain_row + 1] += column_sum(outer * unit)
                small[layer, shift_row : shift_row + 1] += column_sum(outer)
                grad[part, span] = grad[part, span] + inverse * (inner - first - unit * second)

        def renorm(layer, part, source, gain_row, shift_row):
            @pl.loop(0, tokens, step=32)
            def _(start):
                span = pl.ds(pl.multiple_of(start, 32), 32)
                unit, _ = norm_parts(source[layer, part, span])
                value = unit * rows_ref[layer, gain_row : gain_row + 1] + rows_ref[layer, shift_row : shift_row + 1]
                normed[pl.ds(pl.multiple_of(part * tokens + start, 32), 32)] = value.astype(jnp.bfloat16)

        def round_grad(layer, part, bias_row):
            @pl.loop(0, tokens, step=32)
            def _(start):
                span = pl.ds(pl.multiple_of(start, 32), 32)
                value = grad[part, span].astype(jnp.bfloat16)
                low[pl.ds(pl.multiple_of(part * tokens + start, 32), 32)] = value
                small[layer, bias_row : bias_row + 1] += column_sum(value)

        def put(layer, number, group):
            start = (2 * head_width + 2 * head_width, 4 * head_width + hidden_width, 0)[group]
            return pltpu.make_async_copy(
                stage.at[number],
                d_out.at[layer, pl.ds(pl.multiple_of(number * tile, tile), tile), pl.ds(start, stage.shape[2])],
                stage_sem.at[number],
            )

        def mlp_stage(layer, part):
            round_grad(layer, part, 5)

            @pl.when(part == 0)
            def _():
                fetch(layer, 3).wait()
                load(6, layer).wait()

            @pl.loop(0, hidden_width, step=tile)
            def _(start):
                span = pl.ds(pl.multiple_of(start, tile), tile)
                value = jnp.dot(low[rows_of(part)], w_down[:, span], preferred_element_type=jnp.float32)
                value = (value * slope[layer, part, :, span].astype(jnp.float32)).astype(jnp.bfloat16)
                hidden_grad[rows_of(part), span] = value
                up_bias[layer, :, span] += column_sum(value)

            @pl.when(part == 0)
            def _():
                fetch(layer, 2).wait()

            @pl.loop(0, width, step=tile)
            def _(start):
                span = pl.ds(pl.multiple_of(start, tile), tile)
                value = contract_last(hidden_grad[rows_of(part)], w_up[span])
                send[layer, 0, part, :, span] = value.astype(jnp.bfloat16)

            exchange(layer, 0, part).start()

        def weight_tiles(layer, group, free, fill):
            @pl.loop(0, width // tile)
            def _(number):
                pl.when(free)(lambda: put(layer, number, group).wait())
                fill(number, pl.ds(pl.multiple_of(number * tile, tile), tile))
                put(layer, number, group).start()

        def attention_stage(layer, part):
            exchange(layer, 0, part).wait_recv()
            norm_back(layer, 0, part, mid, 1, 4)
            round_grad(layer, part, 3)

            @pl.when(part == 0)
            def _():
                fetch(layer, 1).wait()
                load(1, layer).wait()
                load(2, layer).wait()

            @pl.loop(0, head_width, step=tile)
            def _(start):
                span = pl.ds(pl.multiple_of(start, tile), tile)
                value = jnp.dot(low[rows_of(part)], w_out[:, span], preferred_element_type=jnp.float32)
                mixed_grad[:, span] = value.astype(jnp.bfloat16)

            lane = lax.broadcasted_iota(jnp.int32, (tokens, LANES), 1)
            for pair in range(head_width // LANES):
                spans = [pl.ds(piece * head_width + pair * LANES, LANES) for piece in range(3)]
                q2, k2, v2 = (qkv[layer, part, :, span] for span in spans)
                go2 = mixed_grad[:, pair * LANES : (pair + 1) * LANES]
                halves = []
                for side in range(2):
                    live = (lane < HEAD_DIM) if side == 0 else (lane >= HEAD_DIM)
                    head = 2 * pair + side
                    scores = contract_last(jnp.where(live, q2, jnp.zeros_like(q2)), k2) + mask[part]
                    probs = jnp.exp(scores - lse[layer, part, :, head : head + 1])
                    outer = contract_last(jnp.where(live, go2, jnp.zeros_like(go2)), v2)
                    centre = jnp.sum(probs * outer, axis=-1, keepdims=True)
                    inner = (probs * (outer - centre)).astype(jnp.bfloat16)
                    halves.append((
                        jnp.dot(inner, k2, preferred_element_type=jnp.float32) * scale,
                        contract_rows(inner, q2),
                        contract_rows(probs.astype(jnp.bfloat16), go2),
                    ))
                for piece in range(3):
                    value = jnp.where(lane < HEAD_DIM, halves[0][piece], halves[1][piece]).astype(jnp.bfloat16)
                    qkv_grad[rows_of(part), spans[piece]] = value
                    qkv_bias[layer, :, spans[piece]] += column_sum(value)

            @pl.when(part == 0)
            def _():
                fetch(layer, 0).wait()

            @pl.loop(0, width, step=tile)
            def _(start):
                span = pl.ds(pl.multiple_of(start, tile), tile)
                value = contract_last(qkv_grad[rows_of(part)], w_qkv[span])
                send[layer, 1, part, :, span] = value.astype(jnp.bfloat16)

            exchange(layer, 1, part).start()

        @pl.loop(0, layers)
        def _(turn):
            layer = layers - 1 - turn

            @pl.loop(0, micro)
            def _(part):
                mlp_stage(layer, part)

            @pl.when(layer > 0)
            def _():
                fetch(layer - 1, 3).start()
                fetch(layer - 1, 2).start()

            load(5, layer).wait()

            def fill_down(number, span):
                both = act[layer].reshape(micro * tokens, hidden_width)
                stage[number] = contract_rows(low[:, span], both).astype(jnp.bfloat16)

            weight_tiles(layer, 1, turn > 0, fill_down)
            load(4, layer).wait()

            @pl.loop(0, micro)
            def _(part):
                renorm(layer, part, mid, 1, 4)

            def fill_up(number, span):
                stage[number] = contract_rows(normed[:, span], hidden_grad[...]).astype(jnp.bfloat16)

            weight_tiles(layer, 0, turn >= 0, fill_up)

            @pl.loop(0, micro)
            def _(part):
                attention_stage(layer, part)

            @pl.when(layer > 0)
            def _():
                fetch(layer - 1, 1).start()
                fetch(layer - 1, 0).start()

            load(3, layer).wait()
            load(0, layer).wait()

            @pl.loop(0, micro)
            def _(part):
                renorm(layer, part, hid, 0, 2)

            def fill_attention(number, span):
                both = mixed[layer].reshape(micro * tokens, head_width)
                stage[number, :, : 3 * head_width] = contract_rows(normed[:, span], qkv_grad[...]).astype(jnp.bfloat16)
                stage[number, :, 3 * head_width :] = contract_rows(low[:, span], both).astype(jnp.bfloat16)

            weight_tiles(layer, 2, turn >= 0, fill_attention)

            @pl.loop(0, micro)
            def _(part):
                exchange(layer, 1, part).wait_recv()
                norm_back(layer, 1, part, hid, 0, 2)

        for part in range(micro):
            low[pl.ds(part * tokens, tokens)] = grad[part].astype(jnp.bfloat16)
        ending = [
            pltpu.make_async_copy(small, small_out, end_sem.at[0]),
            pltpu.make_async_copy(qkv_bias, qkv_bias_out, end_sem.at[1]),
            pltpu.make_async_copy(up_bias, up_bias_out, end_sem.at[2]),
            pltpu.make_async_copy(grad, g_out, end_sem.at[3]),
            pltpu.make_async_copy(low, low_out, end_sem.at[4]),
        ]
        for copy in ending:
            copy.start()
        for number in range(width // tile):
            put(0, number, 2).wait()

        @pl.loop(0, layers)
        def _(layer):
            @pl.loop(0, micro)
            def _(part):
                for step in range(2):
                    exchange(layer, step, part).wait_send()

        for copy in ending:
            copy.wait()


def backward(tick, g0, ids, params, full, saves, previous, head_width, hidden_width):
    rows, qkv_bias, up_bias = params
    layers, width, cols = full.shape
    micro, tokens = ids.shape
    shapes = saved_shapes(layers, micro, tokens, width, head_width, hidden_width)
    vmem = pl.BlockSpec(memory_space=pltpu.VMEM)
    hbm = pl.BlockSpec(memory_space=pl.ANY)
    dma = pltpu.SemaphoreType.DMA
    low, wide = jnp.bfloat16, jnp.float32
    outs = (
        ((layers, width, cols), low),
        ((layers, 8, width), wide),
        ((layers, 1, 3 * head_width), wide),
        ((layers, 1, hidden_width), wide),
        ((micro, tokens, width), wide),
        ((micro * tokens, width), low),
    )
    aliased = () if previous is None else tuple(previous)
    return pl.pallas_call(
        functools.partial(backward_kernel, tick, previous is not None, head_width, hidden_width),
        out_shape=[jax.ShapeDtypeStruct(shape, kind) for shape, kind in outs],
        in_specs=[vmem] * 4 + [hbm] * (8 + len(aliased)),
        out_specs=[hbm] * len(outs),
        input_output_aliases={12 + number: number for number in range(len(aliased))},
        scratch_shapes=[
            pltpu.VMEM((width, 3 * head_width), low),
            pltpu.VMEM((width, head_width), low),
            pltpu.VMEM((width, hidden_width), low),
            pltpu.VMEM((width, hidden_width), low),
            *(pltpu.VMEM(shape, kind) for shape, kind in shapes[:7]),
            pltpu.VMEM((micro, tokens, width), wide),
            pltpu.VMEM((micro * tokens, width), low),
            pltpu.VMEM((micro * tokens, hidden_width), low),
            pltpu.VMEM((micro * tokens, 3 * head_width), low),
            pltpu.VMEM((micro * tokens, width), low),
            pltpu.VMEM((tokens, head_width), low),
            pltpu.VMEM((micro, tokens, tokens), wide),
            pltpu.VMEM((layers, 2, micro, tokens, width), low),
            pltpu.VMEM((layers, 2, micro, tokens, width), low),
            pltpu.VMEM((width // 256, 256, 4 * head_width), low),
            pltpu.VMEM((layers, 8, width), wide),
            pltpu.VMEM((layers, 1, 3 * head_width), wide),
            pltpu.VMEM((layers, 1, hidden_width), wide),
            dma((4,)),
            dma((7, layers)),
            dma((layers, 2, micro)),
            dma((layers, 2, micro)),
            dma((width // 256,)),
            dma((5,)),
        ],
        compiler_params=pltpu.CompilerParams(
            collective_id=4 + tick, has_side_effects=True, vmem_limit_bytes=62 << 20
        ),
        name="backward",
    )(g0, ids[:, :, None], ids[:, None, :], rows, full, *saves, *aliased)


def pack_small(small, qkv_bias, up_bias, head_width, count):
    layers, _, width = small.shape
    inner = jnp.concatenate(
        [qkv_bias[:, 0, :head_width], qkv_bias[:, 0, 2 * head_width :], up_bias[:, 0]], axis=1
    )
    inner = jnp.swapaxes(inner.reshape(layers, count, 3, width // count), 1, 2).reshape(layers, 3, width)
    columns = jnp.swapaxes(jnp.concatenate([small[:, :6], inner], axis=1), 1, 2)
    return jnp.pad(columns, ((0, 0), (0, 0), (0, SMALL_COLS - columns.shape[2]))).astype(jnp.bfloat16)


def unpack_grads(full, head_width, hidden_width):
    layers, rows, cols = full.shape
    ends = [3 * head_width, 4 * head_width, 4 * head_width + hidden_width, 4 * head_width + 2 * hidden_width]
    small = jnp.swapaxes(full[:, :, ends[3] : ends[3] + 9], 1, 2)
    return (
        full[:, :, : ends[0]].reshape(layers, rows, 3, head_width),
        full[:, :, ends[0] : ends[1]],
        full[:, :, ends[1] : ends[2]],
        full[:, :, ends[2] : ends[3]],
        small[:, :2],
        small[:, 2:6],
        small[:, 6:].reshape(layers, 1, -1),
    )


def body(
    block_input,
    image_ids,
    qkv_weight,
    out_weight,
    up_weight,
    down_weight,
    norm_gains,
    biases,
    inner_bias,
    cotangent,
):
    section = lax.axis_index("section")
    count = lax.axis_size("fsdp")
    head_width, hidden_width = out_weight.shape[2], up_weight.shape[2]
    shard = pack_shard(qkv_weight, out_weight, up_weight, down_weight, norm_gains, biases, inner_bias)
    full = gather_weights(shard)
    params = unpack_params(full, head_width, count)
    saved = forward(0, block_input, image_ids, params, full, None, head_width, hidden_width)
    received = shifted(saved[8], "section", 1)
    saved = forward(1, received, image_ids, params, full, saved, head_width, hidden_width)
    grads = backward(0, cotangent, image_ids, params, full, saved[:7], None, head_width, hidden_width)
    received = shifted(grads[5], "section", -1).reshape(cotangent.shape)
    grads = backward(1, received, image_ids, params, full, saved[:7], grads, head_width, hidden_width)
    partial, small, qkv_bias, up_bias, input_grad, _ = grads
    columns = pack_small(small, qkv_bias, up_bias, head_width, count)
    partial = lax.dynamic_update_slice(partial, columns, (0, 0, partial.shape[2] - SMALL_COLS))
    summed = unpack_grads(scatter_grads(partial), head_width, hidden_width)
    section_ends = jnp.where(section == 0, input_grad, saved[7])[None]
    return (section_ends, *summed)


def solution(mesh):
    placed = (
        P(None, "fsdp", None),
        P(None, "fsdp"),
        P("section", "fsdp", None, "tensor"),
        P("section", "fsdp", "tensor"),
        P("section", "fsdp", "tensor"),
        P("section", "fsdp", "tensor"),
        P("section", None, "fsdp"),
        P("section", None, "fsdp"),
        P("section", "tensor", "fsdp"),
        P(None, "fsdp", None),
    )
    return jax.shard_map(
        body,
        mesh=mesh,
        in_specs=placed,
        out_specs=(
            P("section", None, "fsdp", None),
            P("section", "fsdp", None, "tensor"),
            P("section", "fsdp", "tensor"),
            P("section", "fsdp", "tensor"),
            P("section", "fsdp", "tensor"),
            P("section", None, "fsdp"),
            P("section", None, "fsdp"),
            P("section", "tensor", "fsdp"),
        ),
        check_vma=False,
    )
```

```python
import functools
import math

import jax
import jax.numpy as jnp
from jax import lax
from jax.experimental import pallas as pl
from jax.experimental.pallas import tpu as pltpu
from jax.sharding import PartitionSpec as P

HEAD_DIM = 64
EPSILON = 1e-06


MESH = pl.DeviceIdType.MESH
X_FIRST_COLS = 1024


def gather_kernel(line, w_ref, g_ref, local_sem, go_sem, sax, rax, sau, rau, sad, rad, sbx, rbx, sbu, rbu, sbd, rbd):
    layers, shard_rows, cols = w_ref.shape
    cols_a = cols - X_FIRST_COLS
    section = lax.axis_index("section")
    place = lax.axis_index("fsdp")
    z = place // 2
    x = lax.rem(place, 2)
    has_up = z < line - 1
    has_down = z > 0
    to_x = {"fsdp": z * 2 + 1 - x}
    to_up = {"fsdp": jnp.minimum(z + 1, line - 1) * 2 + x}
    to_down = {"fsdp": jnp.maximum(z - 1, 0) * 2 + x}

    barrier = pltpu.get_barrier_semaphore()
    pl.semaphore_signal(barrier, inc=1, device_id=to_x, device_id_type=MESH)
    pl.semaphore_signal(barrier, inc=1, device_id={"section": 1 - section}, device_id_type=MESH)

    @pl.when(has_up)
    def _():
        pl.semaphore_signal(barrier, inc=1, device_id=to_up, device_id_type=MESH)

    @pl.when(has_down)
    def _():
        pl.semaphore_signal(barrier, inc=1, device_id=to_down, device_id_type=MESH)

    pl.semaphore_wait(barrier, 2 + jnp.where(has_up, 1, 0) + jnp.where(has_down, 1, 0))

    span_a = pl.ds(0, cols_a)
    span_b = pl.ds(cols_a, X_FIRST_COLS)

    def spot(layer, row_z, row_x, span):
        start = pl.multiple_of((row_z * 2 + row_x) * shard_rows, shard_rows)
        return g_ref.at[layer, pl.ds(start, shard_rows), span]

    def own(layer, span):
        return w_ref.at[layer, :, span]

    def send(source, layer, row_z, row_x, span, send_sem, recv_sem, target):
        return pltpu.make_async_remote_copy(
            src_ref=source,
            dst_ref=spot(layer, row_z, row_x, span),
            send_sem=send_sem,
            recv_sem=recv_sem,
            device_id=target,
            device_id_type=MESH,
        )

    def relay(layer, row_z, row_x, span, send_sem, recv_sem, target):
        return send(spot(layer, row_z, row_x, span), layer, row_z, row_x, span, send_sem, recv_sem, target)

    @pl.when(section == 1)
    def _():
        pl.semaphore_wait(go_sem, 1)

    finish = []

    def launch(copy, condition=None):
        if condition is None:
            copy.start()
            finish.append((copy, None))
        else:
            pl.when(condition)(copy.start)
            finish.append((copy, condition))

    locals_ = []
    for layer in range(layers):
        copy = pltpu.make_async_copy(
            w_ref.at[layer], spot(layer, z, x, pl.ds(0, cols)), local_sem.at[layer]
        )
        copy.start()
        locals_.append(copy)
        a, b = own(layer, span_a), own(layer, span_b)
        launch(send(b, layer, z, x, span_b, sbx.at[layer], rbx.at[layer], to_x))
        launch(send(a, layer, z, x, span_a, sau.at[layer, 0], rau.at[layer, 0], to_up), has_up)
        launch(send(a, layer, z, x, span_a, sad.at[layer, 0], rad.at[layer, 0], to_down), has_down)
        launch(send(a, layer, z, x, span_a, sax.at[layer, 0], rax.at[layer, 0], to_x))
        launch(send(b, layer, z, x, span_b, sbu.at[layer, 0, 0], rbu.at[layer, 0, 0], to_up), has_up)
        launch(send(b, layer, z, x, span_b, sbd.at[layer, 0, 0], rbd.at[layer, 0, 0], to_down), has_down)

    def arrive(layer, row_z, row_x, span, sem):
        relay(layer, row_z, row_x, span, sem, sem, to_x).wait_recv()

    for layer in range(layers):
        arrive(layer, z, 1 - x, span_b, rbx.at[layer])
        launch(relay(layer, z, 1 - x, span_b, sbu.at[layer, 0, 1], rbu.at[layer, 0, 1], to_up), has_up)
        launch(relay(layer, z, 1 - x, span_b, sbd.at[layer, 0, 1], rbd.at[layer, 0, 1], to_down), has_down)
    for hop in range(line - 1):
        for layer in range(layers):
            from_below = z - 1 - hop
            from_above = z + 1 + hop
            below = from_below >= 0
            above = from_above < line
            row_below = jnp.maximum(from_below, 0)
            row_above = jnp.minimum(from_above, line - 1)

            def pass_on(live, row, rau, sau, rbu, sbu, sem_place, onward, target, hop=hop, layer=layer):
                pl.when(live)(lambda: arrive(layer, row, x, span_a, rau.at[layer, hop]))
                launch(relay(layer, row, x, span_a, sax.at[layer, sem_place], rax.at[layer, sem_place], to_x), live)
                if hop + 1 < line - 1:
                    launch(
                        relay(layer, row, x, span_a, sau.at[layer, hop + 1], rau.at[layer, hop + 1], target),
                        live & onward,
                    )
                for side, row_x in ((0, x), (1, 1 - x)):
                    pl.when(live)(
                        functools.partial(arrive, layer, row, row_x, span_b, rbu.at[layer, hop, side])
                    )
                    if hop + 1 < line - 1:
                        launch(
                            relay(
                                layer, row, row_x, span_b,
                                sbu.at[layer, hop + 1, side], rbu.at[layer, hop + 1, side], target,
                            ),
                            live & onward,
                        )

            pass_on(below, row_below, rau, sau, rbu, sbu, 1 + hop, has_up, to_up)
            pass_on(above, row_above, rad, sad, rbd, sbd, line + hop, has_down, to_down)
    for layer in range(layers):
        arrive(layer, z, 1 - x, span_a, rax.at[layer, 0])
        for hop in range(line - 1):
            from_below = z - 1 - hop
            from_above = z + 1 + hop
            pl.when(from_below >= 0)(
                functools.partial(
                    arrive, layer, jnp.maximum(from_below, 0), 1 - x, span_a, rax.at[layer, 1 + hop]
                )
            )
            pl.when(from_above < line)(
                functools.partial(
                    arrive, layer, jnp.minimum(from_above, line - 1), 1 - x, span_a, rax.at[layer, line + hop]
                )
            )

    @pl.when(section == 0)
    def _():
        pl.semaphore_signal(go_sem, inc=1, device_id={"section": 1}, device_id_type=MESH)

    for copy in locals_:
        copy.wait()
    for copy, condition in finish:
        if condition is None:
            copy.wait_send()
        else:
            pl.when(condition)(copy.wait_send)


def gather_weights(shard):
    layers, shard_rows, cols = shard.shape
    count = lax.axis_size("fsdp")
    line = count // 2
    dma = pltpu.SemaphoreType.DMA
    return pl.pallas_call(
        functools.partial(gather_kernel, line),
        out_shape=jax.ShapeDtypeStruct((layers, shard_rows * count, cols), shard.dtype),
        in_specs=[pl.BlockSpec(memory_space=pl.ANY)],
        out_specs=pl.BlockSpec(memory_space=pl.ANY),
        scratch_shapes=[
            dma((layers,)),
            pltpu.SemaphoreType.REGULAR,
            dma((layers, 2 * line - 1)),
            dma((layers, 2 * line - 1)),
            dma((layers, line - 1)),
            dma((layers, line - 1)),
            dma((layers, line - 1)),
            dma((layers, line - 1)),
            dma((layers,)),
            dma((layers,)),
            dma((layers, line - 1, 2)),
            dma((layers, line - 1, 2)),
            dma((layers, line - 1, 2)),
            dma((layers, line - 1, 2)),
        ],
        compiler_params=pltpu.CompilerParams(collective_id=0, has_side_effects=True),
        name="gather_weights",
    )(shard)


SMALL_COLS = 128


def contract_last(left, right):
    return lax.dot_general(
        left, right, (((1,), (1,)), ((), ())), preferred_element_type=jnp.float32
    )


def contract_rows(left, right):
    return lax.dot_general(
        left, right, (((0,), (0,)), ((), ())), preferred_element_type=jnp.float32
    )


def shifted(value, axis, steps):
    count = lax.axis_size(axis)
    initial, last = (max(0, -steps), min(count, count - steps))
    return lax.ppermute(value, axis, [(source, source + steps) for source in range(initial, last)])


def pack_shard(qkv_w, out_w, up_w, down_w, gains, shifts, inner_part):
    layers, rows = qkv_w.shape[:2]
    columns = jnp.concatenate([gains, shifts, inner_part.reshape(layers, -1, rows)], axis=1)
    columns = jnp.swapaxes(columns, 1, 2)
    columns = jnp.pad(columns, ((0, 0), (0, 0), (0, SMALL_COLS - columns.shape[2])))
    return jnp.concatenate([qkv_w.reshape(layers, rows, -1), out_w, up_w, down_w, columns], axis=2)


def unpack_params(full, head_width, count):
    layers, width, cols = full.shape
    small = jnp.swapaxes(full[:, :, cols - SMALL_COLS : cols - SMALL_COLS + 9], 1, 2).astype(jnp.float32)
    inner = small[:, 6:].reshape(layers, 3, count, width // count)
    inner = jnp.swapaxes(inner, 1, 2).reshape(layers, 1, -1)
    query_bias, value_bias, up_bias = jnp.split(inner, [head_width, 2 * head_width], axis=2)
    qkv_bias = jnp.concatenate([query_bias, jnp.zeros_like(query_bias), value_bias], axis=2)
    return small[:, :6], qkv_bias, up_bias


LANES = 128


def forward_kernel(
    tick, has_alias, head_width, hidden_width, h0_ref, ids_col_ref, ids_row_ref, rows_ref, qkv_bias_ref, up_bias_ref, full_ref, *refs
):
    saved_count = 9
    if has_alias:
        refs = refs[saved_count:]
    outs = refs[:saved_count]
    (
        w_qkv, w_out, w_up, w_down, hid, qkv, lse, mixed, mid, act, slope, final, final_low,
        normed, mask, send, recv, w_sem, save_sem, send_sem, recv_sem,
    ) = refs[saved_count:]
    layers, micro, tokens, width = hid.shape
    section = lax.axis_index("section")
    partner = {"tensor": 1 - lax.axis_index("tensor")}

    @pl.when(section == tick)
    def _():
        ends = (0, 3 * head_width, 4 * head_width, 4 * head_width + hidden_width, 4 * head_width + 2 * hidden_width)

        def fetch(layer, index):
            buffer = (w_qkv, w_out, w_up, w_down)[index]
            return pltpu.make_async_copy(
                full_ref.at[layer, :, pl.ds(ends[index], ends[index + 1] - ends[index])],
                buffer.at[layer],
                w_sem.at[layer, index],
            )

        for layer in range(layers):
            for index in range(4):
                fetch(layer, index).start()
        barrier = pltpu.get_barrier_semaphore()
        pl.semaphore_signal(barrier, inc=1, device_id=partner, device_id_type=MESH)
        pl.semaphore_wait(barrier, 1)

        def save(index, source, layer, part):
            return pltpu.make_async_copy(source.at[layer, part], outs[index].at[layer, part], save_sem.at[index, layer, part])

        saves = ((0, hid), (1, qkv), (2, lse), (3, mixed), (4, mid), (5, act), (6, slope))

        def exchange(layer, stage, part):
            return pltpu.make_async_remote_copy(
                src_ref=send.at[layer, stage, part],
                dst_ref=recv.at[layer, stage, part],
                send_sem=send_sem.at[layer, stage, part],
                recv_sem=recv_sem.at[layer, stage, part],
                device_id=partner,
                device_id_type=MESH,
            )

        for part in range(micro):
            col = ids_col_ref[part]
            row = ids_row_ref[part]
            one = lax.broadcasted_iota(jnp.int32, (tokens, tokens), 0)
            two = lax.broadcasted_iota(jnp.int32, (tokens, tokens), 1)
            allowed = ((col == row) & (col >= 0)) | (one == two)
            mask[part] = jnp.where(allowed, 0.0, -1e30)

        def norm_rows(value, gain, shift):
            average = jnp.mean(value, axis=-1, keepdims=True)
            centred = value - average
            spread = jnp.mean(centred * centred, axis=-1, keepdims=True)
            return centred * lax.rsqrt(spread + EPSILON) * gain + shift

        def joined(layer, stage, part, span):
            return send[layer, stage, part, span].astype(jnp.float32) + recv[layer, stage, part, span].astype(jnp.float32)

        def attention_stage(layer, part):
            @pl.when(layer > 0)
            def _():
                exchange(layer - 1, 1, part).wait_recv()

                @pl.loop(0, tokens, step=32)
                def _(start):
                    span = pl.ds(pl.multiple_of(start, 32), 32)
                    hid[layer, part, span] = mid[layer - 1, part, span] + (
                        joined(layer - 1, 1, part, span) + rows_ref[layer - 1, 5:6]
                    )

            @pl.when(layer == 0)
            def _():
                @pl.loop(0, tokens, step=32)
                def _(start):
                    span = pl.ds(pl.multiple_of(start, 32), 32)
                    hid[layer, part, span] = h0_ref[part, span].astype(jnp.float32)

            @pl.loop(0, tokens, step=32)
            def _(start):
                span = pl.ds(pl.multiple_of(start, 32), 32)
                normed[span] = norm_rows(hid[layer, part, span], rows_ref[layer, 0:1], rows_ref[layer, 2:3]).astype(jnp.bfloat16)

            @pl.when(part == 0)
            def _():
                fetch(layer, 0).wait()

            for piece in range(3):
                @pl.loop(0, head_width, step=256)
                def _(start, piece=piece):
                    span = pl.ds(pl.multiple_of(piece * head_width + start, 256), 256)
                    value = jnp.dot(normed[...], w_qkv[layer, :, span], preferred_element_type=jnp.float32)
                    value = (value + qkv_bias_ref[layer, :, span]).astype(jnp.bfloat16)
                    if piece == 0:
                        value = value * jnp.asarray(1.0 / math.sqrt(HEAD_DIM), jnp.bfloat16)
                    qkv[layer, part, :, span] = value

            lane = lax.broadcasted_iota(jnp.int32, (tokens, LANES), 1)
            tops = []
            for pair in range(head_width // LANES):
                q2 = qkv[layer, part, :, pair * LANES : (pair + 1) * LANES]
                k2 = qkv[layer, part, :, head_width + pair * LANES : head_width + (pair + 1) * LANES]
                v2 = qkv[layer, part, :, 2 * head_width + pair * LANES : 2 * head_width + (pair + 1) * LANES]
                halves = []
                for side in range(2):
                    live = (lane < HEAD_DIM) if side == 0 else (lane >= HEAD_DIM)
                    scores = contract_last(jnp.where(live, q2, jnp.zeros_like(q2)), k2) + mask[part]
                    top = jnp.max(scores, axis=-1, keepdims=True)
                    exponent = jnp.exp(scores - top)
                    total = jnp.sum(exponent, axis=-1, keepdims=True)
                    probs = (exponent / total).astype(jnp.bfloat16)
                    halves.append(jnp.dot(probs, v2, preferred_element_type=jnp.float32))
                    head = 2 * pair + side
                    lse[layer, part, :, head : head + 1] = top + jnp.log(total)
                mixed[layer, part, :, pair * LANES : (pair + 1) * LANES] = jnp.where(
                    lane < HEAD_DIM, halves[0], halves[1]
                ).astype(jnp.bfloat16)

            @pl.when(part == 0)
            def _():
                fetch(layer, 1).wait()

            @pl.loop(0, width, step=256)
            def _(start):
                span = pl.ds(pl.multiple_of(start, 256), 256)
                value = contract_last(mixed[layer, part], w_out[layer, span])
                send[layer, 0, part, :, span] = value.astype(jnp.bfloat16)

            exchange(layer, 0, part).start()
            for index in range(4):
                save(index, saves[index][1], layer, part).start()

        def mlp_stage(layer, part):
            exchange(layer, 0, part).wait_recv()

            @pl.loop(0, tokens, step=32)
            def _(start):
                span = pl.ds(pl.multiple_of(start, 32), 32)
                middle = hid[layer, part, span] + (joined(layer, 0, part, span) + rows_ref[layer, 3:4])
                mid[layer, part, span] = middle
                normed[span] = norm_rows(middle, rows_ref[layer, 1:2], rows_ref[layer, 4:5]).astype(jnp.bfloat16)

            @pl.when(part == 0)
            def _():
                fetch(layer, 2).wait()

            @pl.loop(0, hidden_width, step=256)
            def _(start):
                span = pl.ds(pl.multiple_of(start, 256), 256)
                upward = jnp.dot(normed[...], w_up[layer, :, span], preferred_element_type=jnp.float32)
                upward = upward + up_bias_ref[layer, :, span]
                phi = 0.5 + 0.5 * lax.erf(upward * math.sqrt(0.5))
                density = jnp.exp(-0.5 * upward * upward) * (1.0 / math.sqrt(2.0 * math.pi))
                act[layer, part, :, span] = (upward * phi).astype(jnp.bfloat16)
                slope[layer, part, :, span] = (phi + upward * density).astype(jnp.bfloat16)

            @pl.when(part == 0)
            def _():
                fetch(layer, 3).wait()

            @pl.loop(0, width, step=256)
            def _(start):
                span = pl.ds(pl.multiple_of(start, 256), 256)
                value = contract_last(act[layer, part], w_down[layer, span])
                send[layer, 1, part, :, span] = value.astype(jnp.bfloat16)

            exchange(layer, 1, part).start()
            for index in range(4, 7):
                save(index, saves[index][1], layer, part).start()

        @pl.loop(0, layers)
        def _(layer):
            @pl.loop(0, micro)
            def _(part):
                attention_stage(layer, part)

            @pl.loop(0, micro)
            def _(part):
                mlp_stage(layer, part)

        last = layers - 1

        @pl.loop(0, micro)
        def _(part):
            exchange(last, 1, part).wait_recv()

            @pl.loop(0, tokens, step=32)
            def _(start):
                span = pl.ds(pl.multiple_of(start, 32), 32)
                value = mid[last, part, span] + (joined(last, 1, part, span) + rows_ref[last, 5:6])
                final[part, span] = value
                final_low[part, span] = value.astype(jnp.bfloat16)

        ending = [
            pltpu.make_async_copy(final, outs[7], save_sem.at[7, 0, 0]),
            pltpu.make_async_copy(final_low, outs[8], save_sem.at[8, 0, 0]),
        ]
        for copy in ending:
            copy.start()

        @pl.loop(0, layers)
        def _(layer):
            @pl.loop(0, micro)
            def _(part):
                for stage in range(2):
                    exchange(layer, stage, part).wait_send()
                for index, source in saves:
                    save(index, source, layer, part).wait()

        for copy in ending:
            copy.wait()


def saved_shapes(layers, micro, tokens, width, head_width, hidden_width):
    low, full = jnp.bfloat16, jnp.float32
    heads = head_width // HEAD_DIM
    return (
        ((layers, micro, tokens, width), full),
        ((layers, micro, tokens, 3 * head_width), low),
        ((layers, micro, tokens, heads), full),
        ((layers, micro, tokens, head_width), low),
        ((layers, micro, tokens, width), full),
        ((layers, micro, tokens, hidden_width), low),
        ((layers, micro, tokens, hidden_width), low),
        ((micro, tokens, width), full),
        ((micro, tokens, width), low),
    )


def forward(tick, h0, ids, params, full, previous, head_width, hidden_width):
    rows, qkv_bias, up_bias = params
    layers, width = full.shape[:2]
    micro, tokens = ids.shape
    shapes = saved_shapes(layers, micro, tokens, width, head_width, hidden_width)
    vmem = pl.BlockSpec(memory_space=pltpu.VMEM)
    hbm = pl.BlockSpec(memory_space=pl.ANY)
    dma = pltpu.SemaphoreType.DMA
    low = jnp.bfloat16
    aliased = () if previous is None else tuple(previous)
    return pl.pallas_call(
        functools.partial(forward_kernel, tick, previous is not None, head_width, hidden_width),
        out_shape=[jax.ShapeDtypeStruct(shape, kind) for shape, kind in shapes],
        in_specs=[vmem] * 6 + [hbm] * (1 + len(aliased)),
        out_specs=[hbm] * len(shapes),
        input_output_aliases={7 + number: number for number in range(len(aliased))},
        scratch_shapes=[
            pltpu.VMEM((layers, width, 3 * head_width), low),
            pltpu.VMEM((layers, width, head_width), low),
            pltpu.VMEM((layers, width, hidden_width), low),
            pltpu.VMEM((layers, width, hidden_width), low),
            *(pltpu.VMEM(shape, kind) for shape, kind in shapes),
            pltpu.VMEM((tokens, width), low),
            pltpu.VMEM((micro, tokens, tokens), jnp.float32),
            pltpu.VMEM((layers, 2, micro, tokens, width), low),
            pltpu.VMEM((layers, 2, micro, tokens, width), low),
            dma((layers, 4)),
            dma((len(shapes), layers, micro)),
            dma((layers, 2, micro)),
            dma((layers, 2, micro)),
        ],
        compiler_params=pltpu.CompilerParams(
            collective_id=2 + tick, has_side_effects=True, vmem_limit_bytes=62 << 20
        ),
        name="forward",
    )(h0, ids[:, :, None], ids[:, None, :], rows, qkv_bias, up_bias, full, *aliased)


SLOTS = 2


def backward_kernel(
    line, aligned, head_width, hidden_width, g0_ref, ids_col_ref, ids_row_ref, rows_ref, full_ref, *refs
):
    saves = refs[:7]
    (
        out, small_out, inner_out, g_out, d_out, own_in, x_in, z_in,
        w_qkv, w_out, w_up, w_down, hid, qkv, lse, mixed, mid, act, slope, grad, low, hidden_grad, qkv_grad, normed,
        mixed_grad, mask, send, recv, stage, small, inner_sum, given, run_own, run_x, run_z, run_out, small_in, inner_in,
        w_sem, load_sem, send_sem, recv_sem, stage_sem, end_sem, given_sem, own_send, own_recv, x_send, x_recv, z_send, z_recv, run_sem,
        out_sem, small_send, small_recv, inner_send, inner_recv,
    ) = refs[7:]
    held = (hid, qkv, lse, mixed, mid, act, slope)
    layers, micro, tokens, width = hid.shape
    section = lax.axis_index("section")
    partner = {"tensor": 1 - lax.axis_index("tensor")}
    other = {"section": 1 - section}
    place = lax.axis_index("fsdp")
    count = 2 * line
    z = place // 2
    x = lax.rem(place, 2)
    to_x = {"fsdp": z * 2 + 1 - x}
    to_up = {"fsdp": jnp.minimum(z + 1, line - 1) * 2 + x}
    to_down = {"fsdp": jnp.maximum(z - 1, 0) * 2 + x}
    tile = 256
    tiles = width // tile
    shard_rows = width // count
    group_cols = stage.shape[2]
    steps = 3 * line
    groups = 3
    scale = 1.0 / math.sqrt(HEAD_DIM)

    if True:
        ends = (0, 3 * head_width, 4 * head_width, 4 * head_width + hidden_width, 4 * head_width + 2 * hidden_width)

        def fetch(layer, index):
            buffer = (w_qkv, w_out, w_up, w_down)[index]
            return pltpu.make_async_copy(
                full_ref.at[layer, :, pl.ds(ends[index], ends[index + 1] - ends[index])], buffer, w_sem.at[index]
            )

        def load(index, layer):
            return pltpu.make_async_copy(saves[index].at[layer], held[index].at[layer], load_sem.at[index, layer])

        last = layers - 1
        fetch(last, 3).start()
        load(6, last).start()
        fetch(last, 2).start()
        for index in (5, 4):
            load(index, last).start()
        fetch(last, 1).start()
        for index in (1, 2, 3, 0):
            load(index, last).start()
        fetch(last, 0).start()
        for layer in range(last - 1, -1, -1):
            for index in range(7):
                load(index, layer).start()
        barrier = pltpu.get_barrier_semaphore()
        pl.semaphore_signal(barrier, inc=1, device_id=partner, device_id_type=MESH)
        pl.semaphore_signal(barrier, inc=1, device_id=other, device_id_type=MESH)
        for turn in range(1, count):
            peer = {"fsdp": lax.rem(place + turn, count)}
            pl.semaphore_signal(barrier, inc=1, device_id=peer, device_id_type=MESH)
        pl.semaphore_signal(
            barrier, inc=1, device_id={"section": 1 - section, "fsdp": z * 2 + 1 - x}, device_id_type=MESH
        )
        pl.semaphore_wait(barrier, count + 2)

        hand_over = pltpu.make_async_remote_copy(
            src_ref=low, dst_ref=given, send_sem=given_sem.at[0], recv_sem=given_sem.at[1],
            device_id=other, device_id_type=MESH,
        )

        small[...] = jnp.zeros_like(small)
        inner_sum[...] = jnp.zeros_like(inner_sum)
        for part in range(micro):
            col = ids_col_ref[part]
            row = ids_row_ref[part]
            one = lax.broadcasted_iota(jnp.int32, (tokens, tokens), 0)
            two = lax.broadcasted_iota(jnp.int32, (tokens, tokens), 1)
            allowed = ((col == row) & (col >= 0)) | (one == two)
            mask[part] = jnp.where(allowed, 0.0, -1e30)

        @pl.when(section == 1)
        def _():
            for part in range(micro):
                grad[part] = g0_ref[part].astype(jnp.float32)


        def exchange(step, part):
            return pltpu.make_async_remote_copy(
                src_ref=send.at[step, part],
                dst_ref=recv.at[step, part],
                send_sem=send_sem.at[step, part],
                recv_sem=recv_sem.at[step, part],
                device_id=partner,
                device_id_type=MESH,
            )

        def rows_of(part):
            return pl.ds(pl.multiple_of(part * tokens, tokens), tokens)

        def column_sum(value):
            return jnp.sum(value.astype(jnp.float32), axis=0, keepdims=True)

        def norm_parts(value):
            average = jnp.mean(value, axis=-1, keepdims=True)
            centred = value - average
            spread = jnp.mean(centred * centred, axis=-1, keepdims=True)
            inverse = lax.rsqrt(spread + EPSILON)
            return centred * inverse, inverse

        def norm_back(layer, step, part, source, gain_row, shift_row):
            gain = rows_ref[layer, gain_row : gain_row + 1]

            @pl.loop(0, tokens, step=32)
            def _(start):
                span = pl.ds(pl.multiple_of(start, 32), 32)
                outer = send[step, part, span].astype(jnp.float32) + recv[step, part, span].astype(jnp.float32)
                unit, inverse = norm_parts(source[layer, part, span])
                inner = outer * gain
                first = jnp.mean(inner, axis=-1, keepdims=True)
                second = jnp.mean(inner * unit, axis=-1, keepdims=True)
                small[layer, gain_row : gain_row + 1] += column_sum(outer * unit)
                small[layer, shift_row : shift_row + 1] += column_sum(outer)
                grad[part, span] = grad[part, span] + inverse * (inner - first - unit * second)

        def renorm(layer, part, source, gain_row, shift_row):
            @pl.loop(0, tokens, step=32)
            def _(start):
                span = pl.ds(pl.multiple_of(start, 32), 32)
                unit, _ = norm_parts(source[layer, part, span])
                value = unit * rows_ref[layer, gain_row : gain_row + 1] + rows_ref[layer, shift_row : shift_row + 1]
                normed[pl.ds(pl.multiple_of(part * tokens + start, 32), 32)] = value.astype(jnp.bfloat16)

        def round_grad(layer, part, bias_row):
            @pl.loop(0, tokens, step=32)
            def _(start):
                span = pl.ds(pl.multiple_of(start, 32), 32)
                value = grad[part, span].astype(jnp.bfloat16)
                low[pl.ds(pl.multiple_of(part * tokens + start, 32), 32)] = value
                small[layer, bias_row : bias_row + 1] += column_sum(value)

        def columns(group):
            return pl.ds(pl.multiple_of((2 - group) * group_cols, group_cols), group_cols)

        def part_rows(row_z, row_x):
            return pl.ds(pl.multiple_of((row_z * 2 + row_x) * shard_rows, shard_rows), shard_rows)

        def put(layer, turn, number, group):
            return pltpu.make_async_copy(
                stage.at[turn],
                d_out.at[layer, pl.ds(pl.multiple_of(number * tile, tile), tile), columns(group)],
                stage_sem.at[turn],
            )

        def route(step):
            below, above = z, line - 1 - z
            gap = jnp.maximum(below, above) - jnp.minimum(below, above)
            rest = jnp.maximum(step - gap, 0)
            far = step < gap
            upward = jnp.where(far, jnp.where(above > below, 1, 0), 1 - lax.rem(rest, 2))
            reach = jnp.where(far, jnp.maximum(below, above) - step, jnp.minimum(below, above) - rest // 2)
            ends_here = step == line - 1
            target = jnp.where(ends_here, z, jnp.where(upward == 1, z + reach, z - reach))
            return target, upward == 1, ends_here

        def to_partner(turn, group, row_z):
            runner = jnp.where(turn == 0, 1 - section, section)
            return pltpu.make_async_remote_copy(
                src_ref=d_out.at[last - turn, part_rows(row_z, 1 - x), columns(group)],
                dst_ref=x_in.at[turn, group, row_z],
                send_sem=x_send.at[turn, group, row_z],
                recv_sem=x_recv.at[turn, group, row_z],
                device_id={"section": runner, "fsdp": z * 2 + 1 - x},
                device_id_type=MESH,
            )

        def to_other(group, row_z):
            return pltpu.make_async_remote_copy(
                src_ref=d_out.at[last, part_rows(row_z, x), columns(group)],
                dst_ref=own_in.at[group, row_z],
                send_sem=own_send.at[group, row_z],
                recv_sem=own_recv.at[group, row_z],
                device_id=other,
                device_id_type=MESH,
            )

        def onward(turn, group, row_z, slot, side):
            return pltpu.make_async_remote_copy(
                src_ref=run_own.at[slot],
                dst_ref=z_in.at[turn, group, side, row_z],
                send_sem=z_send.at[slot],
                recv_sem=z_recv.at[turn, group, side, row_z],
                device_id=(to_up, to_down)[side],
                device_id_type=MESH,
            )

        def publish(group):
            return pltpu.make_async_copy(run_out, out.at[0, :, columns(group)], out_sem.at[0])

        def publish_other(group):
            return pltpu.make_async_remote_copy(
                src_ref=run_out, dst_ref=out.at[last, :, columns(group)],
                send_sem=out_sem.at[1], recv_sem=out_sem.at[2 + group],
                device_id=other, device_id_type=MESH,
            )

        def add_rows(slot, source):
            @pl.loop(0, shard_rows, step=16)
            def _(start):
                span = pl.ds(pl.multiple_of(start, 16), 16)
                run_own[slot, span] = run_own[slot, span] + source[span]

        def run_sums(turn):
            @pl.loop(0, steps)
            def _(number):
                group = number // line
                step = lax.rem(number, line)
                slot = lax.rem(number, SLOTS)
                target, upward, ends_here = route(step)

                @pl.when((number >= SLOTS) & (lax.rem(number + line - SLOTS, line) != line - 1))
                def _():
                    onward(turn, 0, 0, slot, 0).wait_send()

                if turn == 0:
                    to_other(group, target).wait_recv()
                    source = own_in.at[group, target]
                else:
                    source = d_out.at[last - turn, part_rows(target, x), columns(group)]
                own = pltpu.make_async_copy(source, run_own.at[slot], run_sem.at[0])
                own.start()
                to_partner(turn, group, target).wait_recv()
                mate = pltpu.make_async_copy(x_in.at[turn, group, target], run_x, run_sem.at[1])
                mate.start()
                feeds = (
                    jnp.logical_or(upward, ends_here) & (z > 0),
                    jnp.logical_or(jnp.logical_not(upward), ends_here) & (z < line - 1),
                )
                moves = []
                for side in range(2):
                    move = pltpu.make_async_copy(z_in.at[turn, group, side, target], run_z.at[side], run_sem.at[2 + side])
                    moves.append(move)

                    @pl.when(feeds[side])
                    def _(side=side, move=move):
                        onward(turn, group, target, slot, side).wait_recv()
                        move.start()

                own.wait()
                mate.wait()
                add_rows(slot, run_x)
                for side in range(2):

                    @pl.when(feeds[side])
                    def _(side=side):
                        moves[side].wait()
                        add_rows(slot, run_z.at[side])

                @pl.when(jnp.logical_not(ends_here) & upward)
                def _():
                    onward(turn, group, target, slot, 0).start()

                @pl.when(jnp.logical_not(ends_here) & jnp.logical_not(upward))
                def _():
                    onward(turn, group, target, slot, 1).start()

                @pl.when(ends_here)
                def _():
                    @pl.when(group > 0)
                    def _():
                        publish(group).wait() if turn else publish_other(group).wait_send()

                    @pl.loop(0, shard_rows, step=16)
                    def _(start):
                        span = pl.ds(pl.multiple_of(start, 16), 16)
                        run_out[span] = run_own[slot, span].astype(jnp.float32)

                    publish(group).start() if turn else publish_other(group).start()

            for number in range(steps - SLOTS, steps):
                if number % line != line - 1:
                    onward(turn, 0, 0, number % SLOTS, 0).wait_send()
            publish(0).wait() if turn else publish_other(0).wait_send()

        @pl.when(section == 0)
        def _():
            run_sums(0)
            hand_over.wait_recv()
            for part in range(micro):
                grad[part] = given[pl.ds(part * tokens, tokens)].astype(jnp.float32)

        def mlp_stage(layer, part):
            round_grad(layer, part, 5)

            @pl.when(part == 0)
            def _():
                fetch(layer, 3).wait()
                load(6, layer).wait()

            @pl.loop(0, hidden_width, step=tile)
            def _(start):
                span = pl.ds(pl.multiple_of(start, tile), tile)
                value = jnp.dot(low[rows_of(part)], w_down[:, span], preferred_element_type=jnp.float32)
                value = (value * slope[layer, part, :, span].astype(jnp.float32)).astype(jnp.bfloat16)
                hidden_grad[rows_of(part), span] = value
                place_in = pl.ds(pl.multiple_of(2 * head_width + start, tile), tile)
                inner_sum[layer, :, place_in] += column_sum(value)

            @pl.when(part == 0)
            def _():
                fetch(layer, 2).wait()

            @pl.when(layer < last)
            def _():
                exchange(0, part).wait_send()

            @pl.loop(0, width, step=tile)
            def _(start):
                span = pl.ds(pl.multiple_of(start, tile), tile)
                value = contract_last(hidden_grad[rows_of(part)], w_up[span])
                send[0, part, :, span] = value.astype(jnp.bfloat16)

            exchange(0, part).start()

        def weight_tiles(layer, turn, group, fill):
            def row_of(number):
                return route(number)[0] if tiles == line else number

            def finish(number):
                row = row_of(number)
                put(layer, number, row, group).wait()
                for extra in range(line // tiles):
                    row_z = row * (line // tiles) + extra
                    to_partner(turn, group, row_z).start()
                    pl.when(turn == 0)(to_other(group, row_z).start)

            @pl.loop(0, tiles)
            def _(number):
                row = row_of(number)
                fill(number, pl.ds(pl.multiple_of(row * tile, tile), tile))
                put(layer, number, row, group).start()
                pl.when(number > 0)(lambda: finish(jnp.maximum(number - 1, 0)))

            finish(tiles - 1)

        def attention_stage(layer, part):
            exchange(0, part).wait_recv()
            norm_back(layer, 0, part, mid, 1, 4)
            round_grad(layer, part, 3)

            @pl.when(part == 0)
            def _():
                fetch(layer, 1).wait()
                load(1, layer).wait()
                load(2, layer).wait()

            @pl.loop(0, head_width, step=tile)
            def _(start):
                span = pl.ds(pl.multiple_of(start, tile), tile)
                value = jnp.dot(low[rows_of(part)], w_out[:, span], preferred_element_type=jnp.float32)
                mixed_grad[:, span] = value.astype(jnp.bfloat16)

            lane = lax.broadcasted_iota(jnp.int32, (tokens, LANES), 1)
            for pair in range(head_width // LANES):
                spans = [pl.ds(piece * head_width + pair * LANES, LANES) for piece in range(3)]
                q2, k2, v2 = (qkv[layer, part, :, span] for span in spans)
                go2 = mixed_grad[:, pair * LANES : (pair + 1) * LANES]
                halves = []
                for side in range(2):
                    live = (lane < HEAD_DIM) if side == 0 else (lane >= HEAD_DIM)
                    head = 2 * pair + side
                    scores = contract_last(jnp.where(live, q2, jnp.zeros_like(q2)), k2) + mask[part]
                    probs = jnp.exp(scores - lse[layer, part, :, head : head + 1])
                    outer = contract_last(jnp.where(live, go2, jnp.zeros_like(go2)), v2)
                    centre = jnp.sum(probs * outer, axis=-1, keepdims=True)
                    inner = (probs * (outer - centre)).astype(jnp.bfloat16)
                    halves.append((
                        jnp.dot(inner, k2, preferred_element_type=jnp.float32) * scale,
                        contract_rows(inner, q2),
                        contract_rows(probs.astype(jnp.bfloat16), go2),
                    ))
                for piece in range(3):
                    value = jnp.where(lane < HEAD_DIM, halves[0][piece], halves[1][piece]).astype(jnp.bfloat16)
                    qkv_grad[rows_of(part), spans[piece]] = value
                    if piece != 1:
                        place_in = pl.ds((piece // 2) * head_width + pair * LANES, LANES)
                        inner_sum[layer, :, place_in] += column_sum(value)

            @pl.when(part == 0)
            def _():
                fetch(layer, 0).wait()

            @pl.when(layer < last)
            def _():
                exchange(1, part).wait_send()

            @pl.loop(0, width, step=tile)
            def _(start):
                span = pl.ds(pl.multiple_of(start, tile), tile)
                value = contract_last(qkv_grad[rows_of(part)], w_qkv[span])
                send[1, part, :, span] = value.astype(jnp.bfloat16)

            exchange(1, part).start()

        @pl.loop(0, layers)
        def _(turn):
            layer = last - turn

            @pl.loop(0, micro)
            def _(part):
                mlp_stage(layer, part)

            @pl.when(layer > 0)
            def _():
                fetch(layer - 1, 3).start()
                fetch(layer - 1, 2).start()

            load(5, layer).wait()

            def fill_down(number, span):
                both = act[layer].reshape(micro * tokens, hidden_width)
                stage[number] = contract_rows(low[:, span], both).astype(jnp.bfloat16)

            weight_tiles(layer, turn, 0, fill_down)
            load(4, layer).wait()

            @pl.loop(0, micro)
            def _(part):
                renorm(layer, part, mid, 1, 4)

            def fill_up(number, span):
                stage[number] = contract_rows(normed[:, span], hidden_grad[...]).astype(jnp.bfloat16)

            weight_tiles(layer, turn, 1, fill_up)

            @pl.loop(0, micro)
            def _(part):
                attention_stage(layer, part)

            @pl.when(layer > 0)
            def _():
                fetch(layer - 1, 1).start()
                fetch(layer - 1, 0).start()

            load(3, layer).wait()
            load(0, layer).wait()

            @pl.loop(0, micro)
            def _(part):
                renorm(layer, part, hid, 0, 2)

            def fill_attention(number, span):
                both = mixed[layer].reshape(micro * tokens, head_width)
                stage[number, :, : 3 * head_width] = contract_rows(normed[:, span], qkv_grad[...]).astype(jnp.bfloat16)
                stage[number, :, 3 * head_width :] = contract_rows(low[:, span], both).astype(jnp.bfloat16)

            weight_tiles(layer, turn, 2, fill_attention)

            @pl.loop(0, micro)
            def _(part):
                exchange(1, part).wait_recv()
                norm_back(layer, 1, part, hid, 0, 2)

        for part in range(micro):
            low[pl.ds(part * tokens, tokens)] = grad[part].astype(jnp.bfloat16)
        pl.when(section == 1)(hand_over.start)
        ending = pltpu.make_async_copy(grad, g_out, end_sem.at[0])
        ending.start()

        def small_copies(peer, turn):
            if aligned:
                cut, inner_cut = pl.ds(pl.multiple_of(peer * shard_rows, shard_rows), shard_rows), pl.ds(
                    pl.multiple_of(peer * 3 * shard_rows, 3 * shard_rows), 3 * shard_rows
                )
            else:
                cut, inner_cut = pl.ds(0, width), pl.ds(0, 3 * width)
            made = []
            for source, target, sends, receives in (
                (small.at[:, :, cut], small_in, small_send, small_recv),
                (inner_sum.at[:, :, inner_cut], inner_in, inner_send, inner_recv),
            ):
                made.append(pltpu.make_async_remote_copy(
                    src_ref=source, dst_ref=target.at[turn], send_sem=sends.at[turn], recv_sem=receives.at[turn],
                    device_id={"fsdp": peer}, device_id_type=MESH,
                ))
            return made

        for turn in range(1, count):
            for copy in small_copies(lax.rem(place + turn, count), turn):
                copy.start()

        run_sums(1)
        pl.when(section == 1)(lambda: run_sums(0))

        if aligned:
            mine = pl.ds(pl.multiple_of(place * shard_rows, shard_rows), shard_rows)
            inner_mine = pl.ds(pl.multiple_of(place * 3 * shard_rows, 3 * shard_rows), 3 * shard_rows)
        else:
            mine, inner_mine = pl.ds(0, width), pl.ds(0, 3 * width)
        small_out[...] = small[:, :, mine]
        inner_out[...] = inner_sum[:, :, inner_mine]
        for turn in range(1, count):
            for copy in small_copies(lax.rem(place + turn, count), turn):
                copy.wait()
            small_out[...] += small_in[turn]
            inner_out[...] += inner_in[turn]

        for step in range(2):
            for part in range(micro):
                exchange(step, part).wait_send()

        @pl.loop(0, groups)
        def _(group):
            @pl.loop(0, line)
            def _(row_z):
                to_partner(0, group, row_z).wait_send()
                to_partner(1, group, row_z).wait_send()
                to_other(group, row_z).wait_send()

        for group in range(groups):
            publish_other(group).wait_recv()
        pl.when(section == 1)(hand_over.wait_send)
        ending.wait()


def backward(g0, ids, params, full, saves, head_width, hidden_width):
    rows, qkv_bias, up_bias = params
    layers, width, cols = full.shape
    micro, tokens = ids.shape
    count = lax.axis_size("fsdp")
    line = count // 2
    shard_rows = width // count
    aligned = shard_rows % LANES == 0
    group_cols = 4 * head_width
    small_width = shard_rows if aligned else width
    shapes = saved_shapes(layers, micro, tokens, width, head_width, hidden_width)
    vmem = pl.BlockSpec(memory_space=pltpu.VMEM)
    hbm = pl.BlockSpec(memory_space=pl.ANY)
    dma = pltpu.SemaphoreType.DMA
    low, wide = jnp.bfloat16, jnp.float32
    outs = (
        ((layers, shard_rows, 3 * group_cols), wide),
        ((layers, 8, small_width), wide),
        ((layers, 1, 3 * small_width), wide),
        ((micro, tokens, width), wide),
        ((layers, width, 3 * group_cols), low),
        ((3, line, shard_rows, group_cols), low),
        ((2, 3, line, shard_rows, group_cols), low),
        ((2, 3, 2, line, shard_rows, group_cols), low),
    )
    return pl.pallas_call(
        functools.partial(backward_kernel, line, aligned, head_width, hidden_width),
        out_shape=[jax.ShapeDtypeStruct(shape, kind) for shape, kind in outs],
        in_specs=[vmem] * 4 + [hbm] * 8,
        out_specs=[hbm, vmem, vmem] + [hbm] * 5,
        scratch_shapes=[
            pltpu.VMEM((width, 3 * head_width), low),
            pltpu.VMEM((width, head_width), low),
            pltpu.VMEM((width, hidden_width), low),
            pltpu.VMEM((width, hidden_width), low),
            *(pltpu.VMEM(shape, kind) for shape, kind in shapes[:7]),
            pltpu.VMEM((micro, tokens, width), wide),
            pltpu.VMEM((micro * tokens, width), low),
            pltpu.VMEM((micro * tokens, hidden_width), low),
            pltpu.VMEM((micro * tokens, 3 * head_width), low),
            pltpu.VMEM((micro * tokens, width), low),
            pltpu.VMEM((tokens, head_width), low),
            pltpu.VMEM((micro, tokens, tokens), wide),
            pltpu.VMEM((2, micro, tokens, width), low),
            pltpu.VMEM((2, micro, tokens, width), low),
            pltpu.VMEM((width // 256, 256, group_cols), low),
            pltpu.VMEM((layers, 8, width), wide),
            pltpu.VMEM((layers, 1, 3 * width), wide),
            pltpu.VMEM((micro * tokens, width), low),
            pltpu.VMEM((SLOTS, shard_rows, group_cols), low),
            pltpu.VMEM((shard_rows, group_cols), low),
            pltpu.VMEM((2, shard_rows, group_cols), low),
            pltpu.VMEM((shard_rows, group_cols), wide),
            pltpu.VMEM((count, layers, 8, small_width), wide),
            pltpu.VMEM((count, layers, 1, 3 * small_width), wide),
            dma((4,)),
            dma((7, layers)),
            dma((2, micro)),
            dma((2, micro)),
            dma((width // 256,)),
            dma((1,)),
            dma((2,)),
            dma((3, line)),
            dma((3, line)),
            dma((2, 3, line)),
            dma((2, 3, line)),
            dma((SLOTS,)),
            dma((2, 3, 2, line)),
            dma((4,)),
            dma((5,)),
            dma((count,)),
            dma((count,)),
            dma((count,)),
            dma((count,)),
        ],
        compiler_params=pltpu.CompilerParams(
            collective_id=4, has_side_effects=True, vmem_limit_bytes=63 << 20
        ),
        name="backward",
    )(g0, ids[:, :, None], ids[:, None, :], rows, full, *saves)


def unpack_grads(full, head_width, hidden_width):
    layers, rows, cols = full.shape
    ends = [3 * head_width, 4 * head_width, 4 * head_width + hidden_width, 4 * head_width + 2 * hidden_width]
    return (
        full[:, :, : ends[0]].reshape(layers, rows, 3, head_width),
        full[:, :, ends[0] : ends[1]],
        full[:, :, ends[1] : ends[2]],
        full[:, :, ends[2] : ends[3]],
    )


def body(
    block_input,
    image_ids,
    qkv_weight,
    out_weight,
    up_weight,
    down_weight,
    norm_gains,
    biases,
    inner_bias,
    cotangent,
):
    section = lax.axis_index("section")
    count = lax.axis_size("fsdp")
    head_width, hidden_width = out_weight.shape[2], up_weight.shape[2]
    shard = pack_shard(qkv_weight, out_weight, up_weight, down_weight, norm_gains, biases, inner_bias)
    full = gather_weights(shard)
    params = unpack_params(full, head_width, count)
    saved = forward(0, block_input, image_ids, params, full, None, head_width, hidden_width)
    received = shifted(saved[8], "section", 1)
    saved = forward(1, received, image_ids, params, full, saved, head_width, hidden_width)
    summed, small, inner, input_grad = backward(
        cotangent, image_ids, params, full, saved[:7], head_width, hidden_width
    )[:4]
    rows = qkv_weight.shape[1]
    if small.shape[2] != rows:
        place = lax.axis_index("fsdp")
        small = lax.dynamic_slice_in_dim(small, place * rows, rows, 2)
        inner = lax.dynamic_slice_in_dim(inner, place * 3 * rows, 3 * rows, 2)
    section_ends = jnp.where(section == 0, input_grad, saved[7])[None]
    return (
        section_ends,
        *unpack_grads(summed, head_width, hidden_width),
        small[:, :2],
        small[:, 2:6],
        inner,
    )


def solution(mesh):
    placed = (
        P(None, "fsdp", None),
        P(None, "fsdp"),
        P("section", "fsdp", None, "tensor"),
        P("section", "fsdp", "tensor"),
        P("section", "fsdp", "tensor"),
        P("section", "fsdp", "tensor"),
        P("section", None, "fsdp"),
        P("section", None, "fsdp"),
        P("section", "tensor", "fsdp"),
        P(None, "fsdp", None),
    )
    return jax.shard_map(
        body,
        mesh=mesh,
        in_specs=placed,
        out_specs=(
            P("section", None, "fsdp", None),
            P("section", "fsdp", None, "tensor"),
            P("section", "fsdp", "tensor"),
            P("section", "fsdp", "tensor"),
            P("section", "fsdp", "tensor"),
            P("section", None, "fsdp"),
            P("section", None, "fsdp"),
            P("section", "tensor", "fsdp"),
        ),
        check_vma=False,
    )
```

```python
import functools
import math

import jax
import jax.numpy as jnp
from jax import lax
from jax.experimental import pallas as pl
from jax.experimental.pallas import tpu as pltpu
from jax.sharding import PartitionSpec as P

HEAD_DIM = 64
EPSILON = 1e-06


MESH = pl.DeviceIdType.MESH


def contract_last(left, right):
    return lax.dot_general(
        left, right, (((1,), (1,)), ((), ())), preferred_element_type=jnp.float32
    )


def contract_rows(left, right):
    return lax.dot_general(
        left, right, (((0,), (0,)), ((), ())), preferred_element_type=jnp.float32
    )


LANES = 128
X_FIRST_COLS = 1024


def allowed_bias(ids_row, tokens):
    spread = jnp.broadcast_to(ids_row, (tokens, tokens))
    mirror = jnp.transpose(spread)
    one = lax.broadcasted_iota(jnp.int32, (tokens, tokens), 0)
    two = lax.broadcasted_iota(jnp.int32, (tokens, tokens), 1)
    allowed = ((mirror == spread) & (spread >= 0)) | (one == two)
    return jnp.where(allowed, 0.0, -1e30)


def forward_kernel(line, aligned, h0_ref, ids_ref, small_ref, inner_ref, qkv_in, out_in, up_in, down_in, *refs):
    outs = refs[:8]
    (
        full_ref, guest_full, guest_shard, rows_out,
        w_qkv, w_out, w_up, w_down, hid, qkv, lse, mixed, mid, act, slope, final,
        rows_ref, inner_all, final_low, given, normed, mask, send, recv,
        w_sem, save_sem, send_sem, recv_sem, local_sem, go_sem, guest_sem, push_sem, push_recv, given_sem, small_sem, inner_sem,
        sax, rax, sau, rau, sad, rad, sbx, rbx, sbu, rbu, sbd, rbd,
    ) = refs[8:]
    layers, micro, tokens, width = hid.shape
    head_width, hidden_width = out_in.shape[2], up_in.shape[2]
    section = lax.axis_index("section")
    place = lax.axis_index("fsdp")
    count = 2 * line
    shard_rows = width // count
    z = place // 2
    x = lax.rem(place, 2)
    partner = {"tensor": 1 - lax.axis_index("tensor")}
    other = {"section": 1 - section}
    to_x = {"fsdp": z * 2 + 1 - x}
    to_x_other = {"section": 1 - section, "fsdp": z * 2 + 1 - x}
    has_up = z < line - 1
    has_down = z > 0
    to_up = {"fsdp": jnp.minimum(z + 1, line - 1) * 2 + x}
    to_down = {"fsdp": jnp.maximum(z - 1, 0) * 2 + x}
    ends = (0, 3 * head_width, 4 * head_width, 4 * head_width + hidden_width, 4 * head_width + 2 * hidden_width)
    cols = ends[4]
    cols_a = cols - X_FIRST_COLS
    span_a = pl.ds(0, cols_a)
    span_b = pl.ds(cols_a, X_FIRST_COLS)
    last = layers - 1

    barrier = pltpu.get_barrier_semaphore()
    for peer in (partner, other, to_x_other):
        pl.semaphore_signal(barrier, inc=1, device_id=peer, device_id_type=MESH)
    for turn in range(1, count):
        peer = {"fsdp": lax.rem(place + turn, count)}
        pl.semaphore_signal(barrier, inc=1, device_id=peer, device_id_type=MESH)
    pl.semaphore_wait(barrier, count + 2)

    small_copies = []
    if aligned:
        mine = pl.ds(pl.multiple_of(place * shard_rows, shard_rows), shard_rows)
        inner_mine = pl.ds(pl.multiple_of(place * 3 * shard_rows, 3 * shard_rows), 3 * shard_rows)
        rows_ref[:, :, mine] = small_ref[...]
        inner_all[:, :, inner_mine] = inner_ref[...]
        for turn in range(1, count):
            peer = {"fsdp": lax.rem(place + turn, count)}
            for source, target, sems in (
                (small_ref, rows_ref.at[:, :, mine], small_sem), (inner_ref, inner_all.at[:, :, inner_mine], inner_sem),
            ):
                copy = pltpu.make_async_remote_copy(
                    src_ref=source, dst_ref=target, send_sem=sems.at[0, turn], recv_sem=sems.at[1, turn],
                    device_id=peer, device_id_type=MESH,
                )
                copy.start()
                small_copies.append(copy)
    else:
        rows_ref[...] = small_ref[...]
        inner_all[...] = inner_ref[...]

    def spot(layer, row_z, row_x, span):
        start = pl.multiple_of((row_z * 2 + row_x) * shard_rows, shard_rows)
        target = guest_full if layer is None else full_ref.at[layer]
        return target.at[pl.ds(start, shard_rows), span]

    def pieces(layer, span):
        if layer is None:
            return [(guest_shard.at[:, span], span)]
        if span is span_b:
            return [(down_in.at[layer, :, pl.ds(hidden_width - X_FIRST_COLS, X_FIRST_COLS)], span)]
        return [
            (qkv_in.at[layer], pl.ds(ends[0], 3 * head_width)),
            (out_in.at[layer], pl.ds(ends[1], head_width)),
            (up_in.at[layer], pl.ds(ends[2], hidden_width)),
            (down_in.at[layer, :, pl.ds(0, hidden_width - X_FIRST_COLS)], pl.ds(ends[3], hidden_width - X_FIRST_COLS)),
        ]

    def remote(source, target, send_sem, recv_sem, device):
        return pltpu.make_async_remote_copy(
            src_ref=source, dst_ref=target, send_sem=send_sem, recv_sem=recv_sem, device_id=device, device_id_type=MESH,
        )

    def always(condition, action):
        if condition is None:
            action()
        else:
            pl.when(condition)(action)

    def gather(served):
        finish = []

        def launch(layer, row_z, row_x, span, send_sem, recv_sem, device, condition=None, fresh=False):
            whole = spot(layer, row_z, row_x, span)
            if layer is None and device is to_x and span is span_a:
                device = to_x_other

                def landing(part):
                    start = pl.multiple_of((row_z * 2 + row_x) * shard_rows, shard_rows)
                    return full_ref.at[last, pl.ds(start, shard_rows), part]
            else:

                def landing(part):
                    return spot(layer, row_z, row_x, part)

            def begin():
                for source, part in pieces(layer, span) if fresh else [(whole, span)]:
                    remote(source, landing(part), send_sem, recv_sem, device).start()

            always(condition, begin)
            finish.append((remote(whole, whole, send_sem, recv_sem, device), condition))

        def arrive(layer, row_z, row_x, span, sem):
            remote(spot(layer, row_z, row_x, span), spot(layer, row_z, row_x, span), sem, sem, to_x).wait_recv()

        def deliver(layer, row_z, row_x, half, condition=None):
            if layer is not None:
                return
            span = (span_a, span_b)[half]
            start = pl.multiple_of((row_z * 2 + row_x) * shard_rows, shard_rows)
            index = row_z * 2 + row_x
            copy = remote(
                spot(None, row_z, row_x, span), full_ref.at[last, pl.ds(start, shard_rows), span],
                push_sem.at[index, half], push_recv.at[index, half], other,
            )
            always(condition, copy.start)
            finish.append((copy, condition))

        for layer in served:
            s = 2 if layer is None else layer
            launch(layer, z, x, span_b, sbx.at[s], rbx.at[s], to_x, None, True)
            launch(layer, z, x, span_a, sau.at[s, 0], rau.at[s, 0], to_up, has_up, True)
            launch(layer, z, x, span_a, sad.at[s, 0], rad.at[s, 0], to_down, has_down, True)
            launch(layer, z, x, span_a, sax.at[s, 0], rax.at[s, 0], to_x, None, True)
            launch(layer, z, x, span_b, sbu.at[s, 0, 0], rbu.at[s, 0, 0], to_up, has_up, True)
            launch(layer, z, x, span_b, sbd.at[s, 0, 0], rbd.at[s, 0, 0], to_down, has_down, True)
        for layer in served:
            s = 2 if layer is None else layer
            arrive(layer, z, 1 - x, span_b, rbx.at[s])
            launch(layer, z, 1 - x, span_b, sbu.at[s, 0, 1], rbu.at[s, 0, 1], to_up, has_up)
            launch(layer, z, 1 - x, span_b, sbd.at[s, 0, 1], rbd.at[s, 0, 1], to_down, has_down)
            deliver(layer, z, 1 - x, 1)
        for hop in range(line - 1):
            for layer in served:
                s = 2 if layer is None else layer
                below, above = z - 1 - hop >= 0, z + 1 + hop < line
                row_below, row_above = jnp.maximum(z - 1 - hop, 0), jnp.minimum(z + 1 + hop, line - 1)
                for live, row, sa, ra, sb, rb, number, onward, device in (
                    (below, row_below, sau, rau, sbu, rbu, 1 + hop, has_up, to_up),
                    (above, row_above, sad, rad, sbd, rbd, line + hop, has_down, to_down),
                ):
                    pl.when(live)(functools.partial(arrive, layer, row, x, span_a, ra.at[s, hop]))
                    launch(layer, row, x, span_a, sax.at[s, number], rax.at[s, number], to_x, live)
                    if hop + 1 < line - 1:
                        launch(layer, row, x, span_a, sa.at[s, hop + 1], ra.at[s, hop + 1], device, live & onward)
                    deliver(layer, row, x, 0, live)
                    for side, row_x in ((0, x), (1, 1 - x)):
                        pl.when(live)(functools.partial(arrive, layer, row, row_x, span_b, rb.at[s, hop, side]))
                        if hop + 1 < line - 1:
                            launch(
                                layer, row, row_x, span_b, sb.at[s, hop + 1, side], rb.at[s, hop + 1, side], device,
                                live & onward,
                            )
                        deliver(layer, row, row_x, 1, live)
        for layer in served:
            if layer is not None:
                await_x(layer, layer)
        return finish

    def await_x(layer, s):
        for hop in range(line):
            for row, number, live in (
                (z - hop, hop, z - hop >= 0), (z + hop, line - 1 + hop, z + hop < line),
            )[: 2 if hop else 1]:
                row = jnp.clip(row, 0, line - 1)
                whole = spot(layer, row, 1 - x, span_a)
                pl.when(live)(remote(whole, whole, rax.at[s, number], rax.at[s, number], to_x).wait_recv)

    def close(finish):
        for copy, condition in finish:
            always(condition, copy.wait_send)

    own_copies = []
    for layer in range(layers):
        for span in (span_a, span_b):
            for source, part in pieces(layer, span):
                copy = pltpu.make_async_copy(source, spot(layer, z, x, part), local_sem.at[layer, len(own_copies) % 5])
                copy.start()
                own_copies.append(copy)
    guest_copies = []
    for number, (source, part) in enumerate(pieces(last, span_a) + pieces(last, span_b)):
        guest_copies.append(remote(source, guest_shard.at[:, part], guest_sem.at[0, number], guest_sem.at[1, number], other))

    def fetch(layer, index):
        buffer = (w_qkv, w_out, w_up, w_down)[index]
        return pltpu.make_async_copy(
            full_ref.at[layer, :, pl.ds(ends[index], ends[index + 1] - ends[index])],
            buffer.at[layer],
            w_sem.at[layer, index],
        )

    @pl.when(section == 1)
    def _():
        for copy in guest_copies:
            copy.start()

    @pl.when(section == 0)
    def _():
        finish = gather(list(range(layers)))
        pl.semaphore_signal(go_sem, inc=1, device_id=other, device_id_type=MESH)
        for copy in own_copies:
            copy.wait()
        for layer in range(layers):
            for index in range(4):
                fetch(layer, index).start()
        close(finish)

    @pl.when(section == 1)
    def _():
        pl.semaphore_wait(go_sem, 1)
        finish = gather(list(range(last)))
        pl.semaphore_signal(go_sem, inc=1, device_id=other, device_id_type=MESH)
        for copy in own_copies:
            copy.wait()
        for layer in range(last):
            for index in range(4):
                fetch(layer, index).start()
        close(finish)

    for copy in small_copies:
        copy.wait()

    if True:
        for part in range(micro):
            mask[part] = allowed_bias(ids_ref[part], tokens)

        hand_over = pltpu.make_async_remote_copy(
            src_ref=final_low, dst_ref=given, send_sem=given_sem.at[0], recv_sem=given_sem.at[1],
            device_id=other, device_id_type=MESH,
        )

        @pl.when(section == 0)
        def _():
            for part in range(micro):
                hid[0, part] = h0_ref[part].astype(jnp.float32)

        @pl.when(section == 1)
        def _():
            hand_over.wait_recv()
            for part in range(micro):
                hid[0, part] = given[part].astype(jnp.float32)

        def save(index, source, layer, part):
            return pltpu.make_async_copy(source.at[layer, part], outs[index].at[layer, part], save_sem.at[index, layer, part])

        saves = ((0, hid), (1, qkv), (2, lse), (3, mixed), (4, mid), (5, act), (6, slope))

        def exchange(layer, stage, part):
            return pltpu.make_async_remote_copy(
                src_ref=send.at[layer, stage, part],
                dst_ref=recv.at[layer, stage, part],
                send_sem=send_sem.at[layer, stage, part],
                recv_sem=recv_sem.at[layer, stage, part],
                device_id=partner,
                device_id_type=MESH,
            )

        def norm_rows(value, gain, shift):
            average = jnp.mean(value, axis=-1, keepdims=True)
            centred = value - average
            spread = jnp.mean(centred * centred, axis=-1, keepdims=True)
            return centred * lax.rsqrt(spread + EPSILON) * gain + shift

        def joined(layer, stage, part, span):
            return send[layer, stage, part, span].astype(jnp.float32) + recv[layer, stage, part, span].astype(jnp.float32)

        def attention_stage(layer, part):
            @pl.when(layer > 0)
            def _():
                exchange(layer - 1, 1, part).wait_recv()

                @pl.loop(0, tokens, step=32)
                def _(start):
                    span = pl.ds(pl.multiple_of(start, 32), 32)
                    hid[layer, part, span] = mid[layer - 1, part, span] + (
                        joined(layer - 1, 1, part, span) + rows_ref[layer - 1, 5:6]
                    )

            @pl.loop(0, tokens, step=32)
            def _(start):
                span = pl.ds(pl.multiple_of(start, 32), 32)
                normed[span] = norm_rows(hid[layer, part, span], rows_ref[layer, 0:1], rows_ref[layer, 2:3]).astype(jnp.bfloat16)

            @pl.when(part == 0)
            def _():
                fetch(layer, 0).wait()

            for piece in range(3):
                @pl.loop(0, head_width, step=256)
                def _(start, piece=piece):
                    span = pl.ds(pl.multiple_of(piece * head_width + start, 256), 256)
                    value = jnp.dot(normed[...], w_qkv[layer, :, span], preferred_element_type=jnp.float32)
                    if piece != 1:
                        value = value + inner_all[layer, :, pl.ds(pl.multiple_of(piece // 2 * head_width + start, 256), 256)]
                    value = value.astype(jnp.bfloat16)
                    if piece == 0:
                        value = value * jnp.asarray(1.0 / math.sqrt(HEAD_DIM), jnp.bfloat16)
                    qkv[layer, part, :, span] = value

            lane = lax.broadcasted_iota(jnp.int32, (tokens, LANES), 1)
            tops = []
            for pair in range(head_width // LANES):
                q2 = qkv[layer, part, :, pair * LANES : (pair + 1) * LANES]
                k2 = qkv[layer, part, :, head_width + pair * LANES : head_width + (pair + 1) * LANES]
                v2 = qkv[layer, part, :, 2 * head_width + pair * LANES : 2 * head_width + (pair + 1) * LANES]
                halves = []
                for side in range(2):
                    live = (lane < HEAD_DIM) if side == 0 else (lane >= HEAD_DIM)
                    scores = contract_last(jnp.where(live, q2, jnp.zeros_like(q2)), k2) + mask[part]
                    top = jnp.max(scores, axis=-1, keepdims=True)
                    exponent = jnp.exp(scores - top)
                    total = jnp.sum(exponent, axis=-1, keepdims=True)
                    probs = (exponent / total).astype(jnp.bfloat16)
                    halves.append(jnp.dot(probs, v2, preferred_element_type=jnp.float32))
                    head = 2 * pair + side
                    lse[layer, part, :, head : head + 1] = top + jnp.log(total)
                mixed[layer, part, :, pair * LANES : (pair + 1) * LANES] = jnp.where(
                    lane < HEAD_DIM, halves[0], halves[1]
                ).astype(jnp.bfloat16)

            @pl.when(part == 0)
            def _():
                fetch(layer, 1).wait()

            @pl.loop(0, width, step=256)
            def _(start):
                span = pl.ds(pl.multiple_of(start, 256), 256)
                value = contract_last(mixed[layer, part], w_out[layer, span])
                send[layer, 0, part, :, span] = value.astype(jnp.bfloat16)

            exchange(layer, 0, part).start()
            for index in range(4):
                save(index, saves[index][1], layer, part).start()

        def mlp_stage(layer, part):
            exchange(layer, 0, part).wait_recv()

            @pl.loop(0, tokens, step=32)
            def _(start):
                span = pl.ds(pl.multiple_of(start, 32), 32)
                middle = hid[layer, part, span] + (joined(layer, 0, part, span) + rows_ref[layer, 3:4])
                mid[layer, part, span] = middle
                normed[span] = norm_rows(middle, rows_ref[layer, 1:2], rows_ref[layer, 4:5]).astype(jnp.bfloat16)

            @pl.when(part == 0)
            def _():
                fetch(layer, 2).wait()

            @pl.loop(0, hidden_width, step=256)
            def _(start):
                span = pl.ds(pl.multiple_of(start, 256), 256)
                upward = jnp.dot(normed[...], w_up[layer, :, span], preferred_element_type=jnp.float32)
                upward = upward + inner_all[layer, :, pl.ds(pl.multiple_of(2 * head_width + start, 256), 256)]
                phi = 0.5 + 0.5 * lax.erf(upward * math.sqrt(0.5))
                density = jnp.exp(-0.5 * upward * upward) * (1.0 / math.sqrt(2.0 * math.pi))
                act[layer, part, :, span] = (upward * phi).astype(jnp.bfloat16)
                slope[layer, part, :, span] = (phi + upward * density).astype(jnp.bfloat16)

            @pl.when(part == 0)
            def _():
                fetch(layer, 3).wait()

            @pl.loop(0, width, step=256)
            def _(start):
                span = pl.ds(pl.multiple_of(start, 256), 256)
                value = contract_last(act[layer, part], w_down[layer, span])
                send[layer, 1, part, :, span] = value.astype(jnp.bfloat16)

            exchange(layer, 1, part).start()
            for index in range(4, 7):
                save(index, saves[index][1], layer, part).start()

        @pl.loop(0, layers)
        def _(layer):
            @pl.when((section == 1) & (layer == last))
            def _():
                await_x(last, 2)
                for row_z in range(line):
                    for row_x in range(2):
                        for half in range(2):
                            live = (row_x == x) & (row_z != z) if half == 0 else (row_z * 2 + row_x != place)
                            index = row_z * 2 + row_x
                            whole = spot(last, row_z, row_x, (span_a, span_b)[half])
                            pl.when(live)(
                                remote(whole, whole, push_recv.at[index, half], push_recv.at[index, half], other).wait_recv
                            )
                for index in range(4):
                    fetch(last, index).start()

            @pl.loop(0, micro)
            def _(part):
                attention_stage(layer, part)

            @pl.loop(0, micro)
            def _(part):
                mlp_stage(layer, part)

        @pl.loop(0, micro)
        def _(part):
            exchange(last, 1, part).wait_recv()

            @pl.loop(0, tokens, step=32)
            def _(start):
                span = pl.ds(pl.multiple_of(start, 32), 32)
                value = mid[last, part, span] + (joined(last, 1, part, span) + rows_ref[last, 5:6])
                final[part, span] = value
                final_low[part, span] = value.astype(jnp.bfloat16)

        rows_out[...] = rows_ref[...]
        ending = pltpu.make_async_copy(final, outs[7], save_sem.at[7, 0, 0])
        ending.start()

        @pl.when(section == 0)
        def _():
            hand_over.start()
            for copy in guest_copies:
                copy.wait_recv()
            pl.semaphore_wait(go_sem, 1)
            close(gather([None]))
            hand_over.wait_send()

        @pl.when(section == 1)
        def _():
            for copy in guest_copies:
                copy.wait_send()

        @pl.loop(0, layers)
        def _(layer):
            @pl.loop(0, micro)
            def _(part):
                for stage in range(2):
                    exchange(layer, stage, part).wait_send()
                for index, source in saves:
                    save(index, source, layer, part).wait()

        ending.wait()


def saved_shapes(layers, micro, tokens, width, head_width, hidden_width):
    low, full = jnp.bfloat16, jnp.float32
    heads = head_width // HEAD_DIM
    return (
        ((layers, micro, tokens, width), full),
        ((layers, micro, tokens, 3 * head_width), low),
        ((layers, micro, tokens, heads), full),
        ((layers, micro, tokens, head_width), low),
        ((layers, micro, tokens, width), full),
        ((layers, micro, tokens, hidden_width), low),
        ((layers, micro, tokens, hidden_width), low),
        ((micro, tokens, width), full),
    )


def forward(h0, ids, small, inner, qkv_in, out_in, up_in, down_in):
    layers, shard_rows = qkv_in.shape[:2]
    head_width, hidden_width = out_in.shape[2], up_in.shape[2]
    count = lax.axis_size("fsdp")
    line = count // 2
    width = shard_rows * count
    micro, tokens = ids.shape
    shapes = saved_shapes(layers, micro, tokens, width, head_width, hidden_width)
    cols = 4 * head_width + 2 * hidden_width
    low, wide = jnp.bfloat16, jnp.float32
    outs = shapes + (
        ((layers, width, cols), low),
        ((width, cols), low),
        ((shard_rows, cols), low),
        ((layers, 8, width), wide),
    )
    vmem = pl.BlockSpec(memory_space=pltpu.VMEM)
    hbm = pl.BlockSpec(memory_space=pl.ANY)
    dma = pltpu.SemaphoreType.DMA
    aligned = shard_rows % LANES == 0
    if not aligned:
        small = lax.all_gather(small, "fsdp", axis=2, tiled=True)
        inner = lax.all_gather(inner, "fsdp", axis=2, tiled=True)
    sets = layers + 1
    return pl.pallas_call(
        functools.partial(forward_kernel, line, aligned),
        out_shape=[jax.ShapeDtypeStruct(shape, kind) for shape, kind in outs],
        in_specs=[vmem] * 4 + [hbm] * 4,
        out_specs=[hbm] * (len(outs) - 1) + [vmem],
        scratch_shapes=[
            pltpu.VMEM((layers, width, 3 * head_width), low),
            pltpu.VMEM((layers, width, head_width), low),
            pltpu.VMEM((layers, width, hidden_width), low),
            pltpu.VMEM((layers, width, hidden_width), low),
            *(pltpu.VMEM(shape, kind) for shape, kind in shapes),
            pltpu.VMEM((layers, 8, width), wide),
            pltpu.VMEM((layers, 1, 3 * width), wide),
            pltpu.VMEM((micro, tokens, width), low),
            pltpu.VMEM((micro, tokens, width), low),
            pltpu.VMEM((tokens, width), low),
            pltpu.VMEM((micro, tokens, tokens), wide),
            pltpu.VMEM((layers, 2, micro, tokens, width), low),
            pltpu.VMEM((layers, 2, micro, tokens, width), low),
            dma((layers, 4)),
            dma((len(shapes), layers, micro)),
            dma((layers, 2, micro)),
            dma((layers, 2, micro)),
            dma((layers, 5)),
            pltpu.SemaphoreType.REGULAR,
            dma((2, 5)),
            dma((count, 2)),
            dma((count, 2)),
            dma((2,)),
            dma((2, count)),
            dma((2, count)),
            dma((sets, 2 * line - 1)),
            dma((sets, 2 * line - 1)),
            dma((sets, line - 1)),
            dma((sets, line - 1)),
            dma((sets, line - 1)),
            dma((sets, line - 1)),
            dma((sets,)),
            dma((sets,)),
            dma((sets, line - 1, 2)),
            dma((sets, line - 1, 2)),
            dma((sets, line - 1, 2)),
            dma((sets, line - 1, 2)),
        ],
        compiler_params=pltpu.CompilerParams(
            collective_id=2, has_side_effects=True, vmem_limit_bytes=63 << 20
        ),
        name="forward",
    )(h0, ids[:, None, :], small, inner, qkv_in, out_in, up_in, down_in)


SLOTS = 2


def backward_kernel(
    line, aligned, head_width, hidden_width, g0_ref, ids_ref, rows_ref, full_ref, *refs
):
    saves = refs[:7]
    (
        out, small_out, inner_out, g_out, d_out, own_in, x_in, z_in,
        w_qkv, w_out, w_up, w_down, hid, qkv, lse, mixed, mid, act, slope, grad, low, hidden_grad, qkv_grad, normed,
        mixed_grad, mask, send, recv, stage, small, inner_sum, given, run_own, run_x, run_z, run_out, small_in, inner_in,
        w_sem, load_sem, send_sem, recv_sem, stage_sem, end_sem, given_sem, own_send, own_recv, x_send, x_recv, z_send, z_recv, run_sem,
        out_sem, small_send, small_recv, inner_send, inner_recv,
    ) = refs[7:]
    held = (hid, qkv, lse, mixed, mid, act, slope)
    layers, micro, tokens, width = hid.shape
    section = lax.axis_index("section")
    partner = {"tensor": 1 - lax.axis_index("tensor")}
    other = {"section": 1 - section}
    place = lax.axis_index("fsdp")
    count = 2 * line
    z = place // 2
    x = lax.rem(place, 2)
    to_x = {"fsdp": z * 2 + 1 - x}
    to_up = {"fsdp": jnp.minimum(z + 1, line - 1) * 2 + x}
    to_down = {"fsdp": jnp.maximum(z - 1, 0) * 2 + x}
    tile = 256
    tiles = width // tile
    shard_rows = width // count
    group_cols = stage.shape[2]
    steps = 3 * line
    groups = 3
    scale = 1.0 / math.sqrt(HEAD_DIM)

    if True:
        ends = (0, 3 * head_width, 4 * head_width, 4 * head_width + hidden_width, 4 * head_width + 2 * hidden_width)

        def fetch(layer, index):
            buffer = (w_qkv, w_out, w_up, w_down)[index]
            return pltpu.make_async_copy(
                full_ref.at[layer, :, pl.ds(ends[index], ends[index + 1] - ends[index])], buffer, w_sem.at[index]
            )

        def load(index, layer):
            return pltpu.make_async_copy(saves[index].at[layer], held[index].at[layer], load_sem.at[index, layer])

        last = layers - 1
        fetch(last, 3).start()
        load(6, last).start()
        fetch(last, 2).start()
        for index in (5, 4):
            load(index, last).start()
        fetch(last, 1).start()
        for index in (1, 2, 3, 0):
            load(index, last).start()
        fetch(last, 0).start()
        for layer in range(last - 1, -1, -1):
            for index in range(7):
                load(index, layer).start()
        barrier = pltpu.get_barrier_semaphore()
        pl.semaphore_signal(barrier, inc=1, device_id=partner, device_id_type=MESH)
        pl.semaphore_signal(barrier, inc=1, device_id=other, device_id_type=MESH)
        for turn in range(1, count):
            peer = {"fsdp": lax.rem(place + turn, count)}
            pl.semaphore_signal(barrier, inc=1, device_id=peer, device_id_type=MESH)
        pl.semaphore_signal(
            barrier, inc=1, device_id={"section": 1 - section, "fsdp": z * 2 + 1 - x}, device_id_type=MESH
        )
        pl.semaphore_wait(barrier, count + 2)

        hand_over = pltpu.make_async_remote_copy(
            src_ref=low, dst_ref=given, send_sem=given_sem.at[0], recv_sem=given_sem.at[1],
            device_id=other, device_id_type=MESH,
        )

        small[...] = jnp.zeros_like(small)
        inner_sum[...] = jnp.zeros_like(inner_sum)
        for part in range(micro):
            mask[part] = allowed_bias(ids_ref[part], tokens)

        @pl.when(section == 1)
        def _():
            for part in range(micro):
                grad[part] = g0_ref[part].astype(jnp.float32)


        def exchange(step, part):
            return pltpu.make_async_remote_copy(
                src_ref=send.at[step, part],
                dst_ref=recv.at[step, part],
                send_sem=send_sem.at[step, part],
                recv_sem=recv_sem.at[step, part],
                device_id=partner,
                device_id_type=MESH,
            )

        def rows_of(part):
            return pl.ds(pl.multiple_of(part * tokens, tokens), tokens)

        def column_sum(value):
            return jnp.sum(value.astype(jnp.float32), axis=0, keepdims=True)

        def norm_parts(value):
            average = jnp.mean(value, axis=-1, keepdims=True)
            centred = value - average
            spread = jnp.mean(centred * centred, axis=-1, keepdims=True)
            inverse = lax.rsqrt(spread + EPSILON)
            return centred * inverse, inverse

        def norm_back(layer, step, part, source, gain_row, shift_row):
            gain = rows_ref[layer, gain_row : gain_row + 1]

            @pl.loop(0, tokens, step=32)
            def _(start):
                span = pl.ds(pl.multiple_of(start, 32), 32)
                outer = send[step, part, span].astype(jnp.float32) + recv[step, part, span].astype(jnp.float32)
                unit, inverse = norm_parts(source[layer, part, span])
                inner = outer * gain
                first = jnp.mean(inner, axis=-1, keepdims=True)
                second = jnp.mean(inner * unit, axis=-1, keepdims=True)
                small[layer, gain_row : gain_row + 1] += column_sum(outer * unit)
                small[layer, shift_row : shift_row + 1] += column_sum(outer)
                grad[part, span] = grad[part, span] + inverse * (inner - first - unit * second)

        def renorm(layer, part, source, gain_row, shift_row):
            @pl.loop(0, tokens, step=32)
            def _(start):
                span = pl.ds(pl.multiple_of(start, 32), 32)
                unit, _ = norm_parts(source[layer, part, span])
                value = unit * rows_ref[layer, gain_row : gain_row + 1] + rows_ref[layer, shift_row : shift_row + 1]
                normed[pl.ds(pl.multiple_of(part * tokens + start, 32), 32)] = value.astype(jnp.bfloat16)

        def round_grad(layer, part, bias_row):
            @pl.loop(0, tokens, step=32)
            def _(start):
                span = pl.ds(pl.multiple_of(start, 32), 32)
                value = grad[part, span].astype(jnp.bfloat16)
                low[pl.ds(pl.multiple_of(part * tokens + start, 32), 32)] = value
                small[layer, bias_row : bias_row + 1] += column_sum(value)

        def columns(group):
            return pl.ds(pl.multiple_of((2 - group) * group_cols, group_cols), group_cols)

        def part_rows(row_z, row_x):
            return pl.ds(pl.multiple_of((row_z * 2 + row_x) * shard_rows, shard_rows), shard_rows)

        def put(layer, turn, number, group):
            return pltpu.make_async_copy(
                stage.at[turn],
                d_out.at[layer, pl.ds(pl.multiple_of(number * tile, tile), tile), columns(group)],
                stage_sem.at[turn],
            )

        def route(step):
            below, above = z, line - 1 - z
            gap = jnp.maximum(below, above) - jnp.minimum(below, above)
            rest = jnp.maximum(step - gap, 0)
            far = step < gap
            upward = jnp.where(far, jnp.where(above > below, 1, 0), 1 - lax.rem(rest, 2))
            reach = jnp.where(far, jnp.maximum(below, above) - step, jnp.minimum(below, above) - rest // 2)
            ends_here = step == line - 1
            target = jnp.where(ends_here, z, jnp.where(upward == 1, z + reach, z - reach))
            return target, upward == 1, ends_here

        def to_partner(turn, group, row_z):
            runner = jnp.where(turn == 0, 1 - section, section)
            return pltpu.make_async_remote_copy(
                src_ref=d_out.at[last - turn, part_rows(row_z, 1 - x), columns(group)],
                dst_ref=x_in.at[turn, group, row_z],
                send_sem=x_send.at[turn, group, row_z],
                recv_sem=x_recv.at[turn, group, row_z],
                device_id={"section": runner, "fsdp": z * 2 + 1 - x},
                device_id_type=MESH,
            )

        def to_other(group, row_z):
            return pltpu.make_async_remote_copy(
                src_ref=d_out.at[last, part_rows(row_z, x), columns(group)],
                dst_ref=own_in.at[group, row_z],
                send_sem=own_send.at[group, row_z],
                recv_sem=own_recv.at[group, row_z],
                device_id=other,
                device_id_type=MESH,
            )

        def onward(turn, group, row_z, slot, side):
            return pltpu.make_async_remote_copy(
                src_ref=run_own.at[slot],
                dst_ref=z_in.at[turn, group, side, row_z],
                send_sem=z_send.at[slot],
                recv_sem=z_recv.at[turn, group, side, row_z],
                device_id=(to_up, to_down)[side],
                device_id_type=MESH,
            )

        def publish(group):
            return pltpu.make_async_copy(run_out, out.at[0, :, columns(group)], out_sem.at[0])

        def publish_other(group):
            return pltpu.make_async_remote_copy(
                src_ref=run_out, dst_ref=out.at[last, :, columns(group)],
                send_sem=out_sem.at[1], recv_sem=out_sem.at[2 + group],
                device_id=other, device_id_type=MESH,
            )

        def add_rows(slot, source):
            @pl.loop(0, shard_rows, step=16)
            def _(start):
                span = pl.ds(pl.multiple_of(start, 16), 16)
                run_own[slot, span] = run_own[slot, span] + source[span]

        def run_sums(turn):
            @pl.loop(0, steps)
            def _(number):
                group = number // line
                step = lax.rem(number, line)
                slot = lax.rem(number, SLOTS)
                target, upward, ends_here = route(step)

                @pl.when((number >= SLOTS) & (lax.rem(number + line - SLOTS, line) != line - 1))
                def _():
                    onward(turn, 0, 0, slot, 0).wait_send()

                if turn == 0:
                    to_other(group, target).wait_recv()
                    source = own_in.at[group, target]
                else:
                    source = d_out.at[last - turn, part_rows(target, x), columns(group)]
                own = pltpu.make_async_copy(source, run_own.at[slot], run_sem.at[0])
                own.start()
                to_partner(turn, group, target).wait_recv()
                mate = pltpu.make_async_copy(x_in.at[turn, group, target], run_x, run_sem.at[1])
                mate.start()
                feeds = (
                    jnp.logical_or(upward, ends_here) & (z > 0),
                    jnp.logical_or(jnp.logical_not(upward), ends_here) & (z < line - 1),
                )
                moves = []
                for side in range(2):
                    move = pltpu.make_async_copy(z_in.at[turn, group, side, target], run_z.at[side], run_sem.at[2 + side])
                    moves.append(move)

                    @pl.when(feeds[side])
                    def _(side=side, move=move):
                        onward(turn, group, target, slot, side).wait_recv()
                        move.start()

                own.wait()
                mate.wait()
                add_rows(slot, run_x)
                for side in range(2):

                    @pl.when(feeds[side])
                    def _(side=side):
                        moves[side].wait()
                        add_rows(slot, run_z.at[side])

                @pl.when(jnp.logical_not(ends_here) & upward)
                def _():
                    onward(turn, group, target, slot, 0).start()

                @pl.when(jnp.logical_not(ends_here) & jnp.logical_not(upward))
                def _():
                    onward(turn, group, target, slot, 1).start()

                @pl.when(ends_here)
                def _():
                    @pl.when(group > 0)
                    def _():
                        publish(group).wait() if turn else publish_other(group).wait_send()

                    @pl.loop(0, shard_rows, step=16)
                    def _(start):
                        span = pl.ds(pl.multiple_of(start, 16), 16)
                        run_out[span] = run_own[slot, span].astype(jnp.float32)

                    publish(group).start() if turn else publish_other(group).start()

            for number in range(steps - SLOTS, steps):
                if number % line != line - 1:
                    onward(turn, 0, 0, number % SLOTS, 0).wait_send()
            publish(0).wait() if turn else publish_other(0).wait_send()

        @pl.when(section == 0)
        def _():
            run_sums(0)
            hand_over.wait_recv()
            for part in range(micro):
                grad[part] = given[pl.ds(part * tokens, tokens)].astype(jnp.float32)

        def mlp_stage(layer, part):
            round_grad(layer, part, 5)

            @pl.when(part == 0)
            def _():
                fetch(layer, 3).wait()
                load(6, layer).wait()

            @pl.loop(0, hidden_width, step=tile)
            def _(start):
                span = pl.ds(pl.multiple_of(start, tile), tile)
                value = jnp.dot(low[rows_of(part)], w_down[:, span], preferred_element_type=jnp.float32)
                value = (value * slope[layer, part, :, span].astype(jnp.float32)).astype(jnp.bfloat16)
                hidden_grad[rows_of(part), span] = value
                place_in = pl.ds(pl.multiple_of(2 * head_width + start, tile), tile)
                inner_sum[layer, :, place_in] += column_sum(value)

            @pl.when(part == 0)
            def _():
                fetch(layer, 2).wait()

            @pl.when(layer < last)
            def _():
                exchange(0, part).wait_send()

            @pl.loop(0, width, step=tile)
            def _(start):
                span = pl.ds(pl.multiple_of(start, tile), tile)
                value = contract_last(hidden_grad[rows_of(part)], w_up[span])
                send[0, part, :, span] = value.astype(jnp.bfloat16)

            exchange(0, part).start()

        def weight_tiles(layer, turn, group, fill):
            def row_of(number):
                return route(number)[0] if tiles == line else number

            def finish(number):
                row = row_of(number)
                put(layer, number, row, group).wait()
                for extra in range(line // tiles):
                    row_z = row * (line // tiles) + extra
                    to_partner(turn, group, row_z).start()
                    pl.when(turn == 0)(to_other(group, row_z).start)

            @pl.loop(0, tiles)
            def _(number):
                row = row_of(number)
                fill(number, pl.ds(pl.multiple_of(row * tile, tile), tile))
                put(layer, number, row, group).start()
                pl.when(number > 0)(lambda: finish(jnp.maximum(number - 1, 0)))

            finish(tiles - 1)

        def attention_stage(layer, part):
            exchange(0, part).wait_recv()
            norm_back(layer, 0, part, mid, 1, 4)
            round_grad(layer, part, 3)

            @pl.when(part == 0)
            def _():
                fetch(layer, 1).wait()
                load(1, layer).wait()
                load(2, layer).wait()

            @pl.loop(0, head_width, step=tile)
            def _(start):
                span = pl.ds(pl.multiple_of(start, tile), tile)
                value = jnp.dot(low[rows_of(part)], w_out[:, span], preferred_element_type=jnp.float32)
                mixed_grad[:, span] = value.astype(jnp.bfloat16)

            lane = lax.broadcasted_iota(jnp.int32, (tokens, LANES), 1)
            for pair in range(head_width // LANES):
                spans = [pl.ds(piece * head_width + pair * LANES, LANES) for piece in range(3)]
                q2, k2, v2 = (qkv[layer, part, :, span] for span in spans)
                go2 = mixed_grad[:, pair * LANES : (pair + 1) * LANES]
                halves = []
                for side in range(2):
                    live = (lane < HEAD_DIM) if side == 0 else (lane >= HEAD_DIM)
                    head = 2 * pair + side
                    scores = contract_last(jnp.where(live, q2, jnp.zeros_like(q2)), k2) + mask[part]
                    probs = jnp.exp(scores - lse[layer, part, :, head : head + 1])
                    outer = contract_last(jnp.where(live, go2, jnp.zeros_like(go2)), v2)
                    centre = jnp.sum(probs * outer, axis=-1, keepdims=True)
                    inner = (probs * (outer - centre)).astype(jnp.bfloat16)
                    halves.append((
                        jnp.dot(inner, k2, preferred_element_type=jnp.float32) * scale,
                        contract_rows(inner, q2),
                        contract_rows(probs.astype(jnp.bfloat16), go2),
                    ))
                for piece in range(3):
                    value = jnp.where(lane < HEAD_DIM, halves[0][piece], halves[1][piece]).astype(jnp.bfloat16)
                    qkv_grad[rows_of(part), spans[piece]] = value
                    if piece != 1:
                        place_in = pl.ds((piece // 2) * head_width + pair * LANES, LANES)
                        inner_sum[layer, :, place_in] += column_sum(value)

            @pl.when(part == 0)
            def _():
                fetch(layer, 0).wait()

            @pl.when(layer < last)
            def _():
                exchange(1, part).wait_send()

            @pl.loop(0, width, step=tile)
            def _(start):
                span = pl.ds(pl.multiple_of(start, tile), tile)
                value = contract_last(qkv_grad[rows_of(part)], w_qkv[span])
                send[1, part, :, span] = value.astype(jnp.bfloat16)

            exchange(1, part).start()

        @pl.loop(0, layers)
        def _(turn):
            layer = last - turn

            @pl.loop(0, micro)
            def _(part):
                mlp_stage(layer, part)

            @pl.when(layer > 0)
            def _():
                fetch(layer - 1, 3).start()
                fetch(layer - 1, 2).start()

            load(5, layer).wait()

            def fill_down(number, span):
                both = act[layer].reshape(micro * tokens, hidden_width)
                stage[number] = contract_rows(low[:, span], both).astype(jnp.bfloat16)

            weight_tiles(layer, turn, 0, fill_down)
            load(4, layer).wait()

            @pl.loop(0, micro)
            def _(part):
                renorm(layer, part, mid, 1, 4)

            def fill_up(number, span):
                stage[number] = contract_rows(normed[:, span], hidden_grad[...]).astype(jnp.bfloat16)

            weight_tiles(layer, turn, 1, fill_up)

            @pl.loop(0, micro)
            def _(part):
                attention_stage(layer, part)

            @pl.when(layer > 0)
            def _():
                fetch(layer - 1, 1).start()
                fetch(layer - 1, 0).start()

            load(3, layer).wait()
            load(0, layer).wait()

            @pl.loop(0, micro)
            def _(part):
                renorm(layer, part, hid, 0, 2)

            def fill_attention(number, span):
                both = mixed[layer].reshape(micro * tokens, head_width)
                stage[number, :, : 3 * head_width] = contract_rows(normed[:, span], qkv_grad[...]).astype(jnp.bfloat16)
                stage[number, :, 3 * head_width :] = contract_rows(low[:, span], both).astype(jnp.bfloat16)

            weight_tiles(layer, turn, 2, fill_attention)

            @pl.loop(0, micro)
            def _(part):
                exchange(1, part).wait_recv()
                norm_back(layer, 1, part, hid, 0, 2)

        for part in range(micro):
            low[pl.ds(part * tokens, tokens)] = grad[part].astype(jnp.bfloat16)
        pl.when(section == 1)(hand_over.start)
        ending = pltpu.make_async_copy(grad, g_out, end_sem.at[0])
        ending.start()

        def small_copies(peer, turn):
            if aligned:
                cut, inner_cut = pl.ds(pl.multiple_of(peer * shard_rows, shard_rows), shard_rows), pl.ds(
                    pl.multiple_of(peer * 3 * shard_rows, 3 * shard_rows), 3 * shard_rows
                )
            else:
                cut, inner_cut = pl.ds(0, width), pl.ds(0, 3 * width)
            made = []
            for source, target, sends, receives in (
                (small.at[:, :, cut], small_in, small_send, small_recv),
                (inner_sum.at[:, :, inner_cut], inner_in, inner_send, inner_recv),
            ):
                made.append(pltpu.make_async_remote_copy(
                    src_ref=source, dst_ref=target.at[turn], send_sem=sends.at[turn], recv_sem=receives.at[turn],
                    device_id={"fsdp": peer}, device_id_type=MESH,
                ))
            return made

        for turn in range(1, count):
            for copy in small_copies(lax.rem(place + turn, count), turn):
                copy.start()

        run_sums(1)
        pl.when(section == 1)(lambda: run_sums(0))

        if aligned:
            mine = pl.ds(pl.multiple_of(place * shard_rows, shard_rows), shard_rows)
            inner_mine = pl.ds(pl.multiple_of(place * 3 * shard_rows, 3 * shard_rows), 3 * shard_rows)
        else:
            mine, inner_mine = pl.ds(0, width), pl.ds(0, 3 * width)
        small_out[...] = small[:, :, mine]
        inner_out[...] = inner_sum[:, :, inner_mine]
        for turn in range(1, count):
            for copy in small_copies(lax.rem(place + turn, count), turn):
                copy.wait()
            small_out[...] += small_in[turn]
            inner_out[...] += inner_in[turn]

        for step in range(2):
            for part in range(micro):
                exchange(step, part).wait_send()

        @pl.loop(0, groups)
        def _(group):
            @pl.loop(0, line)
            def _(row_z):
                to_partner(0, group, row_z).wait_send()
                to_partner(1, group, row_z).wait_send()
                to_other(group, row_z).wait_send()

        for group in range(groups):
            publish_other(group).wait_recv()
        pl.when(section == 1)(hand_over.wait_send)
        ending.wait()


def backward(g0, ids, rows, full, saves, head_width, hidden_width):
    layers, width, cols = full.shape
    micro, tokens = ids.shape
    count = lax.axis_size("fsdp")
    line = count // 2
    shard_rows = width // count
    aligned = shard_rows % LANES == 0
    group_cols = 4 * head_width
    small_width = shard_rows if aligned else width
    shapes = saved_shapes(layers, micro, tokens, width, head_width, hidden_width)
    vmem = pl.BlockSpec(memory_space=pltpu.VMEM)
    hbm = pl.BlockSpec(memory_space=pl.ANY)
    dma = pltpu.SemaphoreType.DMA
    low, wide = jnp.bfloat16, jnp.float32
    outs = (
        ((layers, shard_rows, 3 * group_cols), wide),
        ((layers, 8, small_width), wide),
        ((layers, 1, 3 * small_width), wide),
        ((micro, tokens, width), wide),
        ((layers, width, 3 * group_cols), low),
        ((3, line, shard_rows, group_cols), low),
        ((2, 3, line, shard_rows, group_cols), low),
        ((2, 3, 2, line, shard_rows, group_cols), low),
    )
    return pl.pallas_call(
        functools.partial(backward_kernel, line, aligned, head_width, hidden_width),
        out_shape=[jax.ShapeDtypeStruct(shape, kind) for shape, kind in outs],
        in_specs=[vmem] * 3 + [hbm] * 8,
        out_specs=[hbm, vmem, vmem] + [hbm] * 5,
        scratch_shapes=[
            pltpu.VMEM((width, 3 * head_width), low),
            pltpu.VMEM((width, head_width), low),
            pltpu.VMEM((width, hidden_width), low),
            pltpu.VMEM((width, hidden_width), low),
            *(pltpu.VMEM(shape, kind) for shape, kind in shapes[:7]),
            pltpu.VMEM((micro, tokens, width), wide),
            pltpu.VMEM((micro * tokens, width), low),
            pltpu.VMEM((micro * tokens, hidden_width), low),
            pltpu.VMEM((micro * tokens, 3 * head_width), low),
            pltpu.VMEM((micro * tokens, width), low),
            pltpu.VMEM((tokens, head_width), low),
            pltpu.VMEM((micro, tokens, tokens), wide),
            pltpu.VMEM((2, micro, tokens, width), low),
            pltpu.VMEM((2, micro, tokens, width), low),
            pltpu.VMEM((width // 256, 256, group_cols), low),
            pltpu.VMEM((layers, 8, width), wide),
            pltpu.VMEM((layers, 1, 3 * width), wide),
            pltpu.VMEM((micro * tokens, width), low),
            pltpu.VMEM((SLOTS, shard_rows, group_cols), low),
            pltpu.VMEM((shard_rows, group_cols), low),
            pltpu.VMEM((2, shard_rows, group_cols), low),
            pltpu.VMEM((shard_rows, group_cols), wide),
            pltpu.VMEM((count, layers, 8, small_width), wide),
            pltpu.VMEM((count, layers, 1, 3 * small_width), wide),
            dma((4,)),
            dma((7, layers)),
            dma((2, micro)),
            dma((2, micro)),
            dma((width // 256,)),
            dma((1,)),
            dma((2,)),
            dma((3, line)),
            dma((3, line)),
            dma((2, 3, line)),
            dma((2, 3, line)),
            dma((SLOTS,)),
            dma((2, 3, 2, line)),
            dma((4,)),
            dma((5,)),
            dma((count,)),
            dma((count,)),
            dma((count,)),
            dma((count,)),
        ],
        compiler_params=pltpu.CompilerParams(
            collective_id=4, has_side_effects=True, vmem_limit_bytes=63 << 20
        ),
        name="backward",
    )(g0, ids[:, None, :], rows, full, *saves)


def unpack_grads(full, head_width, hidden_width):
    layers, rows, cols = full.shape
    ends = [3 * head_width, 4 * head_width, 4 * head_width + hidden_width, 4 * head_width + 2 * hidden_width]
    return (
        full[:, :, : ends[0]].reshape(layers, rows, 3, head_width),
        full[:, :, ends[0] : ends[1]],
        full[:, :, ends[1] : ends[2]],
        full[:, :, ends[2] : ends[3]],
    )


def body(
    block_input,
    image_ids,
    qkv_weight,
    out_weight,
    up_weight,
    down_weight,
    norm_gains,
    biases,
    inner_bias,
    cotangent,
):
    section = lax.axis_index("section")
    count = lax.axis_size("fsdp")
    head_width, hidden_width = out_weight.shape[2], up_weight.shape[2]
    layers, rows = qkv_weight.shape[:2]
    small = jnp.concatenate([norm_gains, biases, jnp.zeros_like(norm_gains)], axis=1).astype(jnp.float32)
    *saved, full, _, _, row_values = forward(
        block_input, image_ids, small, inner_bias.astype(jnp.float32),
        qkv_weight.reshape(layers, rows, -1), out_weight, up_weight, down_weight,
    )
    summed, small, inner, input_grad = backward(
        cotangent, image_ids, row_values, full, saved[:7], head_width, hidden_width
    )[:4]
    if small.shape[2] != rows:
        place = lax.axis_index("fsdp")
        small = lax.dynamic_slice_in_dim(small, place * rows, rows, 2)
        inner = lax.dynamic_slice_in_dim(inner, place * 3 * rows, 3 * rows, 2)
    section_ends = jnp.where(section == 0, input_grad, saved[7])[None]
    return (
        section_ends,
        *unpack_grads(summed, head_width, hidden_width),
        small[:, :2],
        small[:, 2:6],
        inner,
    )


def solution(mesh):
    placed = (
        P(None, "fsdp", None),
        P(None, "fsdp"),
        P("section", "fsdp", None, "tensor"),
        P("section", "fsdp", "tensor"),
        P("section", "fsdp", "tensor"),
        P("section", "fsdp", "tensor"),
        P("section", None, "fsdp"),
        P("section", None, "fsdp"),
        P("section", "tensor", "fsdp"),
        P(None, "fsdp", None),
    )
    return jax.shard_map(
        body,
        mesh=mesh,
        in_specs=placed,
        out_specs=(
            P("section", None, "fsdp", None),
            P("section", "fsdp", None, "tensor"),
            P("section", "fsdp", "tensor"),
            P("section", "fsdp", "tensor"),
            P("section", "fsdp", "tensor"),
            P("section", None, "fsdp"),
            P("section", None, "fsdp"),
            P("section", "tensor", "fsdp"),
        ),
        check_vma=False,
    )
```

```python
import functools
import math

import jax
import jax.numpy as jnp
from jax import lax
from jax.experimental import pallas as pl
from jax.experimental.pallas import tpu as pltpu
from jax.sharding import PartitionSpec as P

HEAD_DIM = 64
EPSILON = 1e-06


MESH = pl.DeviceIdType.MESH


def contract_last(left, right):
    return lax.dot_general(
        left, right, (((1,), (1,)), ((), ())), preferred_element_type=jnp.float32
    )


def contract_rows(left, right):
    return lax.dot_general(
        left, right, (((0,), (0,)), ((), ())), preferred_element_type=jnp.float32
    )


LANES = 128
X_FIRST_COLS = 1024
GUEST_X_FIRST_COLS = 256


def allowed_bias(ids_row, tokens):
    spread = jnp.broadcast_to(ids_row, (tokens, tokens))
    mirror = jnp.transpose(spread)
    one = lax.broadcasted_iota(jnp.int32, (tokens, tokens), 0)
    two = lax.broadcasted_iota(jnp.int32, (tokens, tokens), 1)
    allowed = ((mirror == spread) & (spread >= 0)) | (one == two)
    return jnp.where(allowed, 0.0, -1e30)


def forward_part(line, aligned, h0_ref, ids_ref, gains_in, shifts_in, inner_in, qkv_in, out_in, up_in, down_in, refs):
    (
        full_ref, guest_full, guest_shard,
        w_qkv, w_out, w_up, w_down, hid, qkv, lse, mixed, mid, act, slope,
        small_ref, inner_ref, own_shard, rows_ref, inner_all, final_low, given, normed, mask, send, recv,
        w_sem, h0_sem, send_sem, recv_sem, local_sem, go_sem, guest_sem, push_sem, push_recv, given_sem, small_sem, inner_sem,
        sax, rax, sau, rau, sad, rad, sbx, rbx, sbu, rbu, sbd, rbd,
    ) = refs
    layers, micro, tokens, width = hid.shape
    head_width, hidden_width = out_in.shape[2], up_in.shape[2]
    section = lax.axis_index("section")
    place = lax.axis_index("fsdp")
    count = 2 * line
    shard_rows = width // count
    z = place // 2
    x = lax.rem(place, 2)
    partner = {"tensor": 1 - lax.axis_index("tensor")}
    other = {"section": 1 - section}
    to_x = {"fsdp": z * 2 + 1 - x}
    to_x_other = {"section": 1 - section, "fsdp": z * 2 + 1 - x}
    has_up = z < line - 1
    has_down = z > 0
    to_up = {"fsdp": jnp.minimum(z + 1, line - 1) * 2 + x}
    to_down = {"fsdp": jnp.maximum(z - 1, 0) * 2 + x}
    ends = (0, 3 * head_width, 4 * head_width, 4 * head_width + hidden_width, 4 * head_width + 2 * hidden_width)
    cols = ends[4]
    guest_cols = cols // 3
    last = layers - 1

    first_copy = pltpu.make_async_copy(h0_ref, given, h0_sem.at[0])
    pl.when(section == 0)(first_copy.start)
    takes = []
    for layer in range(layers):
        for number, (source, start, wide) in enumerate((
            *((qkv_in.at[layer, piece], piece * head_width, head_width) for piece in range(3)),
            (out_in.at[layer], ends[1], head_width), (up_in.at[layer], ends[2], hidden_width),
            (down_in.at[layer], ends[3], hidden_width),
        )):
            take = pltpu.make_async_copy(source, own_shard.at[layer, :, pl.ds(start, wide)], local_sem.at[layer, number])
            take.start()
            takes.append(take)
    barrier = pltpu.get_barrier_semaphore()
    for peer in (partner, other, to_x_other):
        pl.semaphore_signal(barrier, inc=1, device_id=peer, device_id_type=MESH)
    for turn in range(1, count):
        peer = {"fsdp": lax.rem(place + turn, count)}
        pl.semaphore_signal(barrier, inc=1, device_id=peer, device_id_type=MESH)
    pl.semaphore_wait(barrier, count + 2)

    small_ref[:, 0:2] = gains_in[...].astype(jnp.float32)
    small_ref[:, 2:6] = shifts_in[...].astype(jnp.float32)
    small_ref[:, 6:8] = jnp.zeros_like(small_ref[:, 6:8])
    inner_ref[...] = inner_in[...].astype(jnp.float32)
    small_copies = []
    if aligned:
        mine = pl.ds(pl.multiple_of(place * shard_rows, shard_rows), shard_rows)
        inner_mine = pl.ds(pl.multiple_of(place * 3 * shard_rows, 3 * shard_rows), 3 * shard_rows)
        rows_ref[:, :, mine] = small_ref[...]
        inner_all[:, :, inner_mine] = inner_ref[...]
        for turn in range(1, count):
            peer = {"fsdp": lax.rem(place + turn, count)}
            for source, target, sems in (
                (small_ref, rows_ref.at[:, :, mine], small_sem), (inner_ref, inner_all.at[:, :, inner_mine], inner_sem),
            ):
                copy = pltpu.make_async_remote_copy(
                    src_ref=source, dst_ref=target, send_sem=sems.at[0, turn], recv_sem=sems.at[1, turn],
                    device_id=peer, device_id_type=MESH,
                )
                copy.start()
                small_copies.append(copy)
    else:
        rows_ref[...] = small_ref[...]
        inner_all[...] = inner_ref[...]

    def halves(unit):
        if unit < layers:
            return pl.ds(0, cols - X_FIRST_COLS), pl.ds(cols - X_FIRST_COLS, X_FIRST_COLS)
        base, middle = (unit - layers) * guest_cols, guest_cols - GUEST_X_FIRST_COLS
        return pl.ds(base, middle), pl.ds(base + middle, GUEST_X_FIRST_COLS)

    def spot(unit, row_z, row_x, span):
        start = pl.multiple_of((row_z * 2 + row_x) * shard_rows, shard_rows)
        target = full_ref.at[unit] if unit < layers else guest_full
        return target.at[pl.ds(start, shard_rows), span]

    def pieces(unit, half):
        span = halves(unit)[half]
        return [((own_shard.at[unit] if unit < layers else guest_shard).at[:, span], span)]

    def remote(source, target, send_sem, recv_sem, device):
        return pltpu.make_async_remote_copy(
            src_ref=source, dst_ref=target, send_sem=send_sem, recv_sem=recv_sem, device_id=device, device_id_type=MESH,
        )

    def always(condition, action):
        if condition is None:
            action()
        else:
            pl.when(condition)(action)

    def gather(waves, nearly):
        finish = []

        def launch(unit, row_z, row_x, half, send_sem, recv_sem, device, condition=None, fresh=False):
            span = halves(unit)[half]
            whole = spot(unit, row_z, row_x, span)
            direct = unit >= layers and device is to_x and half == 0
            start = pl.multiple_of((row_z * 2 + row_x) * shard_rows, shard_rows)

            def landing(part):
                return full_ref.at[last, pl.ds(start, shard_rows), part] if direct else spot(unit, row_z, row_x, part)

            target = to_x_other if direct else device

            def begin():
                for source, part in pieces(unit, half) if fresh else [(whole, span)]:
                    remote(source, landing(part), send_sem, recv_sem, target).start()

            always(condition, begin)
            finish.append((remote(whole, whole, send_sem, recv_sem, target), condition))

        def arrive(unit, row_z, row_x, half, sem):
            whole = spot(unit, row_z, row_x, halves(unit)[half])
            remote(whole, whole, sem, sem, to_x).wait_recv()

        def deliver(unit, row_z, row_x, half, condition=None):
            if unit < layers:
                return
            span = halves(unit)[half]
            start = pl.multiple_of((row_z * 2 + row_x) * shard_rows, shard_rows)
            index = row_z * 2 + row_x
            copy = remote(
                spot(unit, row_z, row_x, span), full_ref.at[last, pl.ds(start, shard_rows), span],
                push_sem.at[unit - layers, index, half], push_recv.at[unit - layers, index, half], other,
            )
            always(condition, copy.start)
            finish.append((copy, condition))

        def first_sends(wave):
            for u in wave:
                launch(u, z, x, 1, sbx.at[u], rbx.at[u], to_x, None, True)
                launch(u, z, x, 0, sau.at[u, 0], rau.at[u, 0], to_up, has_up, True)
                launch(u, z, x, 0, sad.at[u, 0], rad.at[u, 0], to_down, has_down, True)
                launch(u, z, x, 1, sbu.at[u, 0, 0], rbu.at[u, 0, 0], to_up, has_up, True)
                launch(u, z, x, 1, sbd.at[u, 0, 0], rbd.at[u, 0, 0], to_down, has_down, True)

        def first_across(wave):
            for u in wave:
                launch(u, z, x, 0, sax.at[u, 0], rax.at[u, 0], to_x, None, True)

        first_sends(waves[0])
        first_across(waves[0])
        for number, wave in enumerate(waves):
            for u in wave:
                arrive(u, z, 1 - x, 1, rbx.at[u])
                launch(u, z, 1 - x, 1, sbu.at[u, 0, 1], rbu.at[u, 0, 1], to_up, has_up)
                launch(u, z, 1 - x, 1, sbd.at[u, 0, 1], rbd.at[u, 0, 1], to_down, has_down)
                deliver(u, z, 1 - x, 1)
            for hop in range(line - 1):
                if hop == line - 2 and number + 1 < len(waves):
                    first_sends(waves[number + 1])
                if hop == line - 2 and number + 1 == len(waves):
                    nearly()
                for u in wave:
                    below, above = z - 1 - hop >= 0, z + 1 + hop < line
                    row_below, row_above = jnp.maximum(z - 1 - hop, 0), jnp.minimum(z + 1 + hop, line - 1)
                    for live, row, sa, ra, sb, rb, place_in, onward, device in (
                        (below, row_below, sau, rau, sbu, rbu, 1 + hop, has_up, to_up),
                        (above, row_above, sad, rad, sbd, rbd, line + hop, has_down, to_down),
                    ):
                        pl.when(live)(functools.partial(arrive, u, row, x, 0, ra.at[u, hop]))
                        launch(u, row, x, 0, sax.at[u, place_in], rax.at[u, place_in], to_x, live)
                        if hop + 1 < line - 1:
                            launch(u, row, x, 0, sa.at[u, hop + 1], ra.at[u, hop + 1], device, live & onward)
                        deliver(u, row, x, 0, live)
                        for side, row_x in ((0, x), (1, 1 - x)):
                            pl.when(live)(functools.partial(arrive, u, row, row_x, 1, rb.at[u, hop, side]))
                            if hop + 1 < line - 1:
                                launch(
                                    u, row, row_x, 1, sb.at[u, hop + 1, side], rb.at[u, hop + 1, side], device, live & onward
                                )
                            deliver(u, row, row_x, 1, live)
            if number + 1 < len(waves):
                first_across(waves[number + 1])
        for wave in waves:
            for u in wave:
                if u < layers:
                    await_x(u)
        return finish

    def await_x(unit):
        for hop in range(line):
            for row, number, live in (
                (z - hop, hop, z - hop >= 0), (z + hop, line - 1 + hop, z + hop < line),
            )[: 2 if hop else 1]:
                whole = spot(unit, jnp.clip(row, 0, line - 1), 1 - x, halves(unit)[0])
                pl.when(live)(remote(whole, whole, rax.at[unit, number], rax.at[unit, number], to_x).wait_recv)

    def await_guest(third):
        unit = layers + third
        await_x(unit)
        for row_z in range(line):
            for row_x in range(2):
                for half in range(2):
                    live = (row_x == x) & (row_z != z) if half == 0 else (row_z * 2 + row_x != place)
                    index = row_z * 2 + row_x
                    whole = spot(unit, row_z, row_x, halves(unit)[half])
                    sem = push_recv.at[third, index, half]
                    pl.when(live)(remote(whole, whole, sem, sem, other).wait_recv)

    def close(finish):
        for copy, condition in finish:
            always(condition, copy.wait_send)

    for take in takes:
        take.wait()
    guest_copies = [remote(own_shard.at[last], guest_shard, guest_sem.at[0], guest_sem.at[1], other)]
    own_copies = [
        pltpu.make_async_copy(own_shard.at[layer], spot(layer, z, x, pl.ds(0, cols)), local_sem.at[layer, 6])
        for layer in range(layers)
    ]
    for copy in own_copies:
        copy.start()

    def fetch(layer, index):
        buffer = (w_qkv, w_out, w_up, w_down)[index]
        return pltpu.make_async_copy(
            full_ref.at[layer, :, pl.ds(ends[index], ends[index + 1] - ends[index])],
            buffer,
            w_sem.at[layer, index],
        )

    def give_way():
        pl.semaphore_signal(go_sem, inc=1, device_id=other, device_id_type=MESH)

    for copy in guest_copies:
        copy.start()
    thirds = [[layers + third] for third in range(3)]

    @pl.when(section == 0)
    def _():
        finish = gather([list(range(last))], give_way)
        for copy in own_copies:
            copy.wait()
        for layer in range(last):
            for index in range(4):
                fetch(layer, index).start()
        close(finish)

    @pl.when(section == 1)
    def _():
        for copy in guest_copies:
            copy.wait_recv()
        pl.semaphore_wait(go_sem, 1)
        finish = gather([sum(thirds, []), list(range(last))], give_way)
        for copy in own_copies:
            copy.wait()
        for layer in range(last):
            for index in range(4):
                fetch(layer, index).start()
        close(finish)

    for copy in small_copies:
        copy.wait()

    if True:
        for part in range(micro):
            mask[part] = allowed_bias(ids_ref[part : part + 1], tokens)

        hand_over = pltpu.make_async_remote_copy(
            src_ref=final_low, dst_ref=given, send_sem=given_sem.at[0], recv_sem=given_sem.at[1],
            device_id=other, device_id_type=MESH,
        )

        pl.when(section == 0)(first_copy.wait)
        pl.when(section == 1)(hand_over.wait_recv)
        for part in range(micro):
            hid[0, part] = given[pl.ds(part * tokens, tokens)].astype(jnp.float32)

        def exchange(stage, part):
            return pltpu.make_async_remote_copy(
                src_ref=send.at[stage, part],
                dst_ref=recv.at[stage, part],
                send_sem=send_sem.at[stage, part],
                recv_sem=recv_sem.at[stage, part],
                device_id=partner,
                device_id_type=MESH,
            )

        def norm_rows(value, gain, shift):
            average = jnp.mean(value, axis=-1, keepdims=True)
            centred = value - average
            spread = jnp.mean(centred * centred, axis=-1, keepdims=True)
            return centred * lax.rsqrt(spread + EPSILON) * gain + shift

        def joined(stage, part, span):
            return send[stage, part, span].astype(jnp.float32) + recv[stage, part, span].astype(jnp.float32)

        def attention_stage(layer, part):
            @pl.when(layer > 0)
            def _():
                exchange(1, part).wait_recv()

                @pl.loop(0, tokens, step=112)
                def _(start):
                    span = pl.ds(pl.multiple_of(start, 112), 112)
                    hid[layer, part, span] = mid[layer - 1, part, span] + (
                        joined(1, part, span) + rows_ref[layer - 1, 5:6]
                    )

            @pl.loop(0, tokens, step=112)
            def _(start):
                span = pl.ds(pl.multiple_of(start, 112), 112)
                normed[span] = norm_rows(hid[layer, part, span], rows_ref[layer, 0:1], rows_ref[layer, 2:3]).astype(jnp.bfloat16)

            @pl.when(part == 0)
            def _():
                fetch(layer, 0).wait()

            for piece in range(3):
                @pl.loop(0, head_width, step=512)
                def _(start, piece=piece):
                    span = pl.ds(pl.multiple_of(piece * head_width + start, 512), 512)
                    value = jnp.dot(normed[...], w_qkv[:, span], preferred_element_type=jnp.float32)
                    if piece != 1:
                        value = value + inner_all[layer, :, pl.ds(pl.multiple_of(piece // 2 * head_width + start, 512), 512)]
                    value = value.astype(jnp.bfloat16)
                    if piece == 0:
                        value = value * jnp.asarray(1.0 / math.sqrt(HEAD_DIM), jnp.bfloat16)
                    qkv[layer, part, :, span] = value

            lane = lax.broadcasted_iota(jnp.int32, (tokens, LANES), 1)
            tops = []
            for pair in range(head_width // LANES):
                q2 = qkv[layer, part, :, pair * LANES : (pair + 1) * LANES]
                k2 = qkv[layer, part, :, head_width + pair * LANES : head_width + (pair + 1) * LANES]
                v2 = qkv[layer, part, :, 2 * head_width + pair * LANES : 2 * head_width + (pair + 1) * LANES]
                halves = []
                for side in range(2):
                    live = (lane < HEAD_DIM) if side == 0 else (lane >= HEAD_DIM)
                    scores = contract_last(jnp.where(live, q2, jnp.zeros_like(q2)), k2) + mask[part]
                    top = jnp.max(scores, axis=-1, keepdims=True)
                    exponent = jnp.exp(scores - top)
                    total = jnp.sum(exponent, axis=-1, keepdims=True)
                    probs = (exponent * (1.0 / total)).astype(jnp.bfloat16)
                    halves.append(jnp.dot(probs, v2, preferred_element_type=jnp.float32))
                    head = 2 * pair + side
                    lse[layer, part, :, head : head + 1] = top + jnp.log(total)
                mixed[layer, part, :, pair * LANES : (pair + 1) * LANES] = jnp.where(
                    lane < HEAD_DIM, halves[0], halves[1]
                ).astype(jnp.bfloat16)

            @pl.when(part == 0)
            def _():
                fetch(layer, 1).wait()

            pl.when(layer > 0)(exchange(0, part).wait_send)

            @pl.loop(0, width, step=1024)
            def _(start):
                span = pl.ds(pl.multiple_of(start, 1024), 1024)
                value = contract_last(mixed[layer, part], w_out[span])
                send[0, part, :, span] = value.astype(jnp.bfloat16)

            exchange(0, part).start()

        def mlp_stage(layer, part):
            exchange(0, part).wait_recv()

            @pl.loop(0, tokens, step=112)
            def _(start):
                span = pl.ds(pl.multiple_of(start, 112), 112)
                middle = hid[layer, part, span] + (joined(0, part, span) + rows_ref[layer, 3:4])
                mid[layer, part, span] = middle
                normed[span] = norm_rows(middle, rows_ref[layer, 1:2], rows_ref[layer, 4:5]).astype(jnp.bfloat16)

            @pl.when(part == 0)
            def _():
                fetch(layer, 2).wait()

            @pl.loop(0, hidden_width, step=1024)
            def _(start):
                span = pl.ds(pl.multiple_of(start, 1024), 1024)
                upward = jnp.dot(normed[...], w_up[:, span], preferred_element_type=jnp.float32)
                upward = upward + inner_all[layer, :, pl.ds(pl.multiple_of(2 * head_width + start, 1024), 1024)]
                phi = 0.5 + 0.5 * lax.erf(upward * math.sqrt(0.5))
                density = jnp.exp(-0.5 * upward * upward) * (1.0 / math.sqrt(2.0 * math.pi))
                act[layer, part, :, span] = (upward * phi).astype(jnp.bfloat16)
                slope[layer, part, :, span] = (phi + upward * density).astype(jnp.bfloat16)

            @pl.when((section == 0) | (layer < last))
            def _():
                @pl.when(part == 0)
                def _():
                    fetch(layer, 3).wait()

                pl.when(layer > 0)(exchange(1, part).wait_send)

                @pl.loop(0, width, step=1024)
                def _(start):
                    span = pl.ds(pl.multiple_of(start, 1024), 1024)
                    value = contract_last(act[layer, part], w_down[span])
                    send[1, part, :, span] = value.astype(jnp.bfloat16)

                exchange(1, part).start()


        @pl.loop(0, layers)
        def _(layer):
            @pl.when(layer == last)
            def _():
                await_guest(0)
                fetch(last, 0).start()
                fetch(last, 1).start()

            @pl.loop(0, micro)
            def _(part):
                attention_stage(layer, part)

            @pl.when(layer == last)
            def _():
                await_guest(1)
                fetch(last, 2).start()

            @pl.when((section == 0) & (layer == last))
            def _():
                await_guest(2)
                fetch(last, 3).start()

            @pl.loop(0, micro)
            def _(part):
                mlp_stage(layer, part)

        @pl.when(section == 0)
        def _():
            @pl.loop(0, micro)
            def _(part):
                exchange(1, part).wait_recv()

                @pl.loop(0, tokens, step=112)
                def _(start):
                    span = pl.ds(pl.multiple_of(start, 112), 112)
                    value = mid[last, part, span] + (joined(1, part, span) + rows_ref[last, 5:6])
                    final_low[pl.ds(pl.multiple_of(part * tokens + start, 112), 112)] = value.astype(jnp.bfloat16)

        @pl.when(section == 0)
        def _():
            hand_over.start()
            for copy in guest_copies:
                copy.wait_recv()
            pl.semaphore_wait(go_sem, 1)
            close(gather(thirds, lambda: None))
            hand_over.wait_send()

        for copy in guest_copies:
            copy.wait_send()
        for stage in range(2):
            for part in range(micro):
                exchange(stage, part).wait_send()

    return await_guest


def saved_shapes(layers, micro, tokens, width, head_width, hidden_width):
    low, full = jnp.bfloat16, jnp.float32
    heads = head_width // HEAD_DIM
    return (
        ((layers, micro, tokens, width), full),
        ((layers, micro, tokens, 3 * head_width), low),
        ((layers, micro, tokens, heads), full),
        ((layers, micro, tokens, head_width), low),
        ((layers, micro, tokens, width), full),
        ((layers, micro, tokens, hidden_width), low),
        ((layers, micro, tokens, hidden_width), low),
    )


SLOTS = 4
LENT = (4, 4)
LINE_FIRST_COLS = 256


def backward_part(line, aligned, head_width, hidden_width, g0_ref, rows_ref, full_ref, await_guest, refs):
    (
        out, small_out, inner_out, ends_out, d_out, own_in, x_in, z_in,
        w_qkv, w_out, w_up, w_down, hid, qkv, lse, mixed, mid, act, slope, grad, low, hidden_grad, qkv_grad, normed,
        mixed_grad, mask, send, recv, stage, small, inner_sum, given, run_own, run_x, run_z, run_out, late_in, small_in, inner_in,
        w_sem, g0_sem, send_sem, recv_sem, stage_sem, end_sem, given_sem, own_send, own_recv, x_send, x_recv, z_send, z_recv, run_sem,
        late_send, late_recv, out_sem, small_send, small_recv, inner_send, inner_recv,
    ) = refs
    layers, micro, tokens, width = hid.shape
    section = lax.axis_index("section")
    partner = {"tensor": 1 - lax.axis_index("tensor")}
    other = {"section": 1 - section}
    place = lax.axis_index("fsdp")
    count = 2 * line
    z = place // 2
    x = lax.rem(place, 2)
    to_x = {"fsdp": z * 2 + 1 - x}
    to_up = {"fsdp": jnp.minimum(z + 1, line - 1) * 2 + x}
    to_down = {"fsdp": jnp.maximum(z - 1, 0) * 2 + x}
    tile = 256
    wide_tile = 512
    tiles = width // tile
    shard_rows = width // count
    group_cols = stage.shape[2]
    x_cols = group_cols - LINE_FIRST_COLS
    groups = 3
    scale = 1.0 / math.sqrt(HEAD_DIM)

    if True:
        ends = (0, 3 * head_width, 4 * head_width, 4 * head_width + hidden_width, 4 * head_width + 2 * hidden_width)

        def fetch(layer, index):
            buffer = (w_qkv, w_out, w_up, w_down)[index]
            return pltpu.make_async_copy(
                full_ref.at[layer, :, pl.ds(ends[index], ends[index + 1] - ends[index])], buffer, w_sem.at[layer, index]
            )

        last = layers - 1
        first_copy = pltpu.make_async_copy(g0_ref, given, g0_sem.at[0])
        pl.when(section == 1)(first_copy.start)
        hand_over = pltpu.make_async_remote_copy(
            src_ref=low, dst_ref=given, send_sem=given_sem.at[0], recv_sem=given_sem.at[1],
            device_id=other, device_id_type=MESH,
        )

        small[...] = jnp.zeros_like(small)
        inner_sum[...] = jnp.zeros_like(inner_sum)

        @pl.when(section == 1)
        def _():
            first_copy.wait()
            for part in range(micro):
                grad[part] = given[pl.ds(part * tokens, tokens)].astype(jnp.float32)


        def exchange(step, part):
            return pltpu.make_async_remote_copy(
                src_ref=send.at[1 - step, part],
                dst_ref=recv.at[1 - step, part],
                send_sem=send_sem.at[1 - step, part],
                recv_sem=recv_sem.at[1 - step, part],
                device_id=partner,
                device_id_type=MESH,
            )

        def rows_of(part):
            return pl.ds(pl.multiple_of(part * tokens, tokens), tokens)

        def column_sum(value):
            return jnp.sum(value.astype(jnp.float32), axis=0, keepdims=True)

        def norm_parts(value):
            average = jnp.mean(value, axis=-1, keepdims=True)
            centred = value - average
            spread = jnp.mean(centred * centred, axis=-1, keepdims=True)
            inverse = lax.rsqrt(spread + EPSILON)
            return centred * inverse, inverse

        def norm_back(layer, step, part, source, gain_row, shift_row):
            gain = rows_ref[layer, gain_row : gain_row + 1]

            @pl.loop(0, tokens, step=112)
            def _(start):
                span = pl.ds(pl.multiple_of(start, 112), 112)
                outer = send[1 - step, part, span].astype(jnp.float32) + recv[1 - step, part, span].astype(jnp.float32)
                unit, inverse = norm_parts(source[layer, part, span])
                inner = outer * gain
                first = jnp.mean(inner, axis=-1, keepdims=True)
                second = jnp.mean(inner * unit, axis=-1, keepdims=True)
                small[layer, gain_row : gain_row + 1] += column_sum(outer * unit)
                small[layer, shift_row : shift_row + 1] += column_sum(outer)
                grad[part, span] = grad[part, span] + inverse * (inner - first - unit * second)

        def renorm(layer, part, source, gain_row, shift_row):
            @pl.loop(0, tokens, step=112)
            def _(start):
                span = pl.ds(pl.multiple_of(start, 112), 112)
                unit, _ = norm_parts(source[layer, part, span])
                value = unit * rows_ref[layer, gain_row : gain_row + 1] + rows_ref[layer, shift_row : shift_row + 1]
                normed[pl.ds(pl.multiple_of(part * tokens + start, 112), 112)] = value.astype(jnp.bfloat16)

        def round_grad(layer, part, bias_row):
            @pl.loop(0, tokens, step=112)
            def _(start):
                span = pl.ds(pl.multiple_of(start, 112), 112)
                value = grad[part, span].astype(jnp.bfloat16)
                low[pl.ds(pl.multiple_of(part * tokens + start, 112), 112)] = value
                small[layer, bias_row : bias_row + 1] += column_sum(value)

        def columns(group):
            return pl.ds(pl.multiple_of((2 - group) * group_cols, group_cols), group_cols)

        def x_columns(group):
            return pl.ds(pl.multiple_of((2 - group) * group_cols, LANES), x_cols)

        def line_columns(group):
            return pl.ds(pl.multiple_of((2 - group) * group_cols + x_cols, LANES), LINE_FIRST_COLS)

        def part_rows(row_z, row_x):
            return pl.ds(pl.multiple_of((row_z * 2 + row_x) * shard_rows, shard_rows), shard_rows)

        def put(layer, turn, number, group):
            return pltpu.make_async_copy(
                stage.at[turn],
                d_out.at[layer, pl.ds(pl.multiple_of(number * tile, tile), tile), columns(group)],
                stage_sem.at[turn],
            )

        def route(step):
            below, above = z, line - 1 - z
            gap = jnp.maximum(below, above) - jnp.minimum(below, above)
            rest = jnp.maximum(step - gap, 0)
            far = step < gap
            upward = jnp.where(far, jnp.where(above > below, 1, 0), 1 - lax.rem(rest, 2))
            reach = jnp.where(far, jnp.maximum(below, above) - step, jnp.minimum(below, above) - rest // 2)
            ends_here = step == line - 1
            target = jnp.where(ends_here, z, jnp.where(upward == 1, z + reach, z - reach))
            return target, upward == 1, ends_here

        lent = jnp.where(section == 0, LENT[0], LENT[1])
        borrowed = jnp.where(section == 0, LENT[1], LENT[0])

        def split(number):
            return last - number // groups, lax.rem(number, groups)

        def bay(number, mine):
            return number if mine else 3 * layers + number

        def to_partner(number, row_z):
            layer, group = split(number)
            away = number < lent
            return pltpu.make_async_remote_copy(
                src_ref=d_out.at[layer, part_rows(row_z, 1 - x), x_columns(group)],
                dst_ref=x_in.at[jnp.where(away, 3 * layers + number, number), row_z],
                send_sem=x_send.at[number, row_z],
                recv_sem=x_recv.at[jnp.where(away, 3 * layers + number, number), row_z],
                device_id={"section": jnp.where(away, 1 - section, section), "fsdp": z * 2 + 1 - x},
                device_id_type=MESH,
            )

        def held_rows(number, row_z):
            layer, group = split(number)
            return (
                (d_out.at[layer, part_rows(row_z, x), x_columns(group)], pl.ds(0, x_cols)),
                (d_out.at[layer, part_rows(row_z, 0), line_columns(group)], pl.ds(x_cols, LINE_FIRST_COLS)),
                (d_out.at[layer, part_rows(row_z, 1), line_columns(group)], pl.ds(x_cols + LINE_FIRST_COLS, LINE_FIRST_COLS)),
            )

        def to_other(number, row_z, source, span):
            return pltpu.make_async_remote_copy(
                src_ref=source,
                dst_ref=own_in.at[number, row_z, :, span],
                send_sem=own_send.at[number, row_z],
                recv_sem=own_recv.at[number, row_z],
                device_id=other,
                device_id_type=MESH,
            )

        def to_other_whole(number, row_z):
            return to_other(number, row_z, own_in.at[number, row_z], pl.ds(0, x_cols + 2 * LINE_FIRST_COLS))

        def from_partner(place_in, row_z):
            return pltpu.make_async_remote_copy(
                src_ref=x_in.at[place_in, row_z], dst_ref=x_in.at[place_in, row_z],
                send_sem=x_recv.at[place_in, row_z], recv_sem=x_recv.at[place_in, row_z],
                device_id=to_x, device_id_type=MESH,
            )

        def late(place_in, slot, side):
            return pltpu.make_async_remote_copy(
                src_ref=run_own.at[slot, :, pl.ds(x_cols + side * LINE_FIRST_COLS, LINE_FIRST_COLS)],
                dst_ref=late_in.at[place_in],
                send_sem=late_send.at[0],
                recv_sem=late_recv.at[place_in],
                device_id=to_x,
                device_id_type=MESH,
            )

        def onward(place_in, row_z, slot, side):
            return pltpu.make_async_remote_copy(
                src_ref=run_own.at[slot],
                dst_ref=z_in.at[place_in, side, row_z],
                send_sem=z_send.at[slot],
                recv_sem=z_recv.at[place_in, side, row_z],
                device_id=(to_up, to_down)[side],
                device_id_type=MESH,
            )

        def publish(number):
            layer, group = split(number)
            return pltpu.make_async_copy(run_out, out.at[layer, :, columns(group)], out_sem.at[0])

        def publish_other(number):
            layer, group = split(number)
            return pltpu.make_async_remote_copy(
                src_ref=run_out, dst_ref=out.at[layer, :, columns(group)],
                send_sem=out_sem.at[1], recv_sem=out_sem.at[2 + number],
                device_id=other, device_id_type=MESH,
            )

        def add_rows(slot, source, cols):
            @pl.loop(0, shard_rows, step=16)
            def _(start):
                span = pl.ds(pl.multiple_of(start, 16), 16)
                run_own[slot, span, :cols] = run_own[slot, span, :cols] + source[span]

        def collect(number, mine, target, slot, feeds):
            place_in = bay(number, mine)
            own = pltpu.make_async_copy(own_in.at[0 if mine else number, target], run_own.at[slot], run_sem.at[0])
            if mine:
                for source, span in held_rows(number, target):
                    pltpu.make_async_copy(source, run_own.at[slot, :, span], run_sem.at[0]).start()
            else:
                to_other_whole(number, target).wait_recv()
                own.start()
            from_partner(place_in, target).wait_recv()
            mate = pltpu.make_async_copy(x_in.at[place_in, target], run_x, run_sem.at[1])
            mate.start()
            own.wait()
            mate.wait()
            add_rows(slot, run_x, x_cols)
            moves = []
            for side in range(2):
                move = pltpu.make_async_copy(z_in.at[place_in, side, target], run_z.at[side], run_sem.at[2 + side])
                moves.append(move)

                @pl.when(feeds[side])
                def _(side=side, move=move):
                    onward(place_in, target, 0, side).wait_recv()
                    move.start()

            for side in range(2):

                @pl.when(feeds[side])
                def _(side=side):
                    moves[side].wait()
                    add_rows(slot, run_z.at[side], x_cols + 2 * LINE_FIRST_COLS)

        def pass_on(number, mine, turn, step):
            slot = lax.rem(turn, SLOTS)
            target, upward, _ = route(step)
            place_in = bay(number, mine)

            @pl.when(turn >= SLOTS)
            def _():
                onward(0, 0, slot, 0).wait_send()

            collect(number, mine, target, slot, (upward & (z > 0), jnp.logical_not(upward) & (z < line - 1)))

            @pl.when(upward)
            def _():
                onward(place_in, target, slot, 0).start()

            @pl.when(jnp.logical_not(upward))
            def _():
                onward(place_in, target, slot, 1).start()

        def keep(number, mine, first):
            slot = SLOTS
            place_in = bay(number, mine)
            collect(number, mine, z, slot, (z > 0, z < line - 1))
            for side in range(2):
                pl.when(x == 1 - side)(late(place_in, slot, side).start)

            @pl.when(number > first)
            def _():
                publish(0).wait() if mine else publish_other(0).wait_send()

            @pl.loop(0, shard_rows, step=16)
            def _(start):
                span = pl.ds(pl.multiple_of(start, 16), 16)
                run_out[span, :x_cols] = run_own[slot, span, :x_cols].astype(jnp.float32)

            late(place_in, slot, 0).wait_recv()

            @pl.loop(0, shard_rows, step=16)
            def _(start):
                span = pl.ds(pl.multiple_of(start, 16), 16)
                own_half = jnp.where(
                    x == 0,
                    run_own[slot, span, x_cols : x_cols + LINE_FIRST_COLS].astype(jnp.float32),
                    run_own[slot, span, x_cols + LINE_FIRST_COLS :].astype(jnp.float32),
                )
                run_out[span, x_cols:] = own_half + late_in[place_in, span].astype(jnp.float32)

            late(place_in, slot, 0).wait_send()
            publish(number).start() if mine else publish_other(number).start()

        def run_sums(first, end, mine):
            first, end = jnp.asarray(first, jnp.int32), jnp.asarray(end, jnp.int32)

            @pl.loop(first, end + 1)
            def _(number):
                @pl.when(number < end)
                def _():
                    @pl.loop(0, line - 1)
                    def _(step):
                        pass_on(number, mine, (number - first) * (line - 1) + step, step)

                pl.when(number > first)(lambda: keep(number - 1, mine, first))

            for slot in range(SLOTS):
                pl.when(slot < (end - first) * (line - 1))(onward(0, 0, slot, 0).wait_send)
            pl.when(end > first)(publish(0).wait if mine else publish_other(0).wait_send)

        @pl.when(section == 0)
        def _():
            run_sums(0, LENT[1], False)
            hand_over.wait_recv()
            for part in range(micro):
                grad[part] = given[pl.ds(part * tokens, tokens)].astype(jnp.float32)

        def mlp_stage(layer, part):
            @pl.when((part == 0) & ((layer < last) | (section == 1)))
            def _():
                fetch(layer, 3).wait()

            @pl.loop(0, hidden_width, step=wide_tile)
            def _(start):
                span = pl.ds(pl.multiple_of(start, wide_tile), wide_tile)
                value = jnp.dot(low[rows_of(part)], w_down[:, span], preferred_element_type=jnp.float32)
                value = (value * slope[layer, part, :, span].astype(jnp.float32)).astype(jnp.bfloat16)
                hidden_grad[rows_of(part), span] = value
                place_in = pl.ds(pl.multiple_of(2 * head_width + start, wide_tile), wide_tile)
                inner_sum[layer, :, place_in] += column_sum(value)

            @pl.when((part == 0) & (layer < last))
            def _():
                fetch(layer, 2).wait()

            @pl.when(layer < last)
            def _():
                exchange(0, part).wait_send()

            @pl.loop(0, width, step=wide_tile)
            def _(start):
                span = pl.ds(pl.multiple_of(start, wide_tile), wide_tile)
                value = contract_last(hidden_grad[rows_of(part)], w_up[span])
                send[1, part, :, span] = value.astype(jnp.bfloat16)

            exchange(0, part).start()

        def weight_tiles(layer, turn, group, fill):
            def row_of(number):
                return route(number)[0] if tiles == line else number

            def finish(number):
                row = row_of(number)
                put(layer, number, row, group).wait()
                for extra in range(line // tiles):
                    row_z = row * (line // tiles) + extra
                    made = 3 * turn + group
                    to_partner(made, row_z).start()

                    @pl.when(made < lent)
                    def _(row_z=row_z, made=made):
                        for source, span in held_rows(made, row_z):
                            to_other(made, row_z, source, span).start()

            @pl.loop(0, tiles)
            def _(number):
                row = row_of(number)
                fill(number, pl.ds(pl.multiple_of(row * tile, tile), tile))
                put(layer, number, row, group).start()
                pl.when(number > 0)(lambda: finish(jnp.maximum(number - 1, 0)))

            finish(tiles - 1)

        def attention_stage(layer, part):
            exchange(0, part).wait_recv()
            norm_back(layer, 0, part, mid, 1, 4)
            round_grad(layer, part, 3)

            @pl.when((part == 0) & (layer < last))
            def _():
                fetch(layer, 1).wait()

            @pl.loop(0, head_width, step=wide_tile)
            def _(start):
                span = pl.ds(pl.multiple_of(start, wide_tile), wide_tile)
                value = jnp.dot(low[rows_of(part)], w_out[:, span], preferred_element_type=jnp.float32)
                mixed_grad[:, span] = value.astype(jnp.bfloat16)

            lane = lax.broadcasted_iota(jnp.int32, (tokens, LANES), 1)
            for pair in range(head_width // LANES):
                spans = [pl.ds(piece * head_width + pair * LANES, LANES) for piece in range(3)]
                q2, k2, v2 = (qkv[layer, part, :, span] for span in spans)
                go2 = mixed_grad[:, pair * LANES : (pair + 1) * LANES]
                halves = []
                for side in range(2):
                    live = (lane < HEAD_DIM) if side == 0 else (lane >= HEAD_DIM)
                    head = 2 * pair + side
                    scores = contract_last(jnp.where(live, q2, jnp.zeros_like(q2)), k2) + mask[part]
                    probs = jnp.exp(scores - lse[layer, part, :, head : head + 1])
                    outer = contract_last(jnp.where(live, go2, jnp.zeros_like(go2)), v2)
                    centre = jnp.sum(probs * outer, axis=-1, keepdims=True)
                    inner = (probs * (outer - centre)).astype(jnp.bfloat16)
                    halves.append((
                        jnp.dot(inner, k2, preferred_element_type=jnp.float32) * scale,
                        contract_rows(inner, q2),
                        contract_rows(probs.astype(jnp.bfloat16), go2),
                    ))
                for piece in range(3):
                    value = jnp.where(lane < HEAD_DIM, halves[0][piece], halves[1][piece]).astype(jnp.bfloat16)
                    qkv_grad[rows_of(part), spans[piece]] = value
                    if piece != 1:
                        place_in = pl.ds((piece // 2) * head_width + pair * LANES, LANES)
                        inner_sum[layer, :, place_in] += column_sum(value)

            @pl.when((part == 0) & (layer < last))
            def _():
                fetch(layer, 0).wait()

            @pl.when(layer < last)
            def _():
                exchange(1, part).wait_send()

            @pl.loop(0, width, step=wide_tile)
            def _(start):
                span = pl.ds(pl.multiple_of(start, wide_tile), wide_tile)
                value = contract_last(qkv_grad[rows_of(part)], w_qkv[span])
                send[0, part, :, span] = value.astype(jnp.bfloat16)

            exchange(1, part).start()

        @pl.loop(0, layers)
        def _(turn):
            layer = last - turn

            @pl.loop(0, micro)
            def _(part):
                round_grad(layer, part, 5)


            def fill_down(number, span):
                both = act[layer].reshape(micro * tokens, hidden_width)
                stage[number] = contract_rows(low[:, span], both).astype(jnp.bfloat16)

            weight_tiles(layer, turn, 0, fill_down)

            @pl.when((section == 1) & (layer == last))
            def _():
                await_guest(2)
                fetch(last, 3).start()

            @pl.loop(0, micro)
            def _(part):
                mlp_stage(layer, part)

            @pl.when(layer > 0)
            def _():
                fetch(layer - 1, 3).start()
                fetch(layer - 1, 2).start()


            @pl.loop(0, micro)
            def _(part):
                renorm(layer, part, mid, 1, 4)

            def fill_up(number, span):
                stage[number] = contract_rows(normed[:, span], hidden_grad[...]).astype(jnp.bfloat16)

            weight_tiles(layer, turn, 1, fill_up)

            @pl.loop(0, micro)
            def _(part):
                attention_stage(layer, part)

            @pl.when(layer > 0)
            def _():
                fetch(layer - 1, 1).start()
                fetch(layer - 1, 0).start()


            @pl.loop(0, micro)
            def _(part):
                renorm(layer, part, hid, 0, 2)

            def fill_attention(number, span):
                both = mixed[layer].reshape(micro * tokens, head_width)
                stage[number, :, : 3 * head_width] = contract_rows(normed[:, span], qkv_grad[...]).astype(jnp.bfloat16)
                stage[number, :, 3 * head_width :] = contract_rows(low[:, span], both).astype(jnp.bfloat16)

            weight_tiles(layer, turn, 2, fill_attention)

            @pl.loop(0, micro)
            def _(part):
                exchange(1, part).wait_recv()
                norm_back(layer, 1, part, hid, 0, 2)

        for part in range(micro):
            low[pl.ds(part * tokens, tokens)] = grad[part].astype(jnp.bfloat16)
        pl.when(section == 1)(hand_over.start)
        ending = pltpu.make_async_copy(grad, ends_out, end_sem.at[0])
        pl.when(section == 0)(ending.start)
        pl.when(section == 1)(fetch(last, 3).start)

        def small_copies(peer, turn):
            if aligned:
                cut, inner_cut = pl.ds(pl.multiple_of(peer * shard_rows, shard_rows), shard_rows), pl.ds(
                    pl.multiple_of(peer * 3 * shard_rows, 3 * shard_rows), 3 * shard_rows
                )
            else:
                cut, inner_cut = pl.ds(0, width), pl.ds(0, 3 * width)
            made = []
            for source, target, sends, receives in (
                (small.at[:, :, cut], small_in, small_send, small_recv),
                (inner_sum.at[:, :, inner_cut], inner_in, inner_send, inner_recv),
            ):
                made.append(pltpu.make_async_remote_copy(
                    src_ref=source, dst_ref=target.at[turn], send_sem=sends.at[turn], recv_sem=receives.at[turn],
                    device_id={"fsdp": peer}, device_id_type=MESH,
                ))
            return made

        for turn in range(1, count):
            for copy in small_copies(lax.rem(place + turn, count), turn):
                copy.start()

        run_sums(lent, 3 * layers, True)
        pl.when(section == 1)(lambda: run_sums(0, LENT[0], False))

        @pl.when(section == 1)
        def _():
            fetch(last, 3).wait()
            for part in range(micro):
                exchange(0, part).wait_send()

                @pl.loop(0, width, step=wide_tile)
                def _(start, part=part):
                    span = pl.ds(pl.multiple_of(start, wide_tile), wide_tile)
                    value = contract_last(act[last, part], w_down[span])
                    send[1, part, :, span] = value.astype(jnp.bfloat16)

                exchange(0, part).start()
            for part in range(micro):
                exchange(0, part).wait_recv()

                @pl.loop(0, tokens, step=112)
                def _(start, part=part):
                    span = pl.ds(pl.multiple_of(start, 112), 112)
                    down = send[1, part, span].astype(jnp.float32) + recv[1, part, span].astype(jnp.float32)
                    grad[part, span] = mid[last, part, span] + (down + rows_ref[last, 5:6])

            ending.start()


        if aligned:
            mine = pl.ds(pl.multiple_of(place * shard_rows, shard_rows), shard_rows)
            inner_mine = pl.ds(pl.multiple_of(place * 3 * shard_rows, 3 * shard_rows), 3 * shard_rows)
        else:
            mine, inner_mine = pl.ds(0, width), pl.ds(0, 3 * width)
        small_out[...] = small[:, :, mine]
        inner_out[...] = inner_sum[:, :, inner_mine]
        for turn in range(1, count):
            for copy in small_copies(lax.rem(place + turn, count), turn):
                copy.wait()
            small_out[...] += small_in[turn]
            inner_out[...] += inner_in[turn]

        for step in range(2):
            for part in range(micro):
                exchange(step, part).wait_send()

        @pl.loop(0, 3 * layers)
        def _(number):
            @pl.loop(0, line)
            def _(row_z):
                to_partner(number, row_z).wait_send()
                pl.when(number < lent)(lambda: to_other_whole(number, row_z).wait_send())

            pl.when(number < lent)(lambda: publish_other(number).wait_recv())

        pl.when(section == 1)(hand_over.wait_send)
        ending.wait()


def both_kernel(line, aligned, *refs):
    h0, g0, ids, gains, shifts, inner, qkv_in, out_in, up_in, down_in = refs[:10]
    sums, scratch = refs[10:21], refs[21:]
    results, full_ref, guests = sums[:8], sums[8], sums[9:]
    weights, saves, scratch = scratch[:4], scratch[4:11], scratch[11:]
    small_own, inner_own, own_shard, rows, inner_all, low, given_h, given_g, normed_part, mask, send, recv = scratch[:12]
    scratch = scratch[12:]
    back_buffers, scratch = scratch[:15], scratch[15:]
    w_sem, send_sem, recv_sem = scratch[:3]
    fore_sems, back_sems = scratch[3:24], scratch[24:]
    head_width, hidden_width = out_in.shape[2], up_in.shape[2]
    h0_sem, local_sems = fore_sems[0], fore_sems[1:]
    await_guest = forward_part(
        line, aligned, h0, ids, gains, shifts, inner, qkv_in, out_in, up_in, down_in,
        (
            full_ref, *guests, *weights, *saves, small_own, inner_own, own_shard, rows, inner_all, low, given_h,
            normed_part, mask, send, recv, w_sem, h0_sem, send_sem, recv_sem, *local_sems,
        ),
    )
    grad, hidden_grad, qkv_grad, normed, mixed_grad, stage, small, inner_sum = back_buffers[:8]
    backward_part(
        line, aligned, head_width, hidden_width, g0, rows, full_ref, await_guest,
        (
            *results, *weights, *saves, grad, low, hidden_grad, qkv_grad, normed, mixed_grad, mask, send, recv, stage,
            small, inner_sum, given_g, *back_buffers[8:], w_sem, back_sems[0], send_sem, recv_sem, *back_sems[1:],
        ),
    )


def forward_backward(h0, g0, ids, gains, shifts, inner, qkv_in, out_in, up_in, down_in):
    layers, shard_rows = out_in.shape[:2]
    head_width, hidden_width = out_in.shape[2], up_in.shape[2]
    count = lax.axis_size("fsdp")
    line = count // 2
    width = shard_rows * count
    micro, tokens = ids.shape
    cols = 4 * head_width + 2 * hidden_width
    group_cols = 4 * head_width
    x_cols = group_cols - LINE_FIRST_COLS
    line_cols = x_cols + 2 * LINE_FIRST_COLS
    low, wide = jnp.bfloat16, jnp.float32
    aligned = shard_rows % LANES == 0
    if not aligned:
        gains = lax.all_gather(gains, "fsdp", axis=2, tiled=True)
        shifts = lax.all_gather(shifts, "fsdp", axis=2, tiled=True)
        inner = lax.all_gather(inner, "fsdp", axis=2, tiled=True)
    small_width = shard_rows if aligned else width
    bays = 3 * layers + max(LENT)
    outs = (
        ((layers, shard_rows, cols), wide),
        ((layers, 8, small_width), wide),
        ((layers, 1, 3 * small_width), wide),
        ((micro, tokens, width), wide),
        ((layers, width, cols), low),
        ((max(LENT), line, shard_rows, line_cols), low),
        ((bays, line, shard_rows, x_cols), low),
        ((bays, 2, line, shard_rows, line_cols), low),
        ((layers, width, cols), low),
        ((width, cols), low),
        ((shard_rows, cols), low),
    )
    vmem = pl.BlockSpec(memory_space=pltpu.VMEM)
    hbm = pl.BlockSpec(memory_space=pl.ANY)
    dma = pltpu.SemaphoreType.DMA
    sets = layers + 3
    buffers = (
        ((width, 3 * head_width), low),
        ((width, head_width), low),
        ((width, hidden_width), low),
        ((width, hidden_width), low),
        *saved_shapes(layers, micro, tokens, width, head_width, hidden_width),
        ((layers, 8, gains.shape[2]), wide),
        (inner.shape, wide),
        ((layers, shard_rows, cols), low),
        ((layers, 8, width), wide),
        ((layers, 1, 3 * width), wide),
        ((micro * tokens, width), low),
        ((micro * tokens, width), low),
        ((micro * tokens, width), low),
        ((tokens, width), low),
        ((micro, tokens, tokens), wide),
        ((2, micro, tokens, width), low),
        ((2, micro, tokens, width), low),
        ((micro, tokens, width), wide),
        ((micro * tokens, hidden_width), low),
        ((micro * tokens, 3 * head_width), low),
        ((micro * tokens, width), low),
        ((tokens, head_width), low),
        ((width // 256, 256, group_cols), low),
        ((layers, 8, width), wide),
        ((layers, 1, 3 * width), wide),
        ((SLOTS + 1, shard_rows, line_cols), low),
        ((shard_rows, x_cols), low),
        ((2, shard_rows, line_cols), low),
        ((shard_rows, group_cols), wide),
        ((bays, shard_rows, LINE_FIRST_COLS), low),
        ((count, layers, 8, small_width), wide),
        ((count, layers, 1, 3 * small_width), wide),
    )
    h0 = h0.reshape(micro * tokens, width)
    g0 = g0.reshape(micro * tokens, width)
    return pl.pallas_call(
        functools.partial(both_kernel, line, aligned),
        out_shape=[jax.ShapeDtypeStruct(shape, kind) for shape, kind in outs],
        in_specs=[hbm] * 2 + [vmem] * 4 + [hbm] * 4,
        out_specs=[hbm, vmem, vmem] + [hbm] * 8,
        scratch_shapes=[
            *(pltpu.VMEM(shape, kind) for shape, kind in buffers),
            dma((layers, 4)),
            dma((2, micro)),
            dma((2, micro)),
            dma((1,)),
            dma((layers, 7)),
            pltpu.SemaphoreType.REGULAR,
            dma((2,)),
            dma((3, count, 2)),
            dma((3, count, 2)),
            dma((2,)),
            dma((2, count)),
            dma((2, count)),
            dma((sets, 2 * line - 1)),
            dma((sets, 2 * line - 1)),
            dma((sets, line - 1)),
            dma((sets, line - 1)),
            dma((sets, line - 1)),
            dma((sets, line - 1)),
            dma((sets,)),
            dma((sets,)),
            dma((sets, line - 1, 2)),
            dma((sets, line - 1, 2)),
            dma((sets, line - 1, 2)),
            dma((sets, line - 1, 2)),
            dma((1,)),
            dma((width // 256,)),
            dma((1,)),
            dma((2,)),
            dma((max(LENT), line)),
            dma((max(LENT), line)),
            dma((3 * layers, line)),
            dma((bays, line)),
            dma((SLOTS,)),
            dma((bays, 2, line)),
            dma((4,)),
            dma((1,)),
            dma((bays,)),
            dma((2 + 3 * layers,)),
            dma((count,)),
            dma((count,)),
            dma((count,)),
            dma((count,)),
        ],
        compiler_params=pltpu.CompilerParams(
            collective_id=2, has_side_effects=True, vmem_limit_bytes=63 << 20
        ),
        name="forward_backward",
    )(h0, g0, ids, gains, shifts, inner, qkv_in, out_in, up_in, down_in)


def finish_kernel(
    summed, small_in, inner_in, ends, qkv_out, out_out, up_out, down_out, gains_out, shifts_out, inner_out, ends_out,
    small, inner, parts, halves, sems, out_sems,
):
    layers, _, rows, head_width = qkv_out.shape
    bounds = (0, head_width, 2 * head_width, 3 * head_width, 4 * head_width, 4 * head_width + up_out.shape[2], summed.shape[2])
    loads = [
        pltpu.make_async_copy(small_in, small, sems.at[7, 0]),
        pltpu.make_async_copy(inner_in, inner, sems.at[7, 1]),
    ]
    copies = []
    for layer in range(layers):
        targets = [qkv_out.at[layer, piece] for piece in range(3)] + [out_out.at[layer], up_out.at[layer], down_out.at[layer]]
        for number, target in enumerate(targets):
            source = summed.at[layer, :, pl.ds(bounds[number], bounds[number + 1] - bounds[number])]
            held = parts.at[layer, :, pl.ds(bounds[number], bounds[number + 1] - bounds[number])]
            copies.append((
                pltpu.make_async_copy(source, held, sems.at[number, layer]),
                pltpu.make_async_copy(held, target, out_sems.at[number, layer]),
            ))
    for part in range(ends.shape[0]):
        copies.append((
            pltpu.make_async_copy(ends.at[part], halves.at[part], sems.at[6, part]),
            pltpu.make_async_copy(halves.at[part], ends_out.at[0, part], out_sems.at[6, part]),
        ))
    for copy in loads + [bring for bring, _ in copies]:
        copy.start()
    for bring, store in copies:
        bring.wait()
        store.start()
    for copy in loads:
        copy.wait()
    gains_out[...] = small[:, 0:2]
    shifts_out[...] = small[:, 2:6]
    inner_out[...] = inner[...]
    for _, store in copies:
        store.wait()


def finish(summed, small, inner, ends, head_width, hidden_width):
    layers, rows, cols = summed.shape
    wide = jnp.float32
    shapes = (
        (layers, 3, rows, head_width), (layers, rows, head_width), (layers, rows, hidden_width), (layers, rows, hidden_width),
        (layers, 2, rows), (layers, 4, rows), (layers, 1, 3 * rows), (1, *ends.shape),
    )
    vmem = pl.BlockSpec(memory_space=pltpu.VMEM)
    hbm = pl.BlockSpec(memory_space=pltpu.HBM)
    return pl.pallas_call(
        finish_kernel,
        out_shape=[jax.ShapeDtypeStruct(shape, wide) for shape in shapes],
        in_specs=[hbm] * 4,
        out_specs=[hbm, hbm, hbm, hbm, vmem, vmem, vmem, hbm],
        scratch_shapes=[
            pltpu.VMEM(small.shape, wide),
            pltpu.VMEM(inner.shape, wide),
            pltpu.VMEM(summed.shape, wide),
            pltpu.VMEM(ends.shape, wide),
            pltpu.SemaphoreType.DMA((8, max(layers, ends.shape[0], 2))),
            pltpu.SemaphoreType.DMA((7, max(layers, ends.shape[0]))),
        ],
        compiler_params=pltpu.CompilerParams(vmem_limit_bytes=62 << 20),
        name="finish",
    )(summed, small, inner, ends)


def body(
    block_input,
    image_ids,
    qkv_weight,
    out_weight,
    up_weight,
    down_weight,
    norm_gains,
    biases,
    inner_bias,
    cotangent,
):
    head_width, hidden_width = out_weight.shape[2], up_weight.shape[2]
    layers, rows = qkv_weight.shape[:2]
    summed, small, inner, ends = forward_backward(
        block_input, cotangent, image_ids, norm_gains, biases, inner_bias,
        jnp.swapaxes(qkv_weight, 1, 2), out_weight, up_weight, down_weight,
    )[:4]
    if small.shape[2] != rows:
        place = lax.axis_index("fsdp")
        small = lax.dynamic_slice_in_dim(small, place * rows, rows, 2)
        inner = lax.dynamic_slice_in_dim(inner, place * 3 * rows, 3 * rows, 2)
    qkv_grad, *grads, section_ends = finish(summed, small, inner, ends, head_width, hidden_width)
    return (section_ends, jnp.swapaxes(qkv_grad, 1, 2), *grads)


def solution(mesh):
    placed = (
        P(None, "fsdp", None),
        P(None, "fsdp"),
        P("section", "fsdp", None, "tensor"),
        P("section", "fsdp", "tensor"),
        P("section", "fsdp", "tensor"),
        P("section", "fsdp", "tensor"),
        P("section", None, "fsdp"),
        P("section", None, "fsdp"),
        P("section", "tensor", "fsdp"),
        P(None, "fsdp", None),
    )
    return jax.shard_map(
        body,
        mesh=mesh,
        in_specs=placed,
        out_specs=(
            P("section", None, "fsdp", None),
            P("section", "fsdp", None, "tensor"),
            P("section", "fsdp", "tensor"),
            P("section", "fsdp", "tensor"),
            P("section", "fsdp", "tensor"),
            P("section", None, "fsdp"),
            P("section", None, "fsdp"),
            P("section", "tensor", "fsdp"),
        ),
        check_vma=False,
    )
```
